32 devices in a mesh: dp: 8 (over z, y), ep: 4 (over x, core).
Axes of the slice: x: 2, y: 2, z: 4, core: 2. Of those that a mesh axis runs over, the one named last changes fastest.
Arguments:
- tokens: bfloat16 [4096, 2048], P(('dp', 'ep')), may hold values from -6 to 6
- dense_weights: bfloat16 [2048, 25088], P(('dp', 'ep')), may hold values from -0.70710678 to 0.70710678
- expert_weights: bfloat16 [2048, 8, 4224], P('dp', 'ep'), may hold values from -1.2060454 to 1.2060454
- gain_attn: bfloat16 [2048], replicated, may hold values from 0.5 to 1.5
- gain_ffn: bfloat16 [2048], replicated, may hold values from 0.5 to 1.5
- qkv_bias: bfloat16 [6144], replicated, may hold values from -1.1953125 to 1.1953125
- router_weight: bfloat16 [2048, 9], replicated, may hold values from -0.0625 to 0.0625
- routes: int32 [4096, 4], P(('dp', 'ep')), may hold values from 0 to 7, all different within a row; in each aligned block of 128 rows (0 to 127, 128 to 255, ...) at most 128 rows name the same one
- doc_ids: int32 [4096], P('dp'), may hold values from 0 to 23, as said below
- out_grad: bfloat16 [4096, 2048], P(('dp', 'ep')), may hold values from -6 to 6
Outputs:
- output: bfloat16 [4096, 2048], P(('dp', 'ep'))
- input_grad: float32 [4096, 2048], P(('dp', 'ep'))
- dense_grad: float32 [2048, 25088], P(('dp', 'ep'))
- expert_grad: float32 [2048, 8, 4224], P('dp', 'ep')
- gain_attn_grad: float32 [2048], replicated
- gain_ffn_grad: float32 [2048], replicated
- bias_grad: float32 [6144], replicated
- router_grad: float32 [2048, 9], replicated
The draws below stay inside these ranges and needn't reach their ends.
Inputs may be any that keep to these rules, and one draw needn't show every extreme that they name: `routes`: among the 128 rows of one device no expert is named by more than 128 rows, a bound that some block reaches. `doc_ids`: each group of 512 tokens (one index of dp) holds three sequences with ids 3 g, 3 g + 1, 3 g + 2 in order; the middle one begins on the group's first device and ends on its last.
All inputs are finite; a program needn't handle non-finite values.
Results may differ from the reference program's by a relative error of at most 0.034.
Values may be sent and summed in bfloat16 or wider, within the bound.
No kernel may reach another device: no remote copies, remote signals or barrier semaphores. Data moves between devices by JAX's collectives and lax.ppermute only.
A program may use at most 832 MiB of HBM per device.

```python
import math
import jax
import jax.numpy as jnp
import numpy as np
from jax import lax

D = 2048
H = 16
HD = 128
FF = 1408
SFF = 5632
TOPK = 4
TOK_DEV = 128
EXPERTS = 8
CAP = 128
GROUP_TOK = 512
TOKENS = 4096
N_DP = 8


def draw_doc_ids(key, part):
    key = jax.random.fold_in(key, 11)
    early_cut = jax.random.randint(jax.random.fold_in(key, 1), (N_DP, 1), 1, TOK_DEV)
    late_cut = jax.random.randint(jax.random.fold_in(key, 2), (N_DP, 1), GROUP_TOK - TOK_DEV + 1, GROUP_TOK)
    cut_points = jnp.concatenate([early_cut, late_cut], axis=1).astype(jnp.int32)
    position = jnp.arange(GROUP_TOK, dtype=jnp.int32)
    seq_number = jnp.sum((cut_points[:, None, :] <= position[None, :, None]).astype(jnp.int32), axis=2)
    return (seq_number + 3 * jnp.arange(N_DP, dtype=jnp.int32)[:, None]).reshape(TOKENS)


def draw_dense_weights(key, part):
    key = jax.random.fold_in(key, 23)
    column = jnp.arange(4 * D + 3 * SFF, dtype=jnp.int32)
    column_scale = jnp.where(column < 3 * D, D ** (-0.5), jnp.where(column < 4 * D, (D // 64) ** (-0.5), jnp.where(column < 4 * D + 2 * SFF, D ** (-0.5), (SFF // 16) ** (-0.5))))
    normal_values = jax.random.truncated_normal(key, -4.0, 4.0, (D, 4 * D + 3 * SFF), jnp.float32)
    return (normal_values * column_scale.astype(jnp.float32)[None, :]).astype(jnp.bfloat16)


def draw_expert_weights(key, part):
    key = jax.random.fold_in(key, 37)
    column = jnp.arange(3 * FF, dtype=jnp.int32)
    column_scale = jnp.where(column < 2 * FF, D ** (-0.5), max(FF // 128, 1) ** (-0.5))
    normal_values = jax.random.truncated_normal(key, -4.0, 4.0, (D, EXPERTS, 3 * FF), jnp.float32)
    return (normal_values * column_scale.astype(jnp.float32)[None, None, :]).astype(jnp.bfloat16)


def levels(own_key, dims, shards, low, largest):
    def one(axis_at, parts):
        steps = jax.random.uniform(jax.random.fold_in(jax.random.fold_in(own_key, 6), axis_at), (parts,), jnp.float32, low / len(shards), largest / len(shards))
        return jnp.repeat(jnp.exp(steps), dims[axis_at] // parts).reshape((-1,) + (1,) * (len(dims) - axis_at - 1))

    loudness = one(*shards[0])
    for cut in shards[1:]:
        loudness = loudness * one(*cut)
    return loudness


def assign_block(own_key, own, number, rows, count, top, most, slope):
    ranking = jax.random.permutation(own_key, count)
    heavy_load, common = shares(count, rows * top, most, slope, True), shares(count, rows * top, most, slope, False)
    places = jnp.arange(count)

    def named(sizes, offset_by):
        used = int((sizes > 0).sum())
        fixed = max(1, used // 4)
        moved = fixed + (places - fixed + offset_by * (used - fixed)) % max(1, count - fixed)
        return jnp.zeros((count,), jnp.int32).at[ranking[jnp.where(places < fixed, places, moved)]].set(jnp.asarray(sizes, jnp.int32))

    sizes = jnp.where(number % 4 == 0, named(heavy_load, number // 4), named(common, number - number // 4 - 1))
    mixed = jax.random.permutation(jax.random.fold_in(own, 3), count)
    giver, taker = mixed[0:count // 2 * 2:2], mixed[1:count // 2 * 2:2]
    room = jnp.minimum(sizes[giver] - 1, most - sizes[taker]) // 2
    room = jnp.where((giver == ranking[0]) | (taker == ranking[0]) | (sizes[taker] == 0), 0, jnp.maximum(room, 0))
    moved = jax.random.randint(jax.random.fold_in(own, 4), (count // 2,), 0, 1 << 20) % (room + 1)
    sizes = sizes.at[giver].add(-moved).at[taker].add(moved)
    labels = jnp.searchsorted(jnp.cumsum(sizes), jnp.arange(rows * top), side="right").astype(jnp.int32)
    listing = labels.reshape(top, rows).T
    listing = listing[jax.random.permutation(jax.random.fold_in(own, 1), rows)]
    offset_by = jax.random.randint(jax.random.fold_in(own, 2), (rows, 1), 0, top)
    return jnp.take_along_axis(listing, (jnp.arange(top)[None, :] + offset_by) % top, axis=1)


def shares(count, total, bound, lean, full):
    portions = [(1 << 20) // math.isqrt(rank ** lean) + 1 for rank in range(1, count + 1)]
    largest = bound if full else min(bound, max(-(-total // count), total * portions[0] // sum(portions)))
    least = 1 if total - largest >= count - 1 else 0
    given, rest = [largest] + [least] * (count - 1), total - largest - least * (count - 1)
    while rest > 0:
        free = [i for i in range(1, count) if given[i] < largest] or [i for i in range(1, count) if given[i] < bound]
        whole, budget = sum([portions[i] for i in free]), rest
        for i in free:
            addition = min(bound - given[i], max(1, budget * portions[i] // whole), rest)
            given[i] = given[i] + addition
            rest = rest - addition
    return np.array(given)


def bell_draw(stream_key, shape, width, limit, shards=(), kind=jnp.bfloat16):
    level = levels(stream_key, shape, shards, -0.22, 0.18) if shards else 1.0
    entries = jax.random.normal(stream_key, shape, jnp.float32) * width * level
    return jnp.minimum(jnp.maximum(entries, -limit), limit).astype(kind)


def setup_inputs(seed: int = 0) -> dict:
    seeds = jax.random.split(jax.random.key(seed), 11)
    tokens = bell_draw(seeds[0], (TOKENS, D), 1.0, 6.0, ((0, 32),))
    dense_weights = draw_dense_weights(jax.random.fold_in(seeds[10], 71), 0)
    expert_weights = draw_expert_weights(jax.random.fold_in(seeds[10], 71), 0)
    gain_attn = jnp.clip(1.0 + 0.1 * jax.random.normal(seeds[3], (D,), jnp.float32), 0.5, 1.5).astype(jnp.bfloat16)
    gain_ffn = jnp.clip(1.0 + 0.1 * jax.random.normal(seeds[4], (D,), jnp.float32), 0.5, 1.5).astype(jnp.bfloat16)
    qkv_bias = bell_draw(seeds[5], (3 * D,), 0.2, 1.1953125)
    router_weight = bell_draw(seeds[6], (D, EXPERTS + 1), (4 * D) ** -0.5, 0.0625)
    routes_keys = jax.random.split(jax.random.fold_in(seeds[7], 1), TOKENS // TOK_DEV)
    routes_turns = jax.random.permutation(jax.random.fold_in(seeds[7], 3), TOKENS // TOK_DEV)
    routes = jax.vmap(lambda own, number: assign_block(jax.random.fold_in(seeds[7], 2), own, number, TOK_DEV, EXPERTS, TOPK, CAP, 2))(routes_keys, routes_turns).reshape((TOKENS, TOPK))
    doc_ids = draw_doc_ids(jax.random.fold_in(seeds[10], 71), 0)
    out_grad = bell_draw(seeds[9], (TOKENS, D), 1.0, 6.0, ((0, 32),))
    return dict(tokens=tokens, dense_weights=dense_weights, expert_weights=expert_weights, gain_attn=gain_attn, gain_ffn=gain_ffn, qkv_bias=qkv_bias, router_weight=router_weight, routes=routes, doc_ids=doc_ids, out_grad=out_grad)


norm_eps = 1e-06
rope_base = 1000000.0
exact_mode = lax.Precision.HIGHEST

@jax.custom_vjp
def low(v):
    return lax.optimization_barrier(v.astype(jnp.bfloat16)).astype(jnp.float32)

@jax.custom_vjp
def low_back(v):
    return v

def low_keep(v):
    return (low(v), None)

def low_pass(kept, grad):
    return (grad,)

def back_keep(v):
    return (v, None)

def back_low(kept, grad):
    return (low(grad),)
low.defvjp(low_keep, low_pass)
low_back.defvjp(back_keep, back_low)

def rms_scale(stream, gain):
    return stream * lax.rsqrt(lax.optimization_barrier(jnp.mean(stream * stream, axis=-1, keepdims=True)) + norm_eps) * gain

def rotate(vectors, cosine_table, sine_table):
    half_width = vectors.shape[-1] // 2
    turned = jnp.concatenate([-vectors[..., half_width:], vectors[..., :half_width]], axis=-1)
    return vectors * cosine_table + turned * sine_table

def rope_tables(places):
    steps_along = jnp.arange(HD // 2, dtype=jnp.float32) * (2.0 / HD)
    inverse = jnp.power(jnp.float32(rope_base), -steps_along)
    angles = places.astype(jnp.float32)[:, None] * inverse[None, :]
    angles = jnp.concatenate([angles, angles], axis=1)
    return (jnp.cos(angles)[:, None, :], jnp.sin(angles)[:, None, :])

def silu_value(values):
    return values * jax.nn.sigmoid(values)

def softmax_rows(logits):
    row_max = lax.optimization_barrier(jnp.max(logits, axis=-1, keepdims=True))
    weights = jnp.exp(logits - row_max)
    return weights / lax.optimization_barrier(jnp.sum(weights, axis=-1, keepdims=True))

def attend_group(group_data):
    queries, keys_all, values, doc_group = group_data
    key_order = jnp.arange(GROUP_TOK, dtype=jnp.int32)
    allowed = (doc_group[:, None] == doc_group[None, :]) & (key_order[None, :] <= key_order[:, None])
    scores = low_back(jnp.einsum('qhd,khd->hqk', queries, keys_all, precision=exact_mode) * HD ** (-0.5))
    scores = jnp.where(allowed[None, :, :], scores, -1e+30)
    attend = softmax_rows(scores)
    return jnp.einsum('hqk,khd->qhd', low(attend), values, precision=exact_mode)

def slot_tables(routes):
    blocks = TOKENS // TOK_DEV
    expert_of = routes.reshape(blocks, TOK_DEV * TOPK)
    onehot = (expert_of[:, :, None] == jnp.arange(EXPERTS, dtype=jnp.int32)[None, None, :]).astype(jnp.int32)
    slot_rank = lax.optimization_barrier(jnp.sum((jnp.cumsum(onehot, axis=1) - onehot) * onehot, axis=2)).reshape(-1)
    pick_index = jnp.arange(TOKENS * TOPK, dtype=jnp.int32)
    token_index = pick_index // TOPK
    block_index = token_index // TOK_DEV
    expert_flat = routes.reshape(-1)
    token_table = jnp.zeros((EXPERTS, blocks, CAP), jnp.int32).at[expert_flat, block_index, slot_rank].set(token_index)
    pick_table = jnp.zeros((EXPERTS, blocks, CAP), jnp.int32).at[expert_flat, block_index, slot_rank].set(pick_index)
    live_table = jnp.zeros((EXPERTS, blocks, CAP), jnp.float32).at[expert_flat, block_index, slot_rank].set(1.0)
    return (token_table.reshape(EXPERTS, blocks * CAP), pick_table.reshape(EXPERTS, blocks * CAP), live_table.reshape(EXPERTS, blocks * CAP))

def reference(tokens, dense_weights, expert_weights, gain_attn, gain_ffn, qkv_bias, router_weight, routes, doc_ids, out_grad):
    doc_groups = doc_ids.reshape(N_DP, GROUP_TOK)
    before = lax.optimization_barrier(jnp.sum((doc_groups[:, None, :] < doc_groups[:, :, None]).astype(jnp.int32), axis=2))
    places = (jnp.arange(GROUP_TOK, dtype=jnp.int32)[None, :] - before).reshape(TOKENS)
    cosine_table, sine_table = rope_tables(places)
    token_table, pick_table, live_table = slot_tables(routes)

    def forward(stream, dense_full, experts, gain_one, gain_two, bias_row, router):
        normed = low(rms_scale(stream, gain_one))
        packed = low_back(jnp.dot(normed, dense_full[:, :3 * D], precision=exact_mode) + bias_row)
        queries = low_back(low(rotate(packed[:, :D].reshape(TOKENS, H, HD), cosine_table, sine_table)))
        keys_all = low_back(low(rotate(packed[:, D:2 * D].reshape(TOKENS, H, HD), cosine_table, sine_table)))
        values = low_back(low(packed[:, 2 * D:].reshape(TOKENS, H, HD)))
        shaped = (queries.reshape(N_DP, GROUP_TOK, H, HD), keys_all.reshape(N_DP, GROUP_TOK, H, HD), values.reshape(N_DP, GROUP_TOK, H, HD), doc_groups)
        mixed = lax.map(jax.checkpoint(attend_group), shaped)
        mixed = low_back(low(mixed.reshape(TOKENS, D)))
        branch = low_back(jnp.dot(mixed, dense_full[:, 3 * D:4 * D].T, precision=exact_mode))
        residual = stream + branch
        normed_two = low(rms_scale(residual, gain_two))
        logits = jnp.dot(normed_two, router, precision=exact_mode)
        router_probs = softmax_rows(logits[:, :EXPERTS])
        gate_flat = jnp.take_along_axis(router_probs, routes, axis=1).reshape(-1)

        def expert_block(block_data):
            weights, token_rows, pick_rows, live_rows = block_data
            inputs = low_back(jnp.take(normed_two, token_rows, axis=0)) * live_rows[:, None]
            gate_up = low_back(jnp.dot(inputs, weights[:, :2 * FF], precision=exact_mode))
            hidden = low(silu_value(gate_up[:, :FF]) * gate_up[:, FF:])
            result = low_back(low(jnp.dot(hidden, weights[:, 2 * FF:].T, precision=exact_mode)))
            return result * (jnp.take(gate_flat, pick_rows) * live_rows)[:, None]
        expert_terms = lax.map(jax.checkpoint(expert_block), (jnp.moveaxis(experts, 1, 0), token_table, pick_table, live_table))
        routed = jnp.zeros((TOKENS, D), jnp.float32).at[token_table.reshape(-1)].add(expert_terms.reshape(-1, D))
        shared_gate_up = low_back(jnp.dot(normed_two, dense_full[:, 4 * D:4 * D + 2 * SFF], precision=exact_mode))
        shared_hidden = low(silu_value(shared_gate_up[:, :SFF]) * shared_gate_up[:, SFF:])
        shared_out = low_back(jnp.dot(shared_hidden, dense_full[:, 4 * D + 2 * SFF:].T, precision=exact_mode))
        return residual + routed + jax.nn.sigmoid(logits[:, EXPERTS:]) * shared_out
    output, pullback = jax.vjp(forward, tokens.astype(jnp.float32), dense_weights.astype(jnp.float32), expert_weights.astype(jnp.float32), gain_attn.astype(jnp.float32), gain_ffn.astype(jnp.float32), qkv_bias.astype(jnp.float32), router_weight.astype(jnp.float32))
    gradients = pullback(out_grad.astype(jnp.float32))
    return (output.astype(jnp.bfloat16), gradients[0], gradients[1], gradients[2], gradients[3], gradients[4], gradients[5], gradients[6])
```

```python
import jax
import jax.numpy as jnp
from jax import lax
from jax.sharding import Mesh, PartitionSpec as P

H = 16
HD = 128
FF = 1408
SFF = 5632

norm_eps = 1e-06
rope_base = 1000000.0
AXES = ("ring", "pair", "ep")
PLANE = ("pair", "ep")
f32 = jnp.float32
bf16 = jnp.bfloat16


class Layout:
    def __init__(self, rings):
        self.rings = rings
        self.order = list(range(0, rings, 2)) + list(range(1, rings, 2))[::-1]
        place = {r: i for i, r in enumerate(self.order)}
        self.place = [place[r] for r in range(rings)]
        self.core = self.pairs(lambda r, y, x, c: (r, y, x, 1 - c))
        self.side = self.pairs(lambda r, y, x, c: (r, y, 1 - x, c))
        self.up = self.pairs(lambda r, y, x, c: (r, 1 - y, x, c))
        self.cross = self.pairs(lambda r, y, x, c: (r, 1 - y, 1 - x, c))
        self.onward = self.pairs(lambda r, y, x, c: (self.order[(place[r] + 1) % rings], y, x, c))
        self.backward = self.pairs(lambda r, y, x, c: (self.order[(place[r] - 1) % rings], y, x, c))

    def pairs(self, move):
        found = []
        for r in range(self.rings):
            for y in range(2):
                for x in range(2):
                    for c in range(2):
                        u, v, w, q = move(r, y, x, c)
                        found.append((((r * 2 + y) * 2 + x) * 2 + c, ((u * 2 + v) * 2 + w) * 2 + q))
        return found

    def doubling(self):
        steps = []
        bit = 1
        while bit < self.rings * 8:
            steps.append([(i, i ^ bit) for i in range(self.rings * 8)])
            bit *= 2
        return steps


def permute(rows, pairs):
    return lax.ppermute(rows, AXES, pairs)


def stack(*parts):
    return jnp.concatenate(parts, axis=0)


def plus(a, b):
    return (a.astype(f32) + b.astype(f32)).astype(bf16)


def plane_rows(lay, rows):
    near = (rows, permute(rows, lay.side))
    far = (permute(rows, lay.up), permute(rows, lay.cross))
    near, far = stack(*near), stack(*far)
    return stack(near, permute(near, lay.core), far, permute(far, lay.core))


def plane_sums(lay, parts):
    n = parts.shape[0] // 8
    near = plus(parts[: 2 * n], permute(parts[2 * n : 4 * n], lay.core))
    far = plus(parts[4 * n : 6 * n], permute(parts[6 * n :], lay.core))
    total = near[:n].astype(f32) + permute(near[n:], lay.side).astype(f32)
    total = total + permute(far[:n], lay.up).astype(f32)
    return total + permute(far[n:], lay.cross).astype(f32)


def all_rows(lay, rows):
    blocks = [rows]
    for _ in range(lay.rings - 1):
        blocks.append(permute(blocks[-1], lay.onward))
    return [plane_rows(lay, block) for block in blocks]


def all_sums(lay, parts):
    total = None
    for part in parts[::-1]:
        here = plane_sums(lay, part)
        if total is not None:
            here = here + permute(total.astype(bf16), lay.backward).astype(f32)
        total = here
    return total


def rotate(vectors, cosine_table, sine_table):
    half_width = vectors.shape[-1] // 2
    turned = jnp.concatenate([-vectors[..., half_width:], vectors[..., :half_width]], axis=-1)
    return vectors * cosine_table + turned * sine_table


def unrotate(vectors, cosine_table, sine_table):
    half_width = vectors.shape[-1] // 2
    scaled = vectors * sine_table
    return vectors * cosine_table + jnp.concatenate(
        [scaled[..., half_width:], -scaled[..., :half_width]], axis=-1
    )


def rope_tables(places):
    steps_along = jnp.arange(HD // 2, dtype=f32) * (2.0 / HD)
    inverse = jnp.power(jnp.float32(rope_base), -steps_along)
    angles = places.astype(f32)[..., None] * inverse
    angles = jnp.concatenate([angles, angles], axis=-1)
    return jnp.cos(angles), jnp.sin(angles)


def dot(a, b):
    return jnp.dot(a, b, preferred_element_type=f32)


def dot_t(a, b):
    return jnp.einsum("tf,of->to", a, b, preferred_element_type=f32)


def dot_over(a, b):
    return jnp.einsum("tc,tf->cf", a, b, preferred_element_type=f32)


def ffn_chunk(rows, cots, bits, gate_cols, down_cols, own_expert, units):
    wide = 3 * units
    gate_up = dot(rows, gate_cols)
    g = gate_up[:, :wide]
    u = gate_up[:, wide : 2 * wide]
    logits = gate_up[:, 2 * wide :]
    experts = logits.shape[1] - 1
    expert_logits = logits[:, :experts]
    weights = jnp.exp(expert_logits - jnp.max(expert_logits, axis=1, keepdims=True))
    probs = weights / jnp.sum(weights, axis=1, keepdims=True)
    shared_gate = jax.nn.sigmoid(logits[:, experts:])
    own = (jnp.right_shift(bits[:, None], own_expert + jnp.arange(2, dtype=jnp.int32)[None, :]) & 1).astype(f32)
    own_gates = probs[:, :2] * own
    n = rows.shape[0]

    def spread(a, b, c):
        return jnp.concatenate([jnp.broadcast_to(v, (n, units)) for v in (a, b, c)], axis=1)

    gates = spread(shared_gate, own_gates[:, :1], own_gates[:, 1:])
    hidden_grad = dot(cots, down_cols)
    sig = jax.nn.sigmoid(g)
    silu = g * sig
    hidden = (silu * u).astype(bf16).astype(f32)
    gated = (gates * hidden).astype(bf16)
    gated_grad = hidden_grad * gates
    gate_grad = gated_grad * u * sig * (1.0 + g * (1.0 - sig))
    up_grad = gated_grad * silu
    products = (hidden_grad * hidden).reshape(n, 3, units)
    choice_grad = jnp.sum(products, axis=2)
    own_grad = choice_grad[:, 1:] * own
    weighted = jnp.sum(probs[:, :2] * own_grad, axis=1, keepdims=True)
    probs_grad = jnp.concatenate([own_grad, jnp.zeros((n, experts - 2), f32)], axis=1)
    logit_grad = jnp.concatenate(
        [probs * (probs_grad - weighted), choice_grad[:, :1] * shared_gate * (1.0 - shared_gate)], axis=1
    )
    gate_up_grad = jnp.concatenate([gate_grad, up_grad, logit_grad], axis=1).astype(bf16)
    out_part = dot_t(gated, down_cols).astype(bf16)
    rows_grad = dot_t(gate_up_grad, gate_cols).astype(bf16)
    return out_part, rows_grad, gated, gate_up_grad


def body(lay, tokens, dense_weights, expert_weights, gain_attn, gain_ffn, qkv_bias, router_weight, routes, doc_ids, out_grad):
    row_count, model_width = tokens.shape
    rings = lay.rings
    ring = lax.axis_index("ring")
    pair = lax.axis_index("pair")
    ep = lax.axis_index("ep")
    local_experts = expert_weights.shape[1]
    expert_count = router_weight.shape[1] - 1
    owners = expert_count // local_experts
    dp_count = rings * 2
    score_scale = HD ** (-0.5)
    ring_place = jnp.asarray(lay.place, jnp.int32)[ring]
    behind = [jnp.asarray(lay.order, jnp.int32)[(ring_place - s) % rings] for s in range(rings)]

    stream = tokens.astype(f32)
    gain_one = gain_attn.astype(f32)
    gain_two = gain_ffn.astype(f32)

    heads = H // 8
    share = heads * HD
    mine = dense_weights[:, : 4 * model_width].reshape(dense_weights.shape[0], 4, 8, share)
    mine = mine.transpose(2, 0, 1, 3).reshape(8, dense_weights.shape[0], 4 * share)
    plane_part = lax.all_to_all(mine, PLANE, split_axis=0, concat_axis=0, tiled=True)
    plane_part = plane_part.reshape(1, -1, 4 * share)
    attn_full = jnp.zeros((rings,) + plane_part.shape[1:], bf16)
    moving = plane_part
    for s in range(rings):
        attn_full = lax.dynamic_update_slice(attn_full, moving, (behind[s], 0, 0))
        if s < rings - 1:
            moving = permute(moving, lay.onward)
    attn_full = attn_full.reshape(model_width, 4 * share)
    qkv_cols = attn_full[:, : 3 * share]
    out_cols = attn_full[:, 3 * share :]

    unit_share = SFF // owners
    units = FF // dp_count
    shared = dense_weights[:, 4 * model_width :].reshape(-1, 3, owners, unit_share).transpose(2, 0, 1, 3)
    shared = lax.all_to_all(shared, "ep", split_axis=0, concat_axis=0, tiled=True)
    shared = shared.reshape(-1, 1, 3, dp_count, units)
    routed = expert_weights.reshape(-1, local_experts, 3, dp_count, units)
    ffn = jnp.concatenate([shared, routed], axis=1)
    ffn = ffn.transpose(3, 0, 2, 1, 4).reshape(dp_count, -1, 9 * units)
    ffn = lax.all_to_all(ffn, ("ring", "pair"), split_axis=0, concat_axis=0, tiled=True)
    ffn = ffn.reshape(model_width, 9 * units)
    wide = 3 * units
    own_expert = ep * local_experts
    turn = (own_expert + jnp.arange(expert_count, dtype=jnp.int32)) % expert_count
    router = jnp.concatenate([jnp.take(router_weight, turn, axis=1), router_weight[:, expert_count:]], axis=1)
    gate_cols = jnp.concatenate([ffn[:, : 2 * wide], router], axis=1)
    down_cols = ffn[:, 2 * wide :]

    bits = jnp.sum(jnp.left_shift(jnp.int32(1), routes), axis=1)
    bits = lax.all_gather(bits, AXES, axis=0, tiled=False)
    device_of = []
    for s in range(rings):
        for dy in range(2):
            for dc in range(2):
                for dx in range(2):
                    device_of.append((behind[s] * 2 + (pair ^ dy)) * 4 + (ep ^ (2 * dx + dc)))
    bits = bits[jnp.stack(device_of)].reshape(rings, -1)

    doc_pair = jnp.stack([doc_ids, permute(doc_ids, lay.up)])
    group_len = doc_ids.shape[0]
    before = jnp.sum((doc_pair[:, None, :] < doc_pair[:, :, None]).astype(jnp.int32), axis=2)
    spot = jnp.arange(group_len, dtype=jnp.int32)
    blocks = jnp.stack([ep, ep ^ 2, ep ^ 1, ep ^ 3])

    def in_order(values):
        return values.reshape(2, 4, row_count)[:, blocks].reshape(2, group_len)

    places = in_order(spot[None, :] - before)
    docs = in_order(doc_pair)
    spots = in_order(jnp.stack([spot, spot]))
    cosine, sine = rope_tables(places)
    cosine, sine = cosine[:, :, None, :], sine[:, :, None, :]
    allowed = (docs[:, :, None] == docs[:, None, :]) & (spots[:, None, :] <= spots[:, :, None])
    allowed = allowed[:, None]

    inverse_one = lax.rsqrt(jnp.mean(stream * stream, axis=1, keepdims=True) + norm_eps)
    normed = (stream * inverse_one * gain_one).astype(bf16)
    normed_group = plane_rows(lay, normed)
    slot = pair * 4 + ep
    bias_share = lax.dynamic_slice_in_dim(qkv_bias.astype(f32).reshape(3, 8, share), slot, 1, 1).reshape(3 * share)
    packed = dot(normed_group, qkv_cols) + bias_share

    def split_heads(columns):
        return columns.reshape(2, group_len, heads, HD)

    queries = rotate(split_heads(packed[:, :share]), cosine, sine).astype(bf16)
    keys = rotate(split_heads(packed[:, share : 2 * share]), cosine, sine).astype(bf16)
    values = split_heads(packed[:, 2 * share :].astype(bf16))
    scores = jnp.einsum("gqhd,gkhd->ghqk", queries, keys, preferred_element_type=f32) * score_scale
    scores = jnp.where(allowed, scores, -1e30)
    raw = jnp.exp(scores - jnp.max(scores, axis=3, keepdims=True))
    attend = raw / jnp.sum(raw, axis=3, keepdims=True)
    mixed = jnp.einsum("ghqk,gkhd->gqhd", attend.astype(bf16), values, preferred_element_type=f32)
    mixed = mixed.astype(bf16).reshape(2 * group_len, share)
    branch = plane_sums(lay, dot_t(mixed, out_cols).astype(bf16))
    residual = stream + branch
    inverse_two = lax.rsqrt(jnp.mean(residual * residual, axis=1, keepdims=True) + norm_eps)
    normed_two = (residual * inverse_two * gain_two).astype(bf16)

    cots = all_rows(lay, out_grad)
    rows = all_rows(lay, normed_two)
    chunks = [
        ffn_chunk(rows[s], cots[s], bits[s], gate_cols, down_cols, own_expert, units) for s in range(rings)
    ]
    output_sum = all_sums(lay, [c[0] for c in chunks])
    normed_two_grad = all_sums(lay, [c[1] for c in chunks])
    gate_cols_grad = dot_over(stack(*rows), stack(*[c[3] for c in chunks]))
    down_cols_grad = dot_over(stack(*cots), stack(*[c[2] for c in chunks]))
    output = (residual + output_sum).astype(bf16)

    ffn_grad = jnp.concatenate([gate_cols_grad[:, : 2 * wide].astype(bf16), down_cols_grad.astype(bf16)], axis=1)
    ffn_grad = lax.all_to_all(ffn_grad.reshape(dp_count, -1, 9 * units), ("ring", "pair"), split_axis=0, concat_axis=0, tiled=True)
    ffn_grad = ffn_grad.reshape(dp_count, -1, 3, 3, units).transpose(3, 1, 2, 0, 4)
    expert_grad = ffn_grad[1:].reshape(local_experts, -1, 3 * FF).transpose(1, 0, 2).astype(f32)
    shared_grad = ffn_grad[0].reshape(owners, -1, 3 * unit_share)
    shared_grad = lax.all_to_all(shared_grad, "ep", split_axis=0, concat_axis=0, tiled=True)
    shared_grad = shared_grad.reshape(owners, -1, 3, unit_share).transpose(1, 2, 0, 3).reshape(-1, 3 * SFF)

    router_part = gate_cols_grad[:, 2 * wide :].T
    turn_back = (jnp.arange(expert_count, dtype=jnp.int32) - own_expert) % expert_count
    router_part = jnp.concatenate([jnp.take(router_part[:expert_count], turn_back, axis=0), router_part[expert_count:]], axis=0)

    cotangent = out_grad.astype(f32)
    scaled_two = normed_two_grad * gain_two
    gain_two_grad = jnp.sum(normed_two_grad * residual * inverse_two, axis=0)
    residual_grad = (
        cotangent
        + inverse_two * scaled_two
        - residual * inverse_two**3 * jnp.mean(scaled_two * residual, axis=1, keepdims=True)
    )
    branch_grad = residual_grad.astype(bf16)

    branch_grad_group = plane_rows(lay, branch_grad)
    mixed_grad = dot(branch_grad_group, out_cols).astype(bf16)
    mixed_heads = split_heads(mixed_grad)
    attend_grad = jnp.einsum("gqhd,gkhd->ghqk", mixed_heads, values, preferred_element_type=f32)
    scores_grad = (attend * (attend_grad - jnp.sum(attend * attend_grad, axis=3, keepdims=True))).astype(bf16)
    queries_grad = (jnp.einsum("ghqk,gkhd->gqhd", scores_grad, keys, preferred_element_type=f32) * score_scale).astype(bf16)
    keys_grad = (jnp.einsum("ghqk,gqhd->gkhd", scores_grad, queries, preferred_element_type=f32) * score_scale).astype(bf16)
    values_grad = jnp.einsum("ghqk,gqhd->gkhd", attend.astype(bf16), mixed_heads, preferred_element_type=f32).astype(bf16)
    packed_grad = jnp.concatenate(
        [
            unrotate(queries_grad.astype(f32), cosine, sine).astype(bf16).reshape(2 * group_len, share),
            unrotate(keys_grad.astype(f32), cosine, sine).astype(bf16).reshape(2 * group_len, share),
            values_grad.reshape(2 * group_len, share),
        ],
        axis=1,
    )
    normed_grad = plane_sums(lay, dot_t(packed_grad, qkv_cols).astype(bf16))
    scaled_one = normed_grad * gain_one
    gain_one_grad = jnp.sum(normed_grad * stream * inverse_one, axis=0)
    input_grad = (
        residual_grad
        + inverse_one * scaled_one
        - stream * inverse_one**3 * jnp.mean(scaled_one * stream, axis=1, keepdims=True)
    )
    attn_grad = jnp.concatenate([dot_over(normed_group, packed_grad), dot_over(branch_grad_group, mixed)], axis=1)
    attn_grad = attn_grad.astype(bf16).reshape(rings, -1, 4 * share)
    total = None
    for s in range(rings)[::-1]:
        here = lax.dynamic_index_in_dim(attn_grad, behind[s], 0, keepdims=False).astype(f32)
        if total is not None:
            here = here + permute(total.astype(bf16), lay.backward).astype(f32)
        total = here
    total = total.astype(bf16).reshape(8, -1, 4 * share)
    total = lax.all_to_all(total, PLANE, split_axis=0, concat_axis=0, tiled=True)
    attn_grad = total.reshape(8, -1, 4, share).transpose(1, 2, 0, 3).reshape(-1, 4 * model_width)
    dense_grad = jnp.concatenate([attn_grad, shared_grad], axis=1).astype(f32)

    bias_part = jnp.sum(packed_grad.astype(f32), axis=0).reshape(3, 1, share)
    bias_part = lax.dynamic_update_slice(jnp.zeros((3, 8, share), f32), bias_part, (0, slot, 0))

    def sum_everywhere(values):
        for step in lay.doubling():
            values = values + permute(values, step)
        return values

    early = sum_everywhere(stack(router_part, gain_two_grad[None]))
    late = sum_everywhere(stack(gain_one_grad[None], bias_part.reshape(3, model_width)))
    return (
        output,
        input_grad,
        dense_grad,
        expert_grad,
        late[0],
        early[-1],
        late[1:].reshape(-1),
        early[:-1].T,
    )


def solution(mesh):
    devices = mesh.devices
    lay = Layout(devices.shape[0] // 2)
    inner = Mesh(devices.reshape(lay.rings, 2, devices.shape[1]), AXES)
    rows = P(AXES, None)
    experts = P(("ring", "pair"), "ep", None)
    in_specs = (rows, rows, experts, P(), P(), P(), P(), rows, P(("ring", "pair")), rows)
    out_specs = (rows, rows, rows, experts, P(), P(), P(), P())

    def run(*arguments):
        return body(lay, *arguments)

    return jax.shard_map(run, mesh=inner, in_specs=in_specs, out_specs=out_specs, check_vma=False)
```

```python
import functools

import jax
import jax.numpy as jnp
from jax import lax
from jax.experimental import pallas as pl
from jax.experimental.pallas import tpu as pltpu
from jax.sharding import Mesh, PartitionSpec as P

H = 16
HD = 128
FF = 1408
SFF = 5632

norm_eps = 1e-06
rope_base = 1000000.0
AXES = ("ring", "pair", "ep")
PLANE = ("pair", "ep")
f32 = jnp.float32
bf16 = jnp.bfloat16


class Layout:
    def __init__(self, rings):
        self.rings = rings
        self.order = list(range(0, rings, 2)) + list(range(1, rings, 2))[::-1]
        place = {r: i for i, r in enumerate(self.order)}
        self.place = [place[r] for r in range(rings)]
        self.core = self.pairs(lambda r, y, x, c: (r, y, x, 1 - c))
        self.side = self.pairs(lambda r, y, x, c: (r, y, 1 - x, c))
        self.up = self.pairs(lambda r, y, x, c: (r, 1 - y, x, c))
        self.onward = self.pairs(lambda r, y, x, c: (self.order[(place[r] + 1) % rings], y, x, c))
        self.backward = self.pairs(lambda r, y, x, c: (self.order[(place[r] - 1) % rings], y, x, c))

    def pairs(self, move):
        found = []
        for r in range(self.rings):
            for y in range(2):
                for x in range(2):
                    for c in range(2):
                        u, v, w, q = move(r, y, x, c)
                        found.append((((r * 2 + y) * 2 + x) * 2 + c, ((u * 2 + v) * 2 + w) * 2 + q))
        return found

    def doubling(self):
        steps = []
        bit = 1
        while bit < self.rings * 8:
            steps.append([(i, i ^ bit) for i in range(self.rings * 8)])
            bit *= 2
        return steps


def permute(rows, pairs):
    return lax.ppermute(rows, AXES, pairs)


def stack(*parts):
    return jnp.concatenate(parts, axis=0)


def plus(a, b):
    return (a.astype(f32) + b.astype(f32)).astype(bf16)


def plane_rows(lay, rows):
    side = permute(rows, lay.side)
    up = permute(rows, lay.up)
    near, far = stack(rows, side), stack(up, permute(up, lay.side))
    return stack(near, permute(near, lay.core), far, permute(far, lay.core))


def plane_sums(lay, own, other):
    n = own.shape[0] // 4
    here = plus(own, permute(other, lay.core))
    up = plus(here[2 * n : 3 * n], permute(here[3 * n :], lay.side))
    total = here[:n].astype(f32) + permute(here[n : 2 * n], lay.side).astype(f32)
    return total + permute(up, lay.up).astype(f32)


def rope_tables(places):
    steps_along = jnp.arange(HD // 2, dtype=f32) * (2.0 / HD)
    inverse = jnp.power(jnp.float32(rope_base), -steps_along)
    angles = places.astype(f32)[..., None] * inverse
    angles = jnp.concatenate([angles, angles], axis=-1)
    return jnp.cos(angles), jnp.sin(angles)


def dot(a, b):
    return jnp.dot(a, b, preferred_element_type=f32)


def dot_over(a, b):
    return jnp.einsum("tc,tf->cf", a, b, preferred_element_type=f32)


def after(value, *others):
    return lax.optimization_barrier((value,) + others)[0]


def together(*values):
    return lax.optimization_barrier(values)


def dot_nt(a, b):
    return lax.dot_general(a, b, (((1,), (1,)), ((), ())), preferred_element_type=f32)


def dot_tn(a, b):
    return lax.dot_general(a, b, (((0,), (0,)), ((), ())), preferred_element_type=f32)


def joined(refs):
    return jnp.concatenate([ref[0, 0] for ref in refs], axis=0)


def ffn_kernel(units, pad, experts, where_ref, rows_ref, c0, c1, c2, c3, gate_ref, down_ref, *refs):
    out_own_ref, out_far_ref, own_ref, far_ref, hidden_ref, gate_grad_ref = refs[-6:]
    n, width = rows_ref.shape
    wide = 3 * units
    base = wide // 128 * 128
    at = wide - base
    cots = joined((c0, c1, c2, c3))
    gate_up = dot_nt(rows_ref[...], gate_ref[...])
    hidden_grad = dot_nt(cots[:, :width], down_ref[...])
    g, u = gate_up[:, :pad], gate_up[:, pad:]
    logits = g[:, base : base + 128]
    lane = lax.broadcasted_iota(jnp.int32, (n, 128), 1)
    routed = (lane >= at) & (lane < at + experts)
    peak = jnp.max(jnp.where(routed, logits, -jnp.inf), axis=1, keepdims=True)
    weights = jnp.where(routed, jnp.exp(logits - peak), 0.0)
    probs = weights / jnp.sum(weights, axis=1, keepdims=True)
    shared_gate = jax.nn.sigmoid(logits[:, at + experts : at + experts + 1])
    bits = jnp.right_shift(cots[:, width : width + 128].astype(f32).astype(jnp.int32), where_ref[8])
    own = [(jnp.right_shift(bits, i) & 1).astype(f32)[:, :1] for i in range(2)]
    gate = [probs[:, at + i : at + i + 1] * own[i] for i in range(2)]
    spot = lax.broadcasted_iota(jnp.int32, (n, pad), 1)
    gates = jnp.where(spot < units, shared_gate, jnp.where(spot < 2 * units, gate[0], gate[1]))
    sig = jax.nn.sigmoid(g)
    silu = g * sig
    hidden = (silu * u).astype(bf16).astype(f32)
    gated = (gates * hidden).astype(bf16)
    hidden_ref[...] = gated
    gated_grad = hidden_grad * gates
    up_grad = gated_grad * silu
    gate_grad = gated_grad * u * (sig + silu * (1.0 - sig))
    products = hidden_grad * hidden

    def total(k):
        inside = (spot >= k * units) & (spot < (k + 1) * units)
        return jnp.sum(jnp.where(inside, products, 0.0), axis=1, keepdims=True)

    shared_grad = total(0) * shared_gate * (1.0 - shared_gate)
    own_grad = [total(1 + i) * own[i] for i in range(2)]
    weighted = probs[:, at : at + 1] * own_grad[0] + probs[:, at + 1 : at + 2] * own_grad[1]
    probs_grad = jnp.where(lane == at, own_grad[0], jnp.where(lane == at + 1, own_grad[1], 0.0))
    logit_grad = probs * (probs_grad - weighted)
    logit_grad = jnp.where(lane == at + experts, shared_grad, logit_grad)
    tail = jnp.where(lane < at, gate_grad[:, base : base + 128], logit_grad)
    parts = [gate_grad[:, :base], tail]
    if base + 128 < pad:
        parts.append(gate_grad[:, base + 128 :])
    gate_up_grad = jnp.concatenate(parts + [up_grad], axis=1).astype(bf16)
    gate_grad_ref[...] = gate_up_grad
    out_part = dot(gated, down_ref[...]).astype(bf16)
    out_own_ref[...] = out_part[: n // 2]
    out_far_ref[...] = out_part[n // 2 :]
    rows_grad = dot(gate_up_grad, gate_ref[...]).astype(bf16)
    own_ref[...] = rows_grad[: n // 2]
    far_ref[...] = rows_grad[n // 2 :]


def cot_specs(cots, chunk):
    block = (1, 1) + cots.shape[2:]

    def spec(j):
        return pl.BlockSpec(block, lambda i, where: (where[chunk(i)[1] * 4 + j], chunk(i)[0], 0, 0))

    return [spec(j) for j in range(4)]


def ffn_chunks(first, chunks, where, rows, cots, gate_rows, down_rows, kept, units, experts):
    total, width = rows.shape
    steps = chunks * 2
    tile = total // (cots.shape[1] * 2)
    pad = down_rows.shape[0]

    def among(w):
        return pl.BlockSpec((tile, w), lambda i, where: (first * 2 + i, 0))

    def half(w):
        return pl.BlockSpec((tile // 2, w), lambda i, where: (i, 0))

    def whole(r):
        return pl.BlockSpec((r, width), lambda i, where: (0, 0), pipeline_mode=pl.Buffered(1))

    shapes = [(steps * tile // 2, width)] * 4 + [(total, pad), (total, 2 * pad)]
    kept = list(kept)
    return pl.pallas_call(
        functools.partial(ffn_kernel, units, pad, experts),
        grid_spec=pltpu.PrefetchScalarGridSpec(
            num_scalar_prefetch=1,
            grid=(steps,),
            in_specs=[among(width)]
            + cot_specs(cots, lambda i: (first + i // 2, i % 2))
            + [whole(2 * pad), whole(pad)]
            + [pl.BlockSpec(memory_space=pl.ANY)] * len(kept),
            out_specs=[half(width)] * 4 + [among(pad), among(2 * pad)],
        ),
        out_shape=[jax.ShapeDtypeStruct(shape, bf16) for shape in shapes],
        input_output_aliases={8 + i: 4 + i for i in range(len(kept))},
        compiler_params=pltpu.CompilerParams(vmem_limit_bytes=58 * 1024 * 1024),
        cost_estimate=pl.CostEstimate(
            flops=12 * steps * tile * width * pad,
            bytes_accessed=8 * steps * tile * width,
            transcendentals=2 * steps * tile * pad,
        ),
    )(where, rows, cots, cots, cots, cots, gate_rows, down_rows, *kept)


def down_grad_kernel(wide, where_ref, hidden_ref, c0, c1, c2, c3, out_ref, sums):
    step = pl.program_id(0)
    width = sums.shape[1]

    @pl.when(step == 0)
    def _():
        sums[...] = jnp.zeros_like(sums)

    sums[...] += dot_tn(hidden_ref[...], joined((c0, c1, c2, c3))[:, :width])

    @pl.when(step == pl.num_programs(0) - 1)
    def _():
        count, _, block = out_ref.shape
        for d in range(count):
            out_ref[d, :] = sums[:wide, d * block : (d + 1) * block].astype(bf16)


def down_grad(where, hidden, cots, width, wide, count):
    total, pad = hidden.shape
    steps = cots.shape[1] * 2
    shape = (count, wide, width // count)
    if not whole_tiles(wide, width // count):
        rows = jnp.moveaxis(cots[where[:8]], 0, 1).reshape(total, -1)[:, :width]
        return dot_over(hidden, rows)[:wide].reshape(wide, count, -1).transpose(1, 0, 2).astype(bf16)
    return pl.pallas_call(
        functools.partial(down_grad_kernel, wide),
        grid_spec=pltpu.PrefetchScalarGridSpec(
            num_scalar_prefetch=1,
            grid=(steps,),
            in_specs=[pl.BlockSpec((total // steps, pad), lambda i, where: (i, 0))]
            + cot_specs(cots, lambda i: (i // 2, i % 2)),
            out_specs=pl.BlockSpec(shape, lambda i, where: (0, 2, 0)),
            scratch_shapes=[pltpu.VMEM((pad, width), f32)],
        ),
        out_shape=jax.ShapeDtypeStruct((count, 3 * wide, width // count), bf16),
        compiler_params=pltpu.CompilerParams(vmem_limit_bytes=56 * 1024 * 1024),
        cost_estimate=pl.CostEstimate(flops=2 * total * pad * width, bytes_accessed=2 * total * (pad + width), transcendentals=0),
    )(where, hidden, cots, cots, cots, cots)


def gate_grad_kernel(wide, grad_ref, rows_ref, held_ref, out_ref, router_ref, sums):
    step = pl.program_id(0)

    @pl.when(step == 0)
    def _():
        sums[...] = jnp.zeros_like(sums)

    sums[...] += dot_tn(grad_ref[...], rows_ref[...])

    @pl.when(step == pl.num_programs(0) - 1)
    def _():
        count, _, block = out_ref.shape
        pad = sums.shape[0] // 2
        for d in range(count):
            lanes = slice(d * block, (d + 1) * block)
            out_ref[d, :wide] = sums[:wide, lanes].astype(bf16)
            out_ref[d, wide:] = sums[pad : pad + wide, lanes].astype(bf16)
        base = wide // 8 * 8
        router_ref[...] = sums[base : base + router_ref.shape[0]]


def gate_grad(gate_up_grad, rows, held, wide, count):
    total, pads = gate_up_grad.shape
    width = rows.shape[1]
    tile = 512
    shape = (count, 2 * wide, width // count)
    if not whole_tiles(wide, width // count):
        sums = dot_over(gate_up_grad, rows)
        base = wide // 8 * 8
        both = stack(sums[:wide], sums[pads // 2 : pads // 2 + wide])
        both = both.reshape(2 * wide, count, -1).transpose(1, 0, 2).astype(bf16)
        return jnp.concatenate([both, held], axis=1), sums[base : base + 24]
    return pl.pallas_call(
        functools.partial(gate_grad_kernel, wide),
        grid=(total // tile,),
        in_specs=[
            pl.BlockSpec((tile, pads), lambda i: (i, 0)),
            pl.BlockSpec((tile, width), lambda i: (i, 0)),
            pl.BlockSpec(memory_space=pl.ANY),
        ],
        input_output_aliases={2: 0},
        out_specs=[pl.BlockSpec(shape, lambda i: (0, 0, 0)), pl.BlockSpec((24, width), lambda i: (0, 0))],
        out_shape=[jax.ShapeDtypeStruct(held.shape, bf16), jax.ShapeDtypeStruct((24, width), f32)],
        scratch_shapes=[pltpu.VMEM((pads, width), f32)],
        compiler_params=pltpu.CompilerParams(vmem_limit_bytes=56 * 1024 * 1024),
        cost_estimate=pl.CostEstimate(flops=2 * total * pads * width, bytes_accessed=2 * total * (pads + width), transcendentals=0),
    )(gate_up_grad, rows, held)


def whole_tiles(units, rows):
    return units % 16 == 0 and rows % 128 == 0


def turn_kernel(shared_ref, routed_ref, gate_ref, down_ref):
    kind, who = pl.program_id(0), pl.program_id(1)

    def put(out_ref, block):
        count, units, rows = out_ref.shape
        out_ref[...] = block.T.reshape(count, units, rows)

    for last, out_ref in ((False, gate_ref), (True, down_ref)):
        for own, in_ref in ((False, shared_ref), (True, routed_ref)):

            @pl.when(((kind == 2) == last) & ((who > 0) == own))
            def _(out_ref=out_ref, in_ref=in_ref):
                put(out_ref, in_ref[...])


def turn_weights(shared, routed, count):
    rows, columns = shared.shape
    who = 1 + routed.shape[1] // columns
    span = columns // 3
    units = span // count
    if not whole_tiles(units, rows):
        both = jnp.concatenate([shared, routed], axis=1).reshape(rows, who, 3, count, units)
        both = both.transpose(3, 2, 1, 4, 0).reshape(count, -1, rows)
        return both[:, : 2 * who * units], both[:, 2 * who * units :]
    return pl.pallas_call(
        turn_kernel,
        grid=(3, who),
        in_specs=[
            pl.BlockSpec((rows, span), lambda k, w: (0, k)),
            pl.BlockSpec((rows, span), lambda k, w: (0, jnp.maximum(w - 1, 0) * 3 + k)),
        ],
        out_specs=[
            pl.BlockSpec((count, units, rows), lambda k, w: (0, jnp.where(k < 2, k * who + w, 2 * who - 1), 0)),
            pl.BlockSpec((count, units, rows), lambda k, w: (0, jnp.where(k < 2, 0, w), 0)),
        ],
        out_shape=[jax.ShapeDtypeStruct((count, k * who * units, rows), bf16) for k in (2, 1)],
        compiler_params=pltpu.CompilerParams(vmem_limit_bytes=32 * 1024 * 1024),
        cost_estimate=pl.CostEstimate(flops=0, bytes_accessed=4 * who * rows * columns, transcendentals=0),
    )(shared, routed)


def turn_back_kernel(grad_ref, shared_ref, routed_ref):
    count, wide, rows = grad_ref.shape
    who = 1 + routed_ref.shape[1]
    units = wide // who
    for w in range(who):
        block = grad_ref[:, w * units : (w + 1) * units, :].reshape(count * units, rows).T
        if w == 0:
            shared_ref[...] = block
        else:
            routed_ref[:, w - 1, :] = block.astype(f32)


def turn_grads(grad, experts):
    count, wide, rows = grad.shape
    wide = wide // 3
    span = wide // (1 + experts) * count
    if not whole_tiles(span // count, rows):
        both = grad.reshape(count, 3, 1 + experts, -1, rows)
        both = both.transpose(4, 2, 1, 0, 3).reshape(rows, 1 + experts, 3 * span)
        return both[:, 0], both[:, 1:].astype(f32)
    return pl.pallas_call(
        turn_back_kernel,
        grid=(3,),
        in_specs=[pl.BlockSpec((count, wide, rows), lambda k: (0, k, 0))],
        out_specs=[
            pl.BlockSpec((rows, span), lambda k: (0, k)),
            pl.BlockSpec((rows, experts, span), lambda k: (0, 0, k)),
        ],
        out_shape=[
            jax.ShapeDtypeStruct((rows, 3 * span), bf16),
            jax.ShapeDtypeStruct((rows, experts, 3 * span), f32),
        ],
        compiler_params=pltpu.CompilerParams(vmem_limit_bytes=56 * 1024 * 1024),
        cost_estimate=pl.CostEstimate(flops=0, bytes_accessed=6 * count * wide * rows + 10 * rows * span * 3, transcendentals=0),
    )(grad)


def deal_kernel(share, dense_ref, attn_ref, shared_ref):
    width = share * 8
    for o in range(8):
        for k in range(4):
            at = k * width + o * share
            attn_ref[o, :, k * share : (k + 1) * share] = dense_ref[:, at : at + share]
    owners, _, columns = shared_ref.shape
    span = columns // 3
    for o in range(owners):
        for k in range(3):
            at = 4 * width + (k * owners + o) * span
            shared_ref[o, :, k * span : (k + 1) * span] = dense_ref[:, at : at + span]


def deal_columns(dense, share, owners):
    rows, columns = dense.shape
    shapes = [(8, rows, 4 * share), (owners, rows, (columns - 32 * share) // owners)]
    return pl.pallas_call(
        functools.partial(deal_kernel, share),
        out_shape=[jax.ShapeDtypeStruct(shape, bf16) for shape in shapes],
        compiler_params=pltpu.CompilerParams(vmem_limit_bytes=32 * 1024 * 1024),
        cost_estimate=pl.CostEstimate(flops=0, bytes_accessed=4 * rows * columns, transcendentals=0),
    )(dense)


def collect_kernel(share, attn_ref, shared_ref, dense_ref):
    width = share * 8
    for o in range(8):
        for k in range(4):
            at = k * width + o * share
            dense_ref[:, at : at + share] = attn_ref[o, :, k * share : (k + 1) * share].astype(f32)
    owners, _, columns = shared_ref.shape
    span = columns // 3
    for o in range(owners):
        for k in range(3):
            at = 4 * width + (k * owners + o) * span
            dense_ref[:, at : at + span] = shared_ref[o, :, k * span : (k + 1) * span].astype(f32)


def collect_columns(attn, shared, share):
    rows = attn.shape[1]
    columns = 32 * share + shared.shape[0] * shared.shape[2]
    return pl.pallas_call(
        functools.partial(collect_kernel, share),
        out_shape=jax.ShapeDtypeStruct((rows, columns), f32),
        compiler_params=pltpu.CompilerParams(vmem_limit_bytes=32 * 1024 * 1024),
        cost_estimate=pl.CostEstimate(flops=0, bytes_accessed=6 * rows * columns, transcendentals=0),
    )(attn, shared)


def place_kernel(wide, pad, *refs):
    out_ref = refs[-1]
    for k in range(out_ref.shape[0] // pad):
        out_ref[k * pad : k * pad + wide] = refs[0][0, k * wide : (k + 1) * wide]
        if k == 0 and len(refs) > 2:
            out_ref[wide:pad] = refs[1][...]
        else:
            out_ref[k * pad + wide : (k + 1) * pad] = jnp.zeros((pad - wide, out_ref.shape[1]), bf16)


def place_weights(ffn, wide, pad, *router):
    count, units, block = ffn.shape
    width = count * block
    rows = units // wide * pad
    if not whole_tiles(wide, block):
        parts = ffn.transpose(1, 0, 2).reshape(units // wide, wide, width)
        blank = jnp.zeros((pad - wide, width), bf16)
        return stack(*[v for k in range(units // wide) for v in (parts[k], *(router if k == 0 and router else (blank,)))])

    def column(r):
        return pl.BlockSpec((r, block), lambda i: (0, i))

    return pl.pallas_call(
        functools.partial(place_kernel, wide, pad),
        grid=(count,),
        in_specs=[pl.BlockSpec((1, units, block), lambda i: (i, 0, 0))] + [column(pad - wide)] * len(router),
        out_specs=column(rows),
        out_shape=jax.ShapeDtypeStruct((rows, width), bf16),
        compiler_params=pltpu.CompilerParams(vmem_limit_bytes=32 * 1024 * 1024),
        cost_estimate=pl.CostEstimate(flops=0, bytes_accessed=2 * (rows + units) * width, transcendentals=0),
    )(ffn, *router)


def attend_rows(queries, keys, allowed):
    scores = jnp.where(allowed, dot_nt(queries, keys) * HD ** (-0.5), -1e30)
    raw = jnp.exp(scores - jnp.max(scores, axis=1, keepdims=True))
    return raw / jnp.sum(raw, axis=1, keepdims=True)


def allowed_pairs(own_ref, all_ref):
    return (own_ref[:, :1] == all_ref[0, :1]) & (all_ref[0, 1:2] <= own_ref[:, 1:2])


def piece_at(where_ref, s, piece_ref):
    size = piece_ref.shape[0]
    return pl.ds(pl.multiple_of(where_ref[s] * size, size), size)


def attend_kernel(heads, where_ref, rows_ref, bias_ref, cosine_ref, sine_ref, own_ref, all_ref, *refs):
    pieces, (packed_ref, mixed_ref) = refs[:-2], refs[-2:]
    share = heads * HD
    packed = bias_ref[...]
    for s, piece in enumerate(pieces):
        packed = packed + dot(rows_ref[:, piece_at(where_ref, s, piece)], piece[...])
    cosine, sine = cosine_ref[...], sine_ref[...]
    allowed = allowed_pairs(own_ref, all_ref)

    def turned(at):
        v = packed[:, at : at + HD]
        return (v * cosine + pltpu.roll(v, HD // 2, 1) * sine).astype(bf16)

    for h in range(heads):
        queries, keys = turned(h * HD), turned(share + h * HD)
        values = packed[:, 2 * share + h * HD : 2 * share + (h + 1) * HD].astype(bf16)
        attend = attend_rows(queries, keys, allowed)
        mixed_ref[:, h * HD : (h + 1) * HD] = dot(attend.astype(bf16), values).astype(bf16)
        for k, v in enumerate((queries, keys, values)):
            packed_ref[:, k * share + h * HD : k * share + (h + 1) * HD] = v


def project_kernel(where_ref, mixed_ref, *refs):
    pieces, (near_ref, far_ref) = refs[:-2], refs[-2:]
    half = near_ref.shape[0]
    for s, piece in enumerate(pieces):
        rows = dot_nt(mixed_ref[...], piece[...]).astype(bf16)
        columns = piece_at(where_ref, s, piece)
        near_ref[:, columns] = rows[:half]
        far_ref[:, columns] = rows[half:]


def attend_back_kernel(heads, where_ref, grad_ref, packed_ref, cosine_ref, sine_ref, own_ref, all_ref, *refs):
    pieces, (packed_grad_ref, near_ref, far_ref, bias_ref) = refs[:-4], refs[-4:]
    rings = len(pieces) // 2
    share = heads * HD
    scale = HD ** (-0.5)
    mixed_grad = 0.0
    for s, piece in enumerate(pieces[rings:]):
        mixed_grad = mixed_grad + dot(grad_ref[:, piece_at(where_ref, s, piece)], piece[...])
    mixed_grad = mixed_grad.astype(bf16)
    cosine, sine = cosine_ref[...], sine_ref[...]
    allowed = allowed_pairs(own_ref, all_ref)

    def back(v):
        v = v.astype(bf16).astype(f32)
        return (v * cosine - pltpu.roll(v, HD // 2, 1) * sine).astype(bf16)

    for h in range(heads):
        queries, keys, values = (
            packed_ref[:, k * share + h * HD : k * share + (h + 1) * HD] for k in range(3)
        )
        own_grad = mixed_grad[:, h * HD : (h + 1) * HD]
        attend = attend_rows(queries, keys, allowed)
        attend_grad = dot_nt(own_grad, values)
        scores_grad = attend * (attend_grad - jnp.sum(attend * attend_grad, axis=1, keepdims=True))
        scores_grad = scores_grad.astype(bf16)
        grads = (
            back(dot(scores_grad, keys) * scale),
            back(dot_tn(scores_grad, queries) * scale),
            dot_tn(attend.astype(bf16), own_grad).astype(bf16),
        )
        for k, v in enumerate(grads):
            packed_grad_ref[:, k * share + h * HD : k * share + (h + 1) * HD] = v
    packed_grad = packed_grad_ref[...]
    bias_ref[...] = jnp.broadcast_to(jnp.sum(packed_grad.astype(f32), axis=0, keepdims=True), bias_ref.shape)
    half = near_ref.shape[0]
    for s, piece in enumerate(pieces[:rings]):
        rows_grad = dot_nt(packed_grad, piece[...]).astype(bf16)
        columns = piece_at(where_ref, s, piece)
        near_ref[:, columns] = rows_grad[:half]
        far_ref[:, columns] = rows_grad[half:]


def group_call(kernel, group_len, where, operands, specs, pieces, out_widths, out_types, flops):
    def spec(kind, shape):
        if kind == "rows":
            return pl.BlockSpec((group_len, shape[1]), lambda i, where: (i, 0))
        if kind == "pair":
            return pl.BlockSpec((1,) + shape[1:], lambda i, where: (i, 0, 0))
        return pl.BlockSpec(shape, lambda i, where: (0, 0), pipeline_mode=pl.Buffered(1))

    operands = tuple(operands) + tuple(pieces)
    specs = tuple(specs) + ("all",) * len(pieces)
    return pl.pallas_call(
        kernel,
        grid_spec=pltpu.PrefetchScalarGridSpec(
            num_scalar_prefetch=1,
            grid=(2,),
            in_specs=[spec(k, v.shape) for k, v in zip(specs, operands)],
            out_specs=[pl.BlockSpec((r, w), lambda i, where: (i, 0)) for r, w in out_widths],
        ),
        out_shape=[jax.ShapeDtypeStruct((2 * r, w), t) for (r, w), t in zip(out_widths, out_types)],
        compiler_params=pltpu.CompilerParams(vmem_limit_bytes=48 * 1024 * 1024),
        cost_estimate=pl.CostEstimate(flops=flops, bytes_accessed=sum(2 * v.size for v in operands), transcendentals=0),
    )(where, *operands)


def body(lay, tokens, dense_weights, expert_weights, gain_attn, gain_ffn, qkv_bias, router_weight, routes, doc_ids, out_grad):
    row_count, model_width = tokens.shape
    rings = lay.rings
    ring = lax.axis_index("ring")
    pair = lax.axis_index("pair")
    ep = lax.axis_index("ep")
    local_experts = expert_weights.shape[1]
    expert_count = router_weight.shape[1] - 1
    owners = expert_count // local_experts
    dp_count = rings * 2
    ring_place = jnp.asarray(lay.place, jnp.int32)[ring]
    behind = [jnp.asarray(lay.order, jnp.int32)[(ring_place - s) % rings] for s in range(rings)]
    ring_order = jnp.stack(behind)
    own_expert = ep * local_experts
    where = []
    for dx in range(2):
        for dc in range(2):
            for dy in range(2):
                where.append((pair ^ dy) * 4 + (ep ^ (2 * dx + dc)))
    where = jnp.stack(where + [own_expert]).astype(jnp.int32)

    stream = tokens.astype(f32)
    gain_one = gain_attn.astype(f32)
    gain_two = gain_ffn.astype(f32)
    heads = H // 8
    share = heads * HD
    unit_share = SFF // owners
    units = FF // dp_count
    wide = 3 * units
    pad = (wide + expert_count + 1 + 127) // 128 * 128
    n = row_count

    mine, shared = deal_columns(dense_weights, share, owners)
    bits = jnp.sum(jnp.left_shift(jnp.int32(1), routes), axis=1, keepdims=True).astype(bf16)
    cot_blocks = [jnp.concatenate([out_grad, jnp.broadcast_to(bits, (row_count, 128))], axis=1)]
    mine, shared, cot_blocks[0] = together(mine, shared, cot_blocks[0])
    plane_part = lax.all_to_all(mine, PLANE, split_axis=0, concat_axis=0, tiled=True)
    plane_part = plane_part.reshape(-1, 4 * share)
    for _ in range(rings - 2):
        cot_blocks.append(permute(cot_blocks[-1], lay.onward))

    inverse_one = lax.rsqrt(jnp.mean(stream * stream, axis=1, keepdims=True) + norm_eps)
    normed = (stream * inverse_one * gain_one).astype(bf16)
    doc_pair = jnp.stack([doc_ids, permute(doc_ids, lay.up)])
    group_len = doc_ids.shape[0]
    before = jnp.sum((doc_pair[:, None, :] < doc_pair[:, :, None]).astype(jnp.int32), axis=2)
    spot = jnp.arange(group_len, dtype=jnp.int32)
    near_blocks = jnp.stack([ep, ep ^ 2, ep ^ 1, ep ^ 3])

    def in_order(values):
        return values.reshape(2, 4, row_count)[:, near_blocks].reshape(2, group_len)

    places = in_order(spot[None, :] - before)
    docs = in_order(doc_pair)
    spots = in_order(jnp.stack([spot, spot]))
    cosine, sine = rope_tables(places.reshape(-1))
    sine = jnp.where(jnp.arange(HD) < HD // 2, -sine, sine)
    spots_all = jnp.stack([docs, spots], axis=1)
    spots_own = jnp.stack([docs.reshape(-1), spots.reshape(-1)], axis=1)
    routed = expert_weights.reshape(expert_weights.shape[0], -1)
    router = router_weight.T
    turn = (own_expert + jnp.arange(expert_count, dtype=jnp.int32)) % expert_count
    router = stack(
        jnp.take(router, turn, axis=0),
        router[expert_count:],
        jnp.zeros((pad - wide - expert_count - 1, model_width), bf16),
    )
    slot = pair * 4 + ep
    bias_share = lax.dynamic_slice_in_dim(qkv_bias.astype(f32).reshape(3, 8, share), slot, 1, 1).reshape(1, 3 * share)
    plane_part, cot_blocks[-1], routed, normed, shared = together(plane_part, cot_blocks[-1], routed, normed, shared)

    qkv = [plane_part[:, : 3 * share]]
    qkv.append(permute(qkv[0], lay.onward))
    cot_blocks.append(permute(cot_blocks[-1], lay.onward))
    shared = lax.all_to_all(shared, "ep", split_axis=0, concat_axis=0, tiled=True)
    side, up = permute(normed, lay.side), permute(normed, lay.up)
    qkv[-1], cot_blocks[-1], side, up, cosine, sine = together(qkv[-1], cot_blocks[-1], side, up, cosine, sine)
    cross = permute(up, lay.side)
    near = stack(normed, side)
    near_core = permute(near, lay.core)
    for s in range(2, rings):
        qkv.append(permute(qkv[-1], lay.onward))
        if s == 2:
            gate_ffn, down_ffn = turn_weights(shared.reshape(routed.shape[0], 3 * unit_share), routed, dp_count)
            far = stack(up, cross)
            qkv[-1], near_core, far, gate_ffn, down_ffn = together(qkv[-1], near_core, far, gate_ffn, down_ffn)
            cots = lax.all_gather(after(jnp.stack(cot_blocks), qkv[-1]), PLANE, axis=0, tiled=False)
            far_core = permute(far, lay.core)
    normed_group = stack(near, near_core, far, far_core)
    qkv[-1], normed_group = together(qkv[-1], normed_group)

    outs = [plane_part[:, 3 * share :]]
    for _ in range(rings - 1):
        outs.append(permute(outs[-1] if len(outs) > 1 else after(outs[0], qkv[-1]), lay.onward))
    heads_flops = 8 * heads * group_len * group_len * HD
    packed, mixed = group_call(
        functools.partial(attend_kernel, heads),
        group_len,
        ring_order,
        (normed_group, bias_share, cosine, sine, spots_own, spots_all),
        ("rows", "all", "rows", "rows", "rows", "pair"),
        qkv,
        [(group_len, 3 * share), (group_len, share)],
        [bf16, bf16],
        4 * group_len * model_width * 3 * share + heads_flops,
    )
    down_ffn = lax.all_to_all(after(down_ffn, outs[-1]), ("ring", "pair"), split_axis=0, concat_axis=0, tiled=True)
    branch_parts = group_call(
        project_kernel,
        group_len,
        ring_order,
        (mixed,),
        ("rows",),
        outs,
        [(group_len // 2, model_width)] * 2,
        [bf16, bf16],
        4 * group_len * model_width * share,
    )
    branch = plane_sums(lay, *branch_parts)
    residual = stream + branch
    inverse_two = lax.rsqrt(jnp.mean(residual * residual, axis=1, keepdims=True) + norm_eps)
    normed_two = (residual * inverse_two * gain_two).astype(bf16)
    normed_two = after(normed_two, down_ffn)

    blocks, ups, sides, crosses = [normed_two], [], [], []
    for s in range(rings):
        up, side = permute(blocks[s], lay.up), permute(blocks[s], lay.side)
        sides.append(side)
        if s > 0:
            crosses.append(permute(ups[-1], lay.side))
        if s < rings - 1:
            onward = permute(blocks[s], lay.onward)
            onward, up = together(onward, up)
            blocks.append(onward)
        else:
            up = after(up, blocks[-1])
        ups.append(up)
    gate_ffn = lax.all_to_all(after(gate_ffn, ups[-1]), ("ring", "pair"), split_axis=0, concat_axis=0, tiled=True)
    crosses.append(permute(ups[-1], lay.side))
    down_rows = place_weights(down_ffn, wide, pad)
    rows = []
    for s in range(rings):
        for pieces in ((blocks[s], ups[s]), (sides[s], crosses[s])):
            rows += pieces
            rows += [permute(piece, lay.core) for piece in pieces]
    rows = stack(*rows)
    gate_rows = place_weights(gate_ffn, wide, pad, router)

    chunk, half = 4 * n, 2 * n
    order = list(range(rings))[::-1]
    late = rings // 2
    first_half, last_half = order[: rings - late], order[rings - late :]

    def cut_chunk(which, s, at):
        begin = (s % late if s < late else s - late) * chunk + at
        return which[begin : begin + half]

    def crossed(part, there, some):
        keep = {s: plus(cut_chunk(part, s, 0), cut_chunk(there, s, 0)) for s in some}
        send = {s: plus(cut_chunk(part, s, half), cut_chunk(there, s, half)) for s in some}
        return keep, send

    def all_there(*groups):
        flat, tree = jax.tree.flatten(groups)
        return jax.tree.unflatten(tree, lax.optimization_barrier(tuple(flat)))

    def ffn_half(first, chunks, kept):
        return ffn_chunks(first, chunks, where, rows, cots, gate_rows, down_rows, kept, units, expert_count)

    out_own_a, out_far_a, own_a, far_a, hidden, gate_up_grad = ffn_half(late, rings - late, ())

    keep, send = crossed(own_a, permute(far_a, lay.core), first_half)
    keep, send, hidden, gate_up_grad = all_there(keep, send, hidden, gate_up_grad)
    sided = {s: permute(send[s], lay.side) for s in first_half}
    out_own_b, out_far_b, own_b, far_b, hidden, gate_up_grad = ffn_half(0, late, (hidden, gate_up_grad))
    sided, own_b, far_b, hidden, gate_up_grad = all_there(sided, own_b, far_b, hidden, gate_up_grad)

    far_there = permute(far_b, lay.core)
    halves = {s: plus(keep[s], sided[s]) for s in first_half}
    keep, send = crossed(own_b, far_there, last_half)
    keep, send, halves, hidden = all_there(keep, send, halves, hidden)

    few = (len(last_half) + 1) // 2
    sided = {s: permute(send[s], lay.side) for s in last_half[:few]}
    upped = {s: permute(halves[s][n:], lay.up) for s in first_half}
    ffn_grad = down_grad(where, hidden, cots, model_width, wide, dp_count)
    sided, upped, ffn_grad, gate_up_grad = all_there(sided, upped, ffn_grad, gate_up_grad)

    own_sums = {s: halves[s][:n].astype(f32) + upped[s].astype(f32) for s in first_half}
    total = own_sums[order[0]]
    queue = list(order[1:])

    def step_on(total):
        return permute(total.astype(bf16), lay.backward)

    def step_in(arrived):
        return own_sums[queue.pop(0)] + arrived.astype(f32)

    halves = {s: plus(keep[s], sided[s]) for s in last_half[:few]}
    sided = {s: permute(send[s], lay.side) for s in last_half[few:]}
    upped = {s: permute(halves[s][n:], lay.up) for s in last_half[:few]}
    moving = step_on(total)
    ffn_grad, router_part = gate_grad(gate_up_grad, rows, ffn_grad, wide, dp_count)
    sided, upped, moving, ffn_grad = all_there(sided, upped, moving, ffn_grad)
    total = step_in(moving)
    own_sums.update({s: halves[s][:n].astype(f32) + upped[s].astype(f32) for s in last_half[:few]})

    halves = {s: plus(keep[s], sided[s]) for s in last_half[few:]}
    upped = {s: permute(halves[s][n:], lay.up) for s in last_half[few:]}
    moving = step_on(total)
    upped, moving = all_there(upped, moving)
    total = step_in(moving)
    own_sums.update({s: halves[s][:n].astype(f32) + upped[s].astype(f32) for s in last_half[few:]})
    while queue:
        total = step_in(step_on(total))
    normed_two_grad = total

    start = wide - wide // 8 * 8
    router_part = router_part[start : start + expert_count + 1]
    turn_back = (jnp.arange(expert_count, dtype=jnp.int32) - own_expert) % expert_count
    router_part = stack(jnp.take(router_part[:expert_count], turn_back, axis=0), router_part[expert_count:])

    cotangent = out_grad.astype(f32)
    scaled_two = normed_two_grad * gain_two
    gain_two_grad = jnp.sum(normed_two_grad * residual * inverse_two, axis=0)
    residual_grad = (
        cotangent
        + inverse_two * scaled_two
        - residual * inverse_two**3 * jnp.mean(scaled_two * residual, axis=1, keepdims=True)
    )
    branch_grad = residual_grad.astype(bf16)

    side, up = permute(branch_grad, lay.side), permute(branch_grad, lay.up)
    side, up, ffn_grad = together(side, up, ffn_grad)
    ffn_grad = lax.all_to_all(ffn_grad, ("ring", "pair"), split_axis=0, concat_axis=0, tiled=True)
    near, far = stack(branch_grad, side), stack(up, permute(up, lay.side))
    branch_grad_group = stack(near, permute(near, lay.core), far, permute(far, lay.core))
    packed_grad, near, far, bias_part = group_call(
        functools.partial(attend_back_kernel, heads),
        group_len,
        ring_order,
        (branch_grad_group, packed, cosine, sine, spots_own, spots_all),
        ("rows", "rows", "rows", "rows", "rows", "pair"),
        qkv + outs,
        [(group_len, 3 * share), (group_len // 2, model_width), (group_len // 2, model_width), (8, 3 * share)],
        [bf16, bf16, bf16, f32],
        4 * group_len * model_width * 4 * share + 3 * heads_flops,
    )
    normed_grad = plane_sums(lay, near, far)

    out_there = [permute(after(v, up), lay.core) for v in (out_far_a, out_far_b)]
    keep, send = crossed(out_own_a, out_there[0], first_half)
    more_keep, more_send = crossed(out_own_b, out_there[1], last_half)
    keep.update(more_keep)
    send.update(more_send)
    sided = {s: permute(after(send[s], branch_grad_group), lay.side) for s in first_half}
    sided.update({s: permute(after(send[s], far), lay.side) for s in last_half})
    halves = {s: plus(keep[s], sided[s]) for s in order}
    upped = {s: permute(halves[s][n:], lay.up) for s in order}
    out_sums = {s: halves[s][:n].astype(f32) + upped[s].astype(f32) for s in order}

    scaled_one = normed_grad * gain_one
    gain_one_grad = jnp.sum(normed_grad * stream * inverse_one, axis=0)
    input_grad = (
        residual_grad
        + inverse_one * scaled_one
        - stream * inverse_one**3 * jnp.mean(scaled_one * stream, axis=1, keepdims=True)
    )
    bias_part = (bias_part[0] + bias_part[8]).reshape(3, 1, share)
    bias_part = lax.dynamic_update_slice(jnp.zeros((3, 8, share), f32), bias_part, (0, slot, 0))
    small = stack(router_part, gain_two_grad[None], gain_one_grad[None], bias_part.reshape(3, model_width))
    doubling = lay.doubling()
    for step in doubling[:3]:
        small = small + permute(small, step)

    attn_grads = jnp.concatenate([dot_over(normed_group, packed_grad), dot_over(branch_grad_group, mixed)], axis=1)
    attn_grads = attn_grads.astype(bf16).reshape(rings, -1, 4 * share)
    shared_grad, expert_grad = turn_grads(after(ffn_grad, attn_grads), local_experts)
    shared_grad = lax.all_to_all(
        shared_grad.reshape(owners, -1, 3 * unit_share), "ep", split_axis=0, concat_axis=0, tiled=True
    )
    attn_grads, out_sums, small, shared_grad = all_there(attn_grads, out_sums, small, shared_grad)
    total, output_sum, more = None, None, doubling[3:]
    for i, s in enumerate(order):
        here = lax.dynamic_index_in_dim(attn_grads, behind[s], 0, keepdims=False).astype(f32)
        if i > 0:
            total, out_moving, small = together(total.astype(bf16), output_sum.astype(bf16), small)
            if i == rings - 1:
                total, shared_grad, expert_grad = together(total, shared_grad, expert_grad)
            here = here + permute(total, lay.backward).astype(f32)
            output_sum = out_sums[s] + permute(out_moving, lay.backward).astype(f32)
            if more:
                small = small + permute(small, more.pop(0))
        else:
            output_sum = out_sums[s]
        total = here
    output = (residual + output_sum).astype(bf16)
    total = total.astype(bf16).reshape(8, -1, 4 * share)
    total = lax.all_to_all(total, PLANE, split_axis=0, concat_axis=0, tiled=True)
    dense_grad = collect_columns(total, shared_grad, share)

    router_sum, gain_two_sum, gain_one_sum, bias_sum = jnp.split(small, [expert_count + 1, expert_count + 2, expert_count + 3])
    return (
        output,
        input_grad,
        dense_grad,
        expert_grad,
        gain_one_sum[0],
        gain_two_sum[0],
        bias_sum.reshape(-1),
        router_sum.T,
    )


def solution(mesh):
    devices = mesh.devices
    lay = Layout(devices.shape[0] // 2)
    inner = Mesh(devices.reshape(lay.rings, 2, devices.shape[1]), AXES)
    rows = P(AXES, None)
    experts = P(("ring", "pair"), "ep", None)
    in_specs = (rows, rows, experts, P(), P(), P(), P(), rows, P(("ring", "pair")), rows)
    out_specs = (rows, rows, rows, experts, P(), P(), P(), P())

    def run(*arguments):
        return body(lay, *arguments)

    return jax.shard_map(run, mesh=inner, in_specs=in_specs, out_specs=out_specs, check_vma=False)
```

```python
import functools

import jax
import jax.numpy as jnp
from jax import lax
from jax.experimental import pallas as pl
from jax.experimental.pallas import tpu as pltpu
from jax.sharding import Mesh, PartitionSpec as P

H = 16
HD = 128
FF = 1408
SFF = 5632

norm_eps = 1e-06
rope_base = 1000000.0
AXES = ("ring", "pair", "ep")
PLANE = ("pair", "ep")
SHARED = -1
f32 = jnp.float32
bf16 = jnp.bfloat16


class Layout:
    def __init__(self, rings):
        self.rings = rings
        self.order = list(range(0, rings, 2)) + list(range(1, rings, 2))[::-1]
        place = {r: i for i, r in enumerate(self.order)}
        self.place = [place[r] for r in range(rings)]
        self.core = self.pairs(lambda r, y, x, c: (r, y, x, 1 - c))
        self.side = self.pairs(lambda r, y, x, c: (r, y, 1 - x, c))
        self.side_core = self.pairs(lambda r, y, x, c: (r, y, 1 - x, 1 - c))
        self.up = self.pairs(lambda r, y, x, c: (r, 1 - y, x, c))
        self.cross = self.pairs(lambda r, y, x, c: (r, 1 - y, 1 - x, c))
        self.onward = self.pairs(lambda r, y, x, c: (self.order[(place[r] + 1) % rings], y, x, c))
        self.backward = self.pairs(lambda r, y, x, c: (self.order[(place[r] - 1) % rings], y, x, c))

    def pairs(self, move):
        found = []
        for r in range(self.rings):
            for y in range(2):
                for x in range(2):
                    for c in range(2):
                        u, v, w, q = move(r, y, x, c)
                        found.append((((r * 2 + y) * 2 + x) * 2 + c, ((u * 2 + v) * 2 + w) * 2 + q))
        return found

    def doubling(self):
        steps = []
        bit = 1
        while bit < self.rings * 8:
            steps.append([(i, i ^ bit) for i in range(self.rings * 8)])
            bit *= 2
        return steps


def permute(rows, pairs):
    return lax.ppermute(rows, AXES, pairs)


def stack(*parts):
    return jnp.concatenate(parts, axis=0)


def plus(a, b):
    return (a.astype(f32) + b.astype(f32)).astype(bf16)


def assemble_kernel(*refs):
    parts, out_ref, sems = refs[:-2], refs[-2], refs[-1]
    copies, at = [], 0
    for i, part in enumerate(parts):
        size = part.shape[0]
        copies.append(pltpu.make_async_copy(part, out_ref.at[pl.ds(at, size)], sems.at[i]))
        copies[-1].start()
        at += size
    for copy in copies:
        copy.wait()


def assemble(parts):
    rows = sum(part.shape[0] for part in parts)
    width = parts[0].shape[1]
    if rows * width > 1 << 24:
        return stack(*parts)
    return pl.pallas_call(
        assemble_kernel,
        in_specs=[pl.BlockSpec(memory_space=pltpu.VMEM)] * len(parts),
        out_specs=pl.BlockSpec(memory_space=pl.ANY),
        out_shape=jax.ShapeDtypeStruct((rows, width), bf16),
        scratch_shapes=[pltpu.SemaphoreType.DMA((len(parts),))],
        compiler_params=pltpu.CompilerParams(vmem_limit_bytes=48 * 1024 * 1024),
        cost_estimate=pl.CostEstimate(flops=0, bytes_accessed=4 * rows * width, transcendentals=0),
    )(*parts)


def rope_tables(places):
    steps_along = jnp.arange(HD // 2, dtype=f32) * (2.0 / HD)
    inverse = jnp.power(jnp.float32(rope_base), -steps_along)
    angles = places.astype(f32)[..., None] * inverse
    angles = jnp.concatenate([angles, angles], axis=-1)
    return jnp.cos(angles), jnp.sin(angles)


def dot(a, b):
    return jnp.dot(a, b, preferred_element_type=f32)


def dot_over(a, b):
    return jnp.einsum("tc,tf->cf", a, b, preferred_element_type=f32)


def after(value, *others):
    return lax.optimization_barrier((value,) + others)[0]


def together(*values):
    return lax.optimization_barrier(values)


def dot_nt(a, b):
    return lax.dot_general(a, b, (((1,), (1,)), ((), ())), preferred_element_type=f32)


def dot_tn(a, b):
    return lax.dot_general(a, b, (((0,), (0,)), ((), ())), preferred_element_type=f32)


def units_pass(gate_up, hidden_grad, gates):
    pad = hidden_grad.shape[1]
    g, u = gate_up[:, :pad], gate_up[:, pad:]
    sig = jax.nn.sigmoid(g)
    silu = g * sig
    hidden = (silu * u).astype(bf16).astype(f32)
    gated_grad = hidden_grad * gates
    up_grad = gated_grad * silu
    gate_grad = gated_grad * u * (sig + silu * (1.0 - sig))
    return (gates * hidden).astype(bf16), gate_grad, up_grad, hidden_grad * hidden


def with_logits(gate_grad, logit_grad, up_grad, base, at):
    lane = lax.broadcasted_iota(jnp.int32, logit_grad.shape, 1)
    parts = [gate_grad[:, :base]] if base else []
    parts.append(jnp.where(lane < at, gate_grad[:, base : base + 128], logit_grad))
    if base + 128 < gate_grad.shape[1]:
        parts.append(gate_grad[:, base + 128 :])
    return jnp.concatenate(parts + [up_grad], axis=1).astype(bf16)


def hand_out(wide, gate_sums, down_sums, out_ref, router_ref):
    pad = down_sums.shape[0]
    first = wide // 8 * 8
    router_ref[...] = gate_sums[first : first + router_ref.shape[0]]
    if len(out_ref.shape) == 2:
        out_ref[: 2 * pad] = gate_sums[...].astype(bf16)
        out_ref[2 * pad :] = down_sums[...].astype(bf16)
        return
    count, _, block = out_ref.shape
    for d in range(count):
        lanes = slice(d * block, (d + 1) * block)
        out_ref[d, :wide] = gate_sums[:wide, lanes].astype(bf16)
        out_ref[d, wide : 2 * wide] = gate_sums[pad : pad + wide, lanes].astype(bf16)
        out_ref[d, 2 * wide :] = down_sums[:wide, lanes].astype(bf16)


def add_grads(grad, rows, hidden, cots, gate_sums, down_sums):
    @pl.when(pl.program_id(0) == 0)
    def _():
        gate_sums[...] = jnp.zeros_like(gate_sums)
        down_sums[...] = jnp.zeros_like(down_sums)

    gate_sums[...] += dot_tn(grad, rows)
    down_sums[...] += dot_tn(hidden, cots)


def group_pass(groups, units, experts, where_ref, rows_ref, cots_ref, gate_ref, down_ref):
    n, width = rows_ref.shape
    pad = down_ref.shape[0]
    wide = units * len(groups)
    base = wide // 128 * 128
    at = wide - base
    gate_up = dot_nt(rows_ref[...], gate_ref[...])
    hidden_grad = dot_nt(cots_ref[:, :width], down_ref[...])
    logits = gate_up[:, base : base + 128]
    place = lax.broadcasted_iota(jnp.int32, (n, 128), 1) - at
    routed = (place >= 0) & (place < experts)
    bits = cots_ref[:, width : width + 128].astype(f32).astype(jnp.int32)
    turn = jnp.where(routed, lax.rem(where_ref[0] + place, experts), 0)
    chosen = (jnp.right_shift(bits, turn) & 1).astype(f32)
    peak = jnp.max(jnp.where(routed, logits, -jnp.inf), axis=1, keepdims=True)
    weights = jnp.where(routed, jnp.exp(logits - peak), 0.0)
    probs = weights / jnp.sum(weights, axis=1, keepdims=True)
    shared = jax.nn.sigmoid(logits)
    spot = lax.broadcasted_iota(jnp.int32, (128, pad), 1)
    lane = lax.broadcasted_iota(jnp.int32, (128, pad), 0) - at
    spread = jnp.zeros((128, pad), f32)
    for i, group in enumerate(groups):
        own = (spot >= i * units) & (spot < (i + 1) * units) & (lane == (experts if group == SHARED else group))
        spread = jnp.where(own, 1.0, spread)
    spread = spread.astype(bf16)
    gates = dot(jnp.where(place == experts, shared, probs * chosen).astype(bf16), spread)
    gated, gate_grad, up_grad, products = units_pass(gate_up, hidden_grad, gates)
    sums = dot_nt(products.astype(bf16), spread)
    own = sums * chosen
    mean = jnp.sum(jnp.where(routed, probs * own, 0.0), axis=1, keepdims=True)
    logit_grad = jnp.where(routed, probs * (own - mean), jnp.where(place == experts, sums * shared * (1.0 - shared), 0.0))
    return gated, with_logits(gate_grad, logit_grad, up_grad, base, at)


def first_kernel(
    groups, units, experts, where_ref, rows_ref, cots_ref, gate_ref, down_ref, hidden_ref, grad_ref, out_ref, router_ref, gate_sums, down_sums
):
    gated, grad = group_pass(groups, units, experts, where_ref, rows_ref, cots_ref, gate_ref, down_ref)
    hidden_ref[...] = gated
    grad_ref[...] = grad
    add_grads(grad, rows_ref[...], gated, cots_ref[:, : rows_ref.shape[1]], gate_sums, down_sums)

    @pl.when(pl.program_id(0) == pl.num_programs(0) - 1)
    def _():
        hand_out(units * len(groups), gate_sums, down_sums, out_ref, router_ref)


def grads_kernel(wide, where_ref, rows_ref, cots_ref, hidden_ref, grad_ref, out_ref, router_ref, gate_sums, down_sums):
    cots = cots_ref[:, : rows_ref.shape[1]]
    add_grads(grad_ref[...], rows_ref[...], hidden_ref[...], cots, gate_sums, down_sums)

    @pl.when(pl.program_id(0) == pl.num_programs(0) - 1)
    def _():
        hand_out(wide, gate_sums, down_sums, out_ref, router_ref)


def second_kernel(
    groups, units, experts, where_ref, rows_ref, cots_ref, hidden_in_ref, grad_in_ref, gate_in_ref, down_in_ref, gate_ref, down_ref, *refs
):
    out_own_ref, out_far_ref, own_ref, far_ref, hidden_ref, grad_ref = refs[-6:]
    half = own_ref.shape[0]
    gated, grad = group_pass(groups, units, experts, where_ref, rows_ref, cots_ref, gate_ref, down_ref)
    hidden_ref[...] = gated
    grad_ref[...] = grad
    rows_grad = (dot(grad_in_ref[...], gate_in_ref[...]) + dot(grad, gate_ref[...])).astype(bf16)
    own_ref[...] = rows_grad[:half]
    far_ref[...] = rows_grad[half:]
    out_part = (dot(hidden_in_ref[...], down_in_ref[...]) + dot(gated, down_ref[...])).astype(bf16)
    out_own_ref[...] = out_part[:half]
    out_far_ref[...] = out_part[half:]


def among_all(w, tile, first=0):
    return pl.BlockSpec((tile, w), lambda i, where: (first + i, 0))


def all_of(shape):
    return pl.BlockSpec(shape, lambda i, where: (0,) * len(shape), pipeline_mode=pl.Buffered(1))


def grads_out(wide, pad, width, count):
    direct = whole_tiles(wide, width // count)
    return (count, 3 * wide, width // count) if direct else (3 * pad, width), (24, width)


def to_owners(grad, wide, count):
    if len(grad.shape) == 3:
        return grad
    grad = grad.reshape(3, -1, grad.shape[1])[:, :wide]
    return grad.reshape(3 * wide, count, -1).transpose(1, 0, 2)


def token_grid(cots, rows, tile=512):
    return rows.shape[0] // tile, tile, [among_all(rows.shape[1], tile), among_all(cots.shape[1], tile)]


def first_units(groups, where, rows, cots, gate_rows, down_rows, units, experts, count):
    total, width = rows.shape
    pad = down_rows.shape[0]
    wide = units * len(groups)
    steps, tile, token_specs = token_grid(cots, rows)
    shapes = grads_out(wide, pad, width, count)
    hidden, grad, weights, router = pl.pallas_call(
        functools.partial(first_kernel, groups, units, experts),
        grid_spec=pltpu.PrefetchScalarGridSpec(
            num_scalar_prefetch=1,
            grid=(steps,),
            in_specs=token_specs + [all_of(gate_rows.shape), all_of(down_rows.shape)],
            out_specs=[among_all(pad, tile), among_all(2 * pad, tile), all_of(shapes[0]), all_of(shapes[1])],
            scratch_shapes=[pltpu.VMEM((2 * pad, width), f32), pltpu.VMEM((pad, width), f32)],
        ),
        out_shape=[
            jax.ShapeDtypeStruct((total, pad), bf16),
            jax.ShapeDtypeStruct((total, 2 * pad), bf16),
            jax.ShapeDtypeStruct(shapes[0], bf16),
            jax.ShapeDtypeStruct(shapes[1], f32),
        ],
        compiler_params=pltpu.CompilerParams(vmem_limit_bytes=60 * 1024 * 1024),
        cost_estimate=pl.CostEstimate(flops=12 * total * width * pad, bytes_accessed=4 * total * width, transcendentals=0),
    )(where, rows, cots, gate_rows, down_rows)
    return hidden, grad, to_owners(weights, wide, count), router


def weight_grads(where, rows, cots, hidden, grad, wide, count):
    total, width = rows.shape
    pad = hidden.shape[1]
    steps, tile, token_specs = token_grid(cots, rows)
    shapes = grads_out(wide, pad, width, count)
    weights, router = pl.pallas_call(
        functools.partial(grads_kernel, wide),
        grid_spec=pltpu.PrefetchScalarGridSpec(
            num_scalar_prefetch=1,
            grid=(steps,),
            in_specs=token_specs + [among_all(pad, tile), among_all(2 * pad, tile)],
            out_specs=[all_of(shapes[0]), all_of(shapes[1])],
            scratch_shapes=[pltpu.VMEM((2 * pad, width), f32), pltpu.VMEM((pad, width), f32)],
        ),
        out_shape=[jax.ShapeDtypeStruct(shapes[0], bf16), jax.ShapeDtypeStruct(shapes[1], f32)],
        compiler_params=pltpu.CompilerParams(vmem_limit_bytes=58 * 1024 * 1024),
        cost_estimate=pl.CostEstimate(flops=6 * total * width * pad, bytes_accessed=4 * total * width, transcendentals=0),
    )(where, rows, cots, hidden, grad)
    return to_owners(weights, wide, count), router


def second_units(groups, first, chunks, where, rows, cots, before, own, kept, units, experts):
    total, width = rows.shape
    steps, tile = chunks * 2, 512
    hidden_in, grad_in, gate_in, down_in = before
    gate_rows, down_rows = own
    pad = down_rows.shape[0]

    def half(w):
        return pl.BlockSpec((tile // 2, w), lambda i, where: (i, 0))

    def tokens_of(v):
        return among_all(v if isinstance(v, int) else v.shape[1], tile, first * 2)

    kept = list(kept)
    shapes = [(steps * tile // 2, width)] * 4 + [(total, pad), (total, 2 * pad)]
    return pl.pallas_call(
        functools.partial(second_kernel, groups, units, experts),
        grid_spec=pltpu.PrefetchScalarGridSpec(
            num_scalar_prefetch=1,
            grid=(steps,),
            in_specs=[tokens_of(rows), tokens_of(cots)]
            + [tokens_of(hidden_in), tokens_of(grad_in)]
            + [all_of(v.shape) for v in (gate_in, down_in, gate_rows, down_rows)]
            + [pl.BlockSpec(memory_space=pl.ANY)] * len(kept),
            out_specs=[half(width)] * 4 + [tokens_of(pad), tokens_of(2 * pad)],
        ),
        out_shape=[jax.ShapeDtypeStruct(shape, bf16) for shape in shapes],
        input_output_aliases={9 + i: 4 + i for i in range(len(kept))},
        compiler_params=pltpu.CompilerParams(vmem_limit_bytes=58 * 1024 * 1024),
        cost_estimate=pl.CostEstimate(flops=10 * steps * tile * width * pad, bytes_accessed=8 * steps * tile * width, transcendentals=0),
    )(where, rows, cots, hidden_in, grad_in, gate_in, down_in, gate_rows, down_rows, *kept)


def whole_tiles(units, rows):
    return units % 16 == 0 and rows % 128 == 0


def turn_kernel(columns_ref, out_ref):
    count, units, rows = out_ref.shape
    out_ref[...] = columns_ref[...].T.reshape(count, units, rows)


def turn_weights(columns, who, count, which=0):
    rows, width = columns.shape
    span = width // (3 * who)
    units = span // count
    if not whole_tiles(units, rows):
        columns = columns.reshape(rows, who, 3, count, units)[:, which]
        return columns.transpose(2, 1, 3, 0).reshape(count, -1, rows)
    return pl.pallas_call(
        turn_kernel,
        grid=(3,),
        in_specs=[pl.BlockSpec((rows, span), lambda k: (0, which * 3 + k))],
        out_specs=pl.BlockSpec((count, units, rows), lambda k: (0, k, 0)),
        out_shape=jax.ShapeDtypeStruct((count, 3 * units, rows), bf16),
        compiler_params=pltpu.CompilerParams(vmem_limit_bytes=32 * 1024 * 1024),
        cost_estimate=pl.CostEstimate(flops=0, bytes_accessed=4 * rows * 3 * span, transcendentals=0),
    )(columns)


def turn_back_kernel(first_ref, second_ref, shared_ref, routed_ref):
    count, units, rows = first_ref.shape

    def turned(block):
        return block.reshape(count * units, rows).T

    routed_ref[:, 0, :] = turned(first_ref[...]).astype(f32)
    routed_ref[:, 1, :] = turned(second_ref[:, :units]).astype(f32)
    shared_ref[...] = turned(second_ref[:, units:])


def turn_grads(first, second):
    count, units, rows = first.shape
    units = units // 3
    span = units * count
    if not whole_tiles(units, rows):
        second = second.reshape(count, 3, 2, units, rows)
        first = first.reshape(count, 3, units, rows)
        three = jnp.stack([first, second[:, :, 0], second[:, :, 1]]).transpose(0, 4, 2, 1, 3).reshape(3, rows, 3 * span)
        return three[2], jnp.moveaxis(three[:2], 0, 1).astype(f32)
    return pl.pallas_call(
        turn_back_kernel,
        grid=(3,),
        in_specs=[
            pl.BlockSpec((count, units, rows), lambda k: (0, k, 0)),
            pl.BlockSpec((count, 2 * units, rows), lambda k: (0, k, 0)),
        ],
        out_specs=[
            pl.BlockSpec((rows, span), lambda k: (0, k)),
            pl.BlockSpec((rows, 2, span), lambda k: (0, 0, k)),
        ],
        out_shape=[jax.ShapeDtypeStruct((rows, 3 * span), bf16), jax.ShapeDtypeStruct((rows, 2, 3 * span), f32)],
        compiler_params=pltpu.CompilerParams(vmem_limit_bytes=56 * 1024 * 1024),
        cost_estimate=pl.CostEstimate(flops=0, bytes_accessed=48 * rows * span, transcendentals=0),
    )(first, second)


def deal_kernel(share, dense_ref, attn_ref, shared_ref):
    width = share * 8
    for o in range(8):
        for k in range(4):
            at = k * width + o * share
            attn_ref[o, :, k * share : (k + 1) * share] = dense_ref[:, at : at + share]
    owners, _, columns = shared_ref.shape
    span = columns // 3
    for o in range(owners):
        for k in range(3):
            at = 4 * width + (k * owners + o) * span
            shared_ref[o, :, k * span : (k + 1) * span] = dense_ref[:, at : at + span]


def deal_columns(dense, share, owners):
    rows, columns = dense.shape
    shapes = [(8, rows, 4 * share), (owners, rows, (columns - 32 * share) // owners)]
    return pl.pallas_call(
        functools.partial(deal_kernel, share),
        out_shape=[jax.ShapeDtypeStruct(shape, bf16) for shape in shapes],
        compiler_params=pltpu.CompilerParams(vmem_limit_bytes=32 * 1024 * 1024),
        cost_estimate=pl.CostEstimate(flops=0, bytes_accessed=4 * rows * columns, transcendentals=0),
    )(dense)


def collect_kernel(share, attn_ref, shared_ref, dense_ref):
    width = share * 8
    for o in range(8):
        for k in range(4):
            at = k * width + o * share
            dense_ref[:, at : at + share] = attn_ref[o, :, k * share : (k + 1) * share].astype(f32)
    owners, _, columns = shared_ref.shape
    span = columns // 3
    for o in range(owners):
        for k in range(3):
            at = 4 * width + (k * owners + o) * span
            dense_ref[:, at : at + span] = shared_ref[o, :, k * span : (k + 1) * span].astype(f32)


def collect_columns(attn, shared, share):
    rows = attn.shape[1]
    columns = 32 * share + shared.shape[0] * shared.shape[2]
    return pl.pallas_call(
        functools.partial(collect_kernel, share),
        out_shape=jax.ShapeDtypeStruct((rows, columns), f32),
        compiler_params=pltpu.CompilerParams(vmem_limit_bytes=32 * 1024 * 1024),
        cost_estimate=pl.CostEstimate(flops=0, bytes_accessed=6 * rows * columns, transcendentals=0),
    )(attn, shared)


def place_kernel(units, *refs):
    parts, (router_ref, gate_ref, down_ref) = refs[:-3], refs[-3:]
    pad = down_ref.shape[0]
    wide = units * len(parts)
    blank = jnp.zeros((pad - wide, down_ref.shape[1]), bf16)
    for w, part in enumerate(parts):
        for k, (out_ref, at) in enumerate(((gate_ref, 0), (gate_ref, pad), (down_ref, 0))):
            out_ref[at + w * units : at + (w + 1) * units] = part[0, k * units : (k + 1) * units]
    gate_ref[wide:pad] = router_ref[...]
    gate_ref[pad + wide :] = blank
    down_ref[wide:] = blank


def place_weights(ffn, router):
    count, _, block = ffn.shape
    units = FF // count
    who = ffn.shape[1] // (3 * units)
    wide = units * who
    width = count * block
    pad = (wide + router.shape[0] + 127) // 128 * 128
    router = stack(router, jnp.zeros((pad - wide - router.shape[0], width), bf16))
    if not whole_tiles(units, block):
        gate, up, down = ffn.transpose(1, 0, 2).reshape(who, 3, units, width).transpose(1, 0, 2, 3).reshape(3, wide, width)
        blank = jnp.zeros((pad - wide, width), bf16)
        return stack(gate, router, up, blank), stack(down, blank)

    def column(r):
        return pl.BlockSpec((r, block), lambda i: (0, i))

    return pl.pallas_call(
        functools.partial(place_kernel, units),
        grid=(count,),
        in_specs=[pl.BlockSpec((1, 3 * units, block), lambda i, w=w: (i, w, 0)) for w in range(who)] + [column(pad - wide)],
        out_specs=[column(2 * pad), column(pad)],
        out_shape=[jax.ShapeDtypeStruct((r, width), bf16) for r in (2 * pad, pad)],
        compiler_params=pltpu.CompilerParams(vmem_limit_bytes=32 * 1024 * 1024),
        cost_estimate=pl.CostEstimate(flops=0, bytes_accessed=12 * wide * width, transcendentals=0),
    )(*[ffn] * who, router)


def attend_rows(queries, keys, allowed):
    scores = jnp.where(allowed, dot_nt(queries, keys) * HD ** (-0.5), -1e30)
    raw = jnp.exp(scores - jnp.max(scores, axis=1, keepdims=True))
    return raw / jnp.sum(raw, axis=1, keepdims=True)


def allowed_pairs(own_ref, all_ref):
    return (own_ref[:, :1] == all_ref[0, :1]) & (all_ref[0, 1:2] <= own_ref[:, 1:2])


def piece_at(where_ref, s, piece_ref):
    size = piece_ref.shape[0]
    return pl.ds(pl.multiple_of(where_ref[s] * size, size), size)


def attend_kernel(heads, where_ref, rows_ref, bias_ref, cosine_ref, sine_ref, own_ref, all_ref, *refs):
    pieces, (packed_ref, mixed_ref) = refs[:-2], refs[-2:]
    share = heads * HD
    packed = bias_ref[...]
    for s, piece in enumerate(pieces):
        packed = packed + dot(rows_ref[:, piece_at(where_ref, s, piece)], piece[:, : 3 * share])
    cosine, sine = cosine_ref[...], sine_ref[...]
    allowed = allowed_pairs(own_ref, all_ref)

    def turned(at):
        v = packed[:, at : at + HD]
        return (v * cosine + pltpu.roll(v, HD // 2, 1) * sine).astype(bf16)

    for h in range(heads):
        queries, keys = turned(h * HD), turned(share + h * HD)
        values = packed[:, 2 * share + h * HD : 2 * share + (h + 1) * HD].astype(bf16)
        attend = attend_rows(queries, keys, allowed)
        mixed_ref[:, h * HD : (h + 1) * HD] = dot(attend.astype(bf16), values).astype(bf16)
        for k, v in enumerate((queries, keys, values)):
            packed_ref[:, k * share + h * HD : k * share + (h + 1) * HD] = v


def project_kernel(where_ref, mixed_ref, *refs):
    pieces, (near_ref, far_ref) = refs[:-2], refs[-2:]
    half = near_ref.shape[0]
    for s, piece in enumerate(pieces):
        rows = dot_nt(mixed_ref[...], piece[:, piece.shape[1] * 3 // 4 :]).astype(bf16)
        columns = piece_at(where_ref, s, piece)
        near_ref[:, columns] = rows[:half]
        far_ref[:, columns] = rows[half:]


def attend_back_kernel(heads, where_ref, grad_ref, packed_ref, cosine_ref, sine_ref, own_ref, all_ref, *refs):
    pieces, (packed_grad_ref, near_ref, far_ref, bias_ref) = refs[:-4], refs[-4:]
    share = heads * HD
    scale = HD ** (-0.5)
    mixed_grad = 0.0
    for s, piece in enumerate(pieces):
        mixed_grad = mixed_grad + dot(grad_ref[:, piece_at(where_ref, s, piece)], piece[:, 3 * share :])
    mixed_grad = mixed_grad.astype(bf16)
    cosine, sine = cosine_ref[...], sine_ref[...]
    allowed = allowed_pairs(own_ref, all_ref)

    def back(v):
        v = v.astype(bf16).astype(f32)
        return (v * cosine - pltpu.roll(v, HD // 2, 1) * sine).astype(bf16)

    for h in range(heads):
        queries, keys, values = (
            packed_ref[:, k * share + h * HD : k * share + (h + 1) * HD] for k in range(3)
        )
        own_grad = mixed_grad[:, h * HD : (h + 1) * HD]
        attend = attend_rows(queries, keys, allowed)
        attend_grad = dot_nt(own_grad, values)
        scores_grad = attend * (attend_grad - jnp.sum(attend * attend_grad, axis=1, keepdims=True))
        scores_grad = scores_grad.astype(bf16)
        grads = (
            back(dot(scores_grad, keys) * scale),
            back(dot_tn(scores_grad, queries) * scale),
            dot_tn(attend.astype(bf16), own_grad).astype(bf16),
        )
        for k, v in enumerate(grads):
            packed_grad_ref[:, k * share + h * HD : k * share + (h + 1) * HD] = v
    packed_grad = packed_grad_ref[...]
    bias_ref[...] = jnp.broadcast_to(jnp.sum(packed_grad.astype(f32), axis=0, keepdims=True), bias_ref.shape)
    half = near_ref.shape[0]
    for s, piece in enumerate(pieces):
        rows_grad = dot_nt(packed_grad, piece[:, : 3 * share]).astype(bf16)
        columns = piece_at(where_ref, s, piece)
        near_ref[:, columns] = rows_grad[:half]
        far_ref[:, columns] = rows_grad[half:]


def group_call(kernel, group_len, where, operands, specs, pieces, out_widths, out_types, flops):
    def spec(kind, shape):
        if kind == "rows":
            return pl.BlockSpec((group_len, shape[1]), lambda i, where: (i, 0))
        if kind == "pair":
            return pl.BlockSpec((1,) + shape[1:], lambda i, where: (i, 0, 0))
        return pl.BlockSpec(shape, lambda i, where: (0, 0), pipeline_mode=pl.Buffered(1))

    operands = tuple(operands) + tuple(pieces)
    specs = tuple(specs) + ("all",) * len(pieces)
    return pl.pallas_call(
        kernel,
        grid_spec=pltpu.PrefetchScalarGridSpec(
            num_scalar_prefetch=1,
            grid=(2,),
            in_specs=[spec(k, v.shape) for k, v in zip(specs, operands)],
            out_specs=[pl.BlockSpec((r, w), lambda i, where: (i, 0)) for r, w in out_widths],
        ),
        out_shape=[jax.ShapeDtypeStruct((2 * r, w), t) for (r, w), t in zip(out_widths, out_types)],
        compiler_params=pltpu.CompilerParams(vmem_limit_bytes=48 * 1024 * 1024),
        cost_estimate=pl.CostEstimate(flops=flops, bytes_accessed=sum(2 * v.size for v in operands), transcendentals=0),
    )(where, *operands)


def body(lay, tokens, dense_weights, expert_weights, gain_attn, gain_ffn, qkv_bias, router_weight, routes, doc_ids, out_grad):
    row_count, model_width = tokens.shape
    rings = lay.rings
    ring = lax.axis_index("ring")
    pair = lax.axis_index("pair")
    ep = lax.axis_index("ep")
    local_experts = expert_weights.shape[1]
    expert_count = router_weight.shape[1] - 1
    owners = expert_count // local_experts
    dp_count = rings * 2
    ring_place = jnp.asarray(lay.place, jnp.int32)[ring]
    behind = [jnp.asarray(lay.order, jnp.int32)[(ring_place - s) % rings] for s in range(rings)]
    ring_order = jnp.stack(behind)
    own_expert = ep * local_experts
    where = own_expert[None].astype(jnp.int32)

    stream = tokens.astype(f32)
    gain_one = gain_attn.astype(f32)
    gain_two = gain_ffn.astype(f32)
    heads = H // 8
    share = heads * HD
    unit_share = SFF // owners
    units = FF // dp_count
    n = row_count

    bits = jnp.sum(jnp.left_shift(jnp.int32(1), routes), axis=1, keepdims=True).astype(bf16)
    cot_blocks = [jnp.concatenate([out_grad, jnp.broadcast_to(bits, (row_count, 128))], axis=1)]
    mine, shared = deal_columns(after(dense_weights, cot_blocks[0]), share, owners)
    plane_part = lax.all_to_all(mine, PLANE, split_axis=0, concat_axis=0, tiled=True)
    plane_part = plane_part.reshape(-1, 4 * share)
    cot_blocks.append(permute(cot_blocks[0], lay.onward))
    mine, cot_blocks[1] = together(mine, cot_blocks[1])
    for _ in range(rings - 3):
        cot_blocks.append(permute(cot_blocks[-1], lay.onward))

    inverse_one = lax.rsqrt(jnp.mean(stream * stream, axis=1, keepdims=True) + norm_eps)
    normed = (stream * inverse_one * gain_one).astype(bf16)
    doc_pair = jnp.stack([doc_ids, permute(doc_ids, lay.up)])
    group_len = doc_ids.shape[0]
    before = jnp.sum((doc_pair[:, None, :] < doc_pair[:, :, None]).astype(jnp.int32), axis=2)
    spot = jnp.arange(group_len, dtype=jnp.int32)
    near_blocks = jnp.stack([ep, ep ^ 2, ep ^ 1, ep ^ 3])

    def in_order(values):
        return values.reshape(2, 4, row_count)[:, near_blocks].reshape(2, group_len)

    places = in_order(spot[None, :] - before)
    docs = in_order(doc_pair)
    spots = in_order(jnp.stack([spot, spot]))
    cosine, sine = rope_tables(places.reshape(-1))
    sine = jnp.where(jnp.arange(HD) < HD // 2, -sine, sine)
    spots_all = jnp.stack([docs, spots], axis=1)
    spots_own = jnp.stack([docs.reshape(-1), spots.reshape(-1)], axis=1)
    routed = expert_weights.reshape(expert_weights.shape[0], -1)
    router = router_weight.T
    turn = (own_expert + jnp.arange(expert_count, dtype=jnp.int32)) % expert_count
    router = stack(jnp.take(router, turn, axis=0), router[expert_count:])
    slot = pair * 4 + ep
    bias_share = lax.dynamic_slice_in_dim(qkv_bias.astype(f32).reshape(3, 8, share), slot, 1, 1).reshape(1, 3 * share)
    plane_part, cot_blocks[-1], routed, normed = together(plane_part, cot_blocks[-1], routed, normed)

    qkv = [plane_part, permute(plane_part, lay.onward)]
    cot_blocks.append(permute(cot_blocks[-1], lay.onward))
    side, up = permute(normed, lay.side), permute(normed, lay.up)

    def between_cores(*pieces):
        return [permute(piece, lay.core) for piece in pieces]

    def over(pairs, pieces):
        return [permute(piece, pairs) for piece in pieces]

    cot_sides, cot_ups = over(lay.side, cot_blocks[:1]), over(lay.up, cot_blocks[:1])
    cot_cores = between_cores(*cot_blocks)
    first_ffn, second_ffn = (turn_weights(routed, local_experts, dp_count, w) for w in range(local_experts))
    qkv[-1], cot_blocks[-1], side, up, cot_sides, cot_ups, cosine, sine, first_ffn, second_ffn = lax.optimization_barrier(
        (qkv[-1], cot_blocks[-1], side, up, cot_sides, cot_ups, cosine, sine, first_ffn, second_ffn)
    )
    for s in range(2, rings):
        qkv.append(permute(qkv[-1], lay.onward))
        sides, ups = [], []
        if s == 2:
            cross = permute(up, lay.side)
            cores = between_cores(normed, side, up)
            sides, ups = over(lay.side, cot_blocks[1:2]), over(lay.up, cot_blocks[1:3])
            cross, cores = lax.optimization_barrier((cross, cores))
        elif s == 3:
            cores += between_cores(cross)
            normed_group = assemble((normed, side, *cores[:2], up, cross, *cores[2:]))
            sides, ups = over(lay.side, cot_blocks[2:]), over(lay.up, cot_blocks[3:])
        sides, ups, qkv[-1] = lax.optimization_barrier((sides, ups, qkv[-1]))
        cot_sides, cot_ups = cot_sides + sides, cot_ups + ups
    qkv[-1], normed_group = together(qkv[-1], normed_group)

    cot_crosses = [
        permute(cot_sides[s], lay.up) if s % 2 else permute(cot_ups[s], lay.side) for s in range(rings)
    ]
    heads_flops = 8 * heads * group_len * group_len * HD
    packed, mixed = group_call(
        functools.partial(attend_kernel, heads),
        group_len,
        ring_order,
        (normed_group, bias_share, cosine, sine, spots_own, spots_all),
        ("rows", "all", "rows", "rows", "rows", "pair"),
        qkv,
        [(group_len, 3 * share), (group_len, share)],
        [bf16, bf16],
        4 * group_len * model_width * 3 * share + heads_flops,
    )
    received = [lax.dynamic_index_in_dim(shared, ep ^ k, 0, keepdims=False) for k in range(4)]
    received[1:3] = [permute(v, pairs) for v, pairs in zip(received[1:3], (lay.core, lay.side))]
    branch_parts = group_call(
        project_kernel,
        group_len,
        ring_order,
        (mixed,),
        ("rows",),
        qkv,
        [(group_len // 2, model_width)] * 2,
        [bf16, bf16],
        4 * group_len * model_width * share,
    )
    *branch_parts, cot_crosses, first_ffn = lax.optimization_barrier((*branch_parts, cot_crosses, first_ffn))

    def to_units(ffn):
        return lax.all_to_all(ffn, ("ring", "pair"), split_axis=0, concat_axis=0, tiled=True)

    first_ffn = to_units(first_ffn)
    here = plus(branch_parts[0], permute(branch_parts[1], lay.core))
    cross, side = permute(here[3 * n :], lay.side), permute(here[n : 2 * n], lay.side)
    cots = []
    for s in range(rings):
        cores = [cot_cores[s]] + between_cores(cot_ups[s], cot_sides[s], cot_crosses[s])
        cots += [cot_blocks[s], cot_ups[s], *cores[:2], cot_sides[s], cot_crosses[s], *cores[2:]]
    cots = assemble(cots)
    cross, side, cots = together(cross, side, cots)
    received[3] = permute(after(received[3], cross), lay.side_core)
    up = permute(plus(here[2 * n : 3 * n], cross), lay.up)
    branch = here[:n].astype(f32) + side.astype(f32) + after(up, first_ffn, *received).astype(f32)
    residual = stream + branch
    inverse_two = lax.rsqrt(jnp.mean(residual * residual, axis=1, keepdims=True) + norm_eps)
    normed_two = (residual * inverse_two * gain_two).astype(bf16)

    blocks, ups, sides, crosses, inner = [normed_two], [], [], [], []

    for s in range(rings - 1):
        onward = permute(blocks[s], lay.onward)
        up, side = permute(blocks[s], lay.up), permute(blocks[s], lay.side)
        more, last = [], s == rings - 2
        if s >= 2:
            more.append(permute(ups[s - 2], lay.side))
            inner.append(between_cores(blocks[s - 2], ups[s - 2], sides[s - 2]))
        if last:
            more.append(permute(sides[s - 1], lay.up))
            inner.append(between_cores(blocks[s - 1], ups[s - 1], sides[s - 1]))
        if s == 1:
            shared_ffn = jnp.stack(received)[jnp.arange(4, dtype=jnp.int32) ^ ep].reshape(-1, 3 * unit_share)
            shared_ffn = turn_weights(shared_ffn, 1, dp_count)
            second_ffn = jnp.concatenate([second_ffn, shared_ffn], axis=1)
            second_ffn, onward = together(second_ffn, onward)
        onward, up, side, *more = together(onward, up, side, *more)
        blocks.append(onward)
        ups.append(up)
        sides.append(side)
        crosses += more
    up, side = permute(blocks[-1], lay.up), permute(blocks[-1], lay.side)
    inner.append(between_cores(blocks[-2], ups[-1], sides[-1]))
    up, side, crossing = together(up, side, ups[-1])
    ups.append(up)
    sides.append(side)
    second_ffn = to_units(after(second_ffn, up))
    inner.append(between_cores(blocks[-1], up, side))
    crossing, crossed_too = permute(crossing, lay.side), permute(up, lay.side)

    crosses += together(crossing, crossed_too)
    rows = []
    for s in range(rings):
        cores = inner[s] + between_cores(crosses[s])
        rows += [blocks[s], ups[s], *cores[:2], sides[s], crosses[s], *cores[2:]]
    rows = assemble(rows)

    first_rows = place_weights(first_ffn, router)
    late = rings // 2
    first_hidden, first_grad, first_weights_grad, first_router = first_units(
        (0,), where, rows, cots, *first_rows, units, expert_count, dp_count
    )
    first_weights_grad = to_units(first_weights_grad)
    second_rows = place_weights(after(second_ffn, first_hidden), router)

    chunk, half = 4 * n, 2 * n
    order = list(range(rings))[::-1]
    first_half, last_half = order[: rings - late], order[rings - late :]

    def cut_chunk(which, s, at):
        begin = (s % late if s < late else s - late) * chunk + at
        return which[begin : begin + half]

    def crossed(part, there, some):
        keep = {s: plus(cut_chunk(part, s, 0), cut_chunk(there, s, 0)) for s in some}
        send = {s: plus(cut_chunk(part, s, half), cut_chunk(there, s, half)) for s in some}
        return keep, send

    def all_there(*groups):
        flat, tree = jax.tree.flatten(groups)
        return jax.tree.unflatten(tree, lax.optimization_barrier(tuple(flat)))

    def ffn_half(first, chunks, kept):
        return second_units(
            (1, SHARED), first, chunks, where, rows, cots, (first_hidden, first_grad) + tuple(first_rows), second_rows, kept, units, expert_count
        )

    out_own_a, out_far_a, own_a, far_a, hidden, gate_up_grad = ffn_half(late, rings - late, ())

    keep, send = crossed(own_a, permute(far_a, lay.core), first_half)
    keep, send, hidden, gate_up_grad = all_there(keep, send, hidden, gate_up_grad)
    out_there_a = permute(after(out_far_a, hidden), lay.core)
    sided = {s: permute(send[s], lay.side) for s in first_half}
    out_own_b, out_far_b, own_b, far_b, hidden, gate_up_grad = ffn_half(0, late, (hidden, gate_up_grad))
    sided, own_b, far_b, hidden, gate_up_grad, first_weights_grad, out_there_a = all_there(
        sided, own_b, far_b, hidden, gate_up_grad, first_weights_grad, out_there_a
    )

    far_there = permute(far_b, lay.core)
    halves = {s: plus(keep[s], sided[s]) for s in first_half}
    upped = {order[0]: permute(halves[order[0]][n:], lay.up)}
    keep, send = crossed(own_b, far_there, last_half)
    keep, send, halves, hidden, upped = all_there(keep, send, halves, hidden, upped)
    own_sums = {order[0]: halves[order[0]][:n].astype(f32) + upped[order[0]].astype(f32)}
    total = own_sums[order[0]]
    queue = list(order[1:])

    def step_on(total):
        return permute(total.astype(bf16), lay.backward)

    def step_in(arrived):
        return own_sums[queue.pop(0)] + arrived.astype(f32)

    few = (len(last_half) + 1) // 2
    sided = {s: permute(send[s], lay.side) for s in last_half[:few]}
    upped = {s: permute(halves[s][n:], lay.up) for s in first_half[1:]}
    moving = step_on(total)
    ffn_grad, second_router = weight_grads(where, rows, cots, hidden, gate_up_grad, 2 * units, dp_count)
    out_there_b = permute(out_far_b, lay.core)
    sided, upped, moving, ffn_grad, out_there_b = all_there(sided, upped, moving, ffn_grad, out_there_b)
    own_sums.update({s: halves[s][:n].astype(f32) + upped[s].astype(f32) for s in first_half[1:]})
    total = step_in(moving)

    halves = {s: plus(keep[s], sided[s]) for s in last_half[:few]}
    sided = {s: permute(send[s], lay.side) for s in last_half[few:]}
    upped = {s: permute(halves[s][n:], lay.up) for s in last_half[:few]}
    moving = step_on(total)
    out_keep, out_send = crossed(out_own_a, out_there_a, first_half)
    sided, upped, moving, out_keep, out_send = all_there(sided, upped, moving, out_keep, out_send)
    own_sums.update({s: halves[s][:n].astype(f32) + upped[s].astype(f32) for s in last_half[:few]})
    total = step_in(moving)

    halves = {s: plus(keep[s], sided[s]) for s in last_half[few:]}
    upped = {s: permute(halves[s][n:], lay.up) for s in last_half[few:]}
    moving = step_on(total)
    more_keep, more_send = crossed(out_own_b, out_there_b, last_half)
    upped, moving, more_keep, more_send = all_there(upped, moving, more_keep, more_send)
    out_keep.update(more_keep)
    out_send.update(more_send)
    own_sums.update({s: halves[s][:n].astype(f32) + upped[s].astype(f32) for s in last_half[few:]})
    total = step_in(moving)
    while queue:
        total = step_in(step_on(total))
    normed_two_grad = total

    def router_rows(part, wide):
        start = wide - wide // 8 * 8
        return part[start : start + expert_count + 1]

    router_part = router_rows(first_router, units) + router_rows(second_router, 2 * units)
    turn_back = (jnp.arange(expert_count, dtype=jnp.int32) - own_expert) % expert_count
    router_part = stack(jnp.take(router_part[:expert_count], turn_back, axis=0), router_part[expert_count:])

    cotangent = out_grad.astype(f32)
    scaled_two = normed_two_grad * gain_two
    gain_two_grad = jnp.sum(normed_two_grad * residual * inverse_two, axis=0)
    residual_grad = (
        cotangent
        + inverse_two * scaled_two
        - residual * inverse_two**3 * jnp.mean(scaled_two * residual, axis=1, keepdims=True)
    )
    branch_grad = residual_grad.astype(bf16)

    side, up = permute(branch_grad, lay.side), permute(branch_grad, lay.up)
    core = permute(branch_grad, lay.core)
    side, up, core, ffn_grad = together(side, up, core, ffn_grad)
    ffn_grad = lax.all_to_all(ffn_grad, ("ring", "pair"), split_axis=0, concat_axis=0, tiled=True)
    cross = permute(up, lay.side)
    cores = [core, *between_cores(side, up)]
    cores.append(permute(cross, lay.core))
    branch_grad_group = assemble((branch_grad, side, *cores[:2], up, cross, *cores[2:]))
    keep, send = out_keep, out_send
    branch_grad_group = together(branch_grad_group)[0]

    quarter = [order[k :: 4] for k in range(4)] if rings > 4 else [[s] for s in order]
    sided = {s: permute(send[s], lay.side) for s in quarter[0]}
    packed_grad, near, far, bias_part = group_call(
        functools.partial(attend_back_kernel, heads),
        group_len,
        ring_order,
        (branch_grad_group, packed, cosine, sine, spots_own, spots_all),
        ("rows", "rows", "rows", "rows", "rows", "pair"),
        qkv,
        [(group_len, 3 * share), (group_len // 2, model_width), (group_len // 2, model_width), (8, 3 * share)],
        [bf16, bf16, bf16, f32],
        4 * group_len * model_width * 4 * share + 3 * heads_flops,
    )
    sided, packed_grad, near, far = all_there(sided, packed_grad, near, far)

    halves = {s: plus(keep[s], sided[s]) for s in quarter[0]}
    sided = {s: permute(send[s], lay.side) for s in quarter[1]}
    here = plus(near, permute(far, lay.core))
    attn_grads = jnp.concatenate([dot_over(normed_group, packed_grad), dot_over(branch_grad_group, mixed)], axis=1)
    attn_grads = attn_grads.astype(bf16).reshape(rings, -1, 4 * share)
    sided, attn_grads, here, halves = all_there(sided, attn_grads, here, halves)

    out_halves = {s: plus(keep[s], sided[s]) for s in quarter[1]}
    out_halves.update(halves)
    side, cross = permute(here[n : 2 * n], lay.side), permute(here[3 * n :], lay.side)
    def grads_at(s):
        return lax.dynamic_index_in_dim(attn_grads, behind[s], 0, keepdims=False).astype(f32)

    moving = permute(grads_at(order[0]).astype(bf16), lay.backward)
    side, cross, ffn_grad = together(side, cross, ffn_grad)

    up = permute(plus(here[2 * n : 3 * n], cross), lay.up)
    sided = {s: permute(send[s], lay.side) for s in quarter[2]}
    first_up = permute(out_halves[order[0]][n:], lay.up)
    sided, up, moving, first_up = all_there(sided, up, moving, first_up)
    output_sum = out_halves[order[0]][:n].astype(f32) + first_up.astype(f32)
    normed_grad = here[:n].astype(f32) + side.astype(f32) + up.astype(f32)
    scaled_one = normed_grad * gain_one
    gain_one_grad = jnp.sum(normed_grad * stream * inverse_one, axis=0)
    input_grad = (
        residual_grad
        + inverse_one * scaled_one
        - stream * inverse_one**3 * jnp.mean(scaled_one * stream, axis=1, keepdims=True)
    )
    bias_part = (bias_part[0] + bias_part[8]).reshape(3, 1, share)
    bias_part = lax.dynamic_update_slice(jnp.zeros((3, 8, share), f32), bias_part, (0, slot, 0))
    small = stack(router_part, gain_two_grad[None], gain_one_grad[None], bias_part.reshape(3, model_width))
    doubling = lay.doubling()

    total = grads_at(order[1]) + moving.astype(f32)
    out_halves.update({s: plus(keep[s], sided[s]) for s in quarter[2]})
    out_sums, out_queue = {}, list(order[1:])

    def outs_on(output_sum):
        return permute(output_sum.astype(bf16), lay.backward)

    def outs_over(some):
        return {s: permute(out_halves[s][n:], lay.up) for s in some}

    def outs_in(outs_up):
        out_sums.update({s: out_halves[s][:n].astype(f32) + outs_up[s].astype(f32) for s in outs_up})

    for i, s in enumerate(order[2:]):
        moving = permute(total.astype(bf16), lay.backward)
        if i == 0:
            outs_up = outs_over((quarter[0] + quarter[1])[1:])
            outgoing = outs_on(output_sum)
            sided = {s: permute(send[s], lay.side) for s in quarter[3]}
            for step in doubling[:2]:
                small = small + permute(small, step)
            shared_columns_grad, expert_grad = turn_grads(first_weights_grad, ffn_grad)
            moving, outs_up, sided, small, shared_columns_grad, expert_grad, outgoing = all_there(
                moving, outs_up, sided, small, shared_columns_grad, expert_grad, outgoing
            )
            outs_in(outs_up)
            output_sum = out_sums[out_queue.pop(0)] + outgoing.astype(f32)
            out_halves.update({s: plus(keep[s], sided[s]) for s in quarter[3]})
            outs_up = outs_over(quarter[2] + quarter[3])
            shared_columns_grad = lax.all_to_all(
                shared_columns_grad.reshape(owners, -1, 3 * unit_share),
                "ep",
                split_axis=0,
                concat_axis=0,
                tiled=True,
            )
        else:
            if i == 1:
                small = small + permute(small, doubling[2])
            if i == rings - 3:
                moving, small, shared_columns_grad = together(moving, small, shared_columns_grad)
            if i == 1:
                outs_in(outs_up)
            if i >= 1:
                output_sum = out_sums[out_queue.pop(0)] + outs_on(output_sum).astype(f32)
        total = grads_at(s) + moving.astype(f32)
    total = total.astype(bf16).reshape(8, -1, 4 * share)
    total = lax.all_to_all(total, PLANE, split_axis=0, concat_axis=0, tiled=True)
    for step in doubling[3:]:
        small = small + permute(small, step)
    while out_queue:
        output_sum = out_sums[out_queue.pop(0)] + outs_on(output_sum).astype(f32)
    output = (residual + output_sum).astype(bf16)
    dense_grad = collect_columns(total, shared_columns_grad, share)

    router_sum, gain_two_sum, gain_one_sum, bias_sum = jnp.split(small, [expert_count + 1, expert_count + 2, expert_count + 3])
    return (
        output,
        input_grad,
        dense_grad,
        expert_grad,
        gain_one_sum[0],
        gain_two_sum[0],
        bias_sum.reshape(-1),
        router_sum.T,
    )


def solution(mesh):
    devices = mesh.devices
    lay = Layout(devices.shape[0] // 2)
    inner = Mesh(devices.reshape(lay.rings, 2, devices.shape[1]), AXES)
    rows = P(AXES, None)
    experts = P(("ring", "pair"), "ep", None)
    in_specs = (rows, rows, experts, P(), P(), P(), P(), rows, P(("ring", "pair")), rows)
    out_specs = (rows, rows, rows, experts, P(), P(), P(), P())

    def run(*arguments):
        return body(lay, *arguments)

    return jax.shard_map(run, mesh=inner, in_specs=in_specs, out_specs=out_specs, check_vma=False)
```

```python
import functools

import jax
import jax.numpy as jnp
from jax import lax
from jax.experimental import pallas as pl
from jax.experimental.pallas import tpu as pltpu
from jax.sharding import Mesh, PartitionSpec as P

H = 16
HD = 128
FF = 1408
SFF = 5632

norm_eps = 1e-06
rope_base = 1000000.0
AXES = ("ring", "pair", "ep")
PLANE = ("pair", "ep")
SHARED = -1
f32 = jnp.float32
bf16 = jnp.bfloat16


class Layout:
    def __init__(self, rings):
        self.rings = rings
        self.order = list(range(0, rings, 2)) + list(range(1, rings, 2))[::-1]
        place = {r: i for i, r in enumerate(self.order)}
        self.place = [place[r] for r in range(rings)]
        self.core = self.pairs(lambda r, y, x, c: (r, y, x, 1 - c))
        self.side = self.pairs(lambda r, y, x, c: (r, y, 1 - x, c))
        self.side_core = self.pairs(lambda r, y, x, c: (r, y, 1 - x, 1 - c))
        self.up = self.pairs(lambda r, y, x, c: (r, 1 - y, x, c))
        self.cross = self.pairs(lambda r, y, x, c: (r, 1 - y, 1 - x, c))
        self.onward = self.pairs(lambda r, y, x, c: (self.order[(place[r] + 1) % rings], y, x, c))
        self.backward = self.pairs(lambda r, y, x, c: (self.order[(place[r] - 1) % rings], y, x, c))

    def pairs(self, move):
        found = []
        for r in range(self.rings):
            for y in range(2):
                for x in range(2):
                    for c in range(2):
                        u, v, w, q = move(r, y, x, c)
                        found.append((((r * 2 + y) * 2 + x) * 2 + c, ((u * 2 + v) * 2 + w) * 2 + q))
        return found

    def doubling(self):
        steps = []
        bit = 1
        while bit < self.rings * 8:
            steps.append([(i, i ^ bit) for i in range(self.rings * 8)])
            bit *= 2
        return steps


def permute(rows, pairs):
    return lax.ppermute(rows, AXES, pairs)


def stack(*parts):
    return jnp.concatenate(parts, axis=0)


def plus(a, b):
    return (a.astype(f32) + b.astype(f32)).astype(bf16)


def assemble_kernel(*refs):
    parts, out_ref, sems = refs[:-2], refs[-2], refs[-1]
    copies, at = [], 0
    for i, part in enumerate(parts):
        size = part.shape[0]
        copies.append(pltpu.make_async_copy(part, out_ref.at[pl.ds(at, size)], sems.at[i]))
        copies[-1].start()
        at += size
    for copy in copies:
        copy.wait()


def assemble(parts):
    rows = sum(part.shape[0] for part in parts)
    width = parts[0].shape[1]
    if rows * width > 1 << 24:
        return stack(*parts)
    return pl.pallas_call(
        assemble_kernel,
        in_specs=[pl.BlockSpec(memory_space=pltpu.VMEM)] * len(parts),
        out_specs=pl.BlockSpec(memory_space=pl.ANY),
        out_shape=jax.ShapeDtypeStruct((rows, width), bf16),
        scratch_shapes=[pltpu.SemaphoreType.DMA((len(parts),))],
        compiler_params=pltpu.CompilerParams(vmem_limit_bytes=48 * 1024 * 1024),
        cost_estimate=pl.CostEstimate(flops=0, bytes_accessed=4 * rows * width, transcendentals=0),
    )(*parts)


def rope_tables(places):
    steps_along = jnp.arange(HD // 2, dtype=f32) * (2.0 / HD)
    inverse = jnp.power(jnp.float32(rope_base), -steps_along)
    angles = places.astype(f32)[..., None] * inverse
    angles = jnp.concatenate([angles, angles], axis=-1)
    return jnp.cos(angles), jnp.sin(angles)


def dot(a, b):
    return jnp.dot(a, b, preferred_element_type=f32)


def dot_over(a, b):
    return jnp.einsum("tc,tf->cf", a, b, preferred_element_type=f32)


def after(value, *others):
    return lax.optimization_barrier((value,) + others)[0]


def together(*values):
    return lax.optimization_barrier(values)


def dot_nt(a, b):
    return lax.dot_general(a, b, (((1,), (1,)), ((), ())), preferred_element_type=f32)


def dot_tn(a, b):
    return lax.dot_general(a, b, (((0,), (0,)), ((), ())), preferred_element_type=f32)


def units_pass(gate_up, hidden_grad, gates):
    pad = hidden_grad.shape[1]
    g, u = gate_up[:, :pad], gate_up[:, pad:]
    sig = jax.nn.sigmoid(g)
    silu = g * sig
    hidden = (silu * u).astype(bf16).astype(f32)
    gated_grad = hidden_grad * gates
    up_grad = gated_grad * silu
    gate_grad = gated_grad * u * (sig + silu * (1.0 - sig))
    return (gates * hidden).astype(bf16), gate_grad, up_grad, hidden_grad * hidden


def with_logits(gate_grad, logit_grad, up_grad, base, at):
    lane = lax.broadcasted_iota(jnp.int32, logit_grad.shape, 1)
    parts = [gate_grad[:, :base]] if base else []
    parts.append(jnp.where(lane < at, gate_grad[:, base : base + 128], logit_grad))
    if base + 128 < gate_grad.shape[1]:
        parts.append(gate_grad[:, base + 128 :])
    return jnp.concatenate(parts + [up_grad], axis=1).astype(bf16)


def hand_out(wide, gate_sums, down_sums, out_ref, router_ref):
    pad = down_sums.shape[0]
    first = wide // 8 * 8
    router_ref[...] = gate_sums[first : first + router_ref.shape[0]]
    if len(out_ref.shape) == 2:
        out_ref[: 2 * pad] = gate_sums[...].astype(bf16)
        out_ref[2 * pad :] = down_sums[...].astype(bf16)
        return
    count, _, block = out_ref.shape
    for d in range(count):
        lanes = slice(d * block, (d + 1) * block)
        out_ref[d, :wide] = gate_sums[:wide, lanes].astype(bf16)
        out_ref[d, wide : 2 * wide] = gate_sums[pad : pad + wide, lanes].astype(bf16)
        out_ref[d, 2 * wide :] = down_sums[:wide, lanes].astype(bf16)


def add_grads(grad, rows, hidden, cots, gate_sums, down_sums):
    @pl.when(pl.program_id(0) == 0)
    def _():
        gate_sums[...] = jnp.zeros_like(gate_sums)
        down_sums[...] = jnp.zeros_like(down_sums)

    gate_sums[...] += dot_tn(grad, rows)
    down_sums[...] += dot_tn(hidden, cots)


def group_pass(groups, units, experts, where_ref, rows_ref, cots_ref, gate_ref, down_ref):
    n, width = rows_ref.shape
    pad = down_ref.shape[0]
    wide = units * len(groups)
    base = wide // 128 * 128
    at = wide - base
    gate_up = dot_nt(rows_ref[...], gate_ref[...])
    hidden_grad = dot_nt(cots_ref[:, :width], down_ref[...])
    logits = gate_up[:, base : base + 128]
    place = lax.broadcasted_iota(jnp.int32, (n, 128), 1) - at
    routed = (place >= 0) & (place < experts)
    bits = cots_ref[:, width : width + 128].astype(f32).astype(jnp.int32)
    turn = jnp.where(routed, lax.rem(where_ref[0] + place, experts), 0)
    chosen = (jnp.right_shift(bits, turn) & 1).astype(f32)
    peak = jnp.max(jnp.where(routed, logits, -jnp.inf), axis=1, keepdims=True)
    weights = jnp.where(routed, jnp.exp(logits - peak), 0.0)
    probs = weights / jnp.sum(weights, axis=1, keepdims=True)
    shared = jax.nn.sigmoid(logits)
    spot = lax.broadcasted_iota(jnp.int32, (128, pad), 1)
    lane = lax.broadcasted_iota(jnp.int32, (128, pad), 0) - at
    spread = jnp.zeros((128, pad), f32)
    for i, group in enumerate(groups):
        own = (spot >= i * units) & (spot < (i + 1) * units) & (lane == (experts if group == SHARED else group))
        spread = jnp.where(own, 1.0, spread)
    spread = spread.astype(bf16)
    gates = dot(jnp.where(place == experts, shared, probs * chosen).astype(bf16), spread)
    gated, gate_grad, up_grad, products = units_pass(gate_up, hidden_grad, gates)
    sums = dot_nt(products.astype(bf16), spread)
    own = sums * chosen
    mean = jnp.sum(jnp.where(routed, probs * own, 0.0), axis=1, keepdims=True)
    logit_grad = jnp.where(routed, probs * (own - mean), jnp.where(place == experts, sums * shared * (1.0 - shared), 0.0))
    return gated, with_logits(gate_grad, logit_grad, up_grad, base, at)


def first_kernel(groups, units, experts, count, where_ref, *refs):
    pieces, refs = refs[:count], refs[count:]
    cots_ref, gate_ref, down_ref, rows_ref, hidden_ref, grad_ref, out_ref, router_ref, gate_sums, down_sums, held, sems = refs
    step, steps = pl.program_id(0), pl.num_programs(0)
    each, size = held.shape[1] // pieces[0].shape[0], pieces[0].shape[0]

    def copy(piece, slot, t):
        return pltpu.make_async_copy(piece, held.at[slot, pl.ds(t * size, size)], sems.at[slot, t])

    for j in range(count // each):

        @pl.when(step == max(j - 1, 0))
        def _(j=j):
            for t in range(each):
                copy(pieces[j * each + t], j % 2, t).start()

    slot = lax.rem(step, 2)
    for t in range(each):
        copy(pieces[t], slot, t).wait()
    rows_ref[...] = held[slot]
    gated, grad = group_pass(groups, units, experts, where_ref, rows_ref, cots_ref, gate_ref, down_ref)
    hidden_ref[...] = gated
    grad_ref[...] = grad
    add_grads(grad, rows_ref[...], gated, cots_ref[:, : rows_ref.shape[1]], gate_sums, down_sums)

    @pl.when(step == steps - 1)
    def _():
        hand_out(units * len(groups), gate_sums, down_sums, out_ref, router_ref)


def grads_kernel(wide, where_ref, rows_ref, cots_ref, hidden_ref, grad_ref, out_ref, router_ref, gate_sums, down_sums):
    cots = cots_ref[:, : rows_ref.shape[1]]
    add_grads(grad_ref[...], rows_ref[...], hidden_ref[...], cots, gate_sums, down_sums)

    @pl.when(pl.program_id(0) == pl.num_programs(0) - 1)
    def _():
        hand_out(wide, gate_sums, down_sums, out_ref, router_ref)


def second_kernel(
    groups, units, experts, where_ref, rows_ref, cots_ref, hidden_in_ref, grad_in_ref, gate_in_ref, down_in_ref, gate_ref, down_ref, *refs
):
    out_own_ref, out_far_ref, own_ref, far_ref, hidden_ref, grad_ref = refs[-6:]
    half = own_ref.shape[0]
    gated, grad = group_pass(groups, units, experts, where_ref, rows_ref, cots_ref, gate_ref, down_ref)
    hidden_ref[...] = gated
    grad_ref[...] = grad
    rows_grad = (dot(grad_in_ref[...], gate_in_ref[...]) + dot(grad, gate_ref[...])).astype(bf16)
    own_ref[...] = rows_grad[:half]
    far_ref[...] = rows_grad[half:]
    out_part = (dot(hidden_in_ref[...], down_in_ref[...]) + dot(gated, down_ref[...])).astype(bf16)
    out_own_ref[...] = out_part[:half]
    out_far_ref[...] = out_part[half:]


def among_all(w, tile, first=0):
    return pl.BlockSpec((tile, w), lambda i, where: (first + i, 0))


def all_of(shape):
    return pl.BlockSpec(shape, lambda i, where: (0,) * len(shape), pipeline_mode=pl.Buffered(1))


def grads_out(wide, pad, width, count):
    direct = whole_tiles(wide, width // count)
    return (count, 3 * wide, width // count) if direct else (3 * pad, width), (24, width)


def to_owners(grad, wide, count):
    if len(grad.shape) == 3:
        return grad
    grad = grad.reshape(3, -1, grad.shape[1])[:, :wide]
    return grad.reshape(3 * wide, count, -1).transpose(1, 0, 2)


def token_grid(cots, rows, tile=512):
    return rows.shape[0] // tile, tile, [among_all(rows.shape[1], tile), among_all(cots.shape[1], tile)]


def first_units(groups, where, pieces, cots, gate_rows, down_rows, units, experts, count):
    total, width = cots.shape[0], gate_rows.shape[1]
    pad = down_rows.shape[0]
    wide = units * len(groups)
    tile = 512
    shapes = grads_out(wide, pad, width, count)
    rows, hidden, grad, weights, router = pl.pallas_call(
        functools.partial(first_kernel, groups, units, experts, len(pieces)),
        grid_spec=pltpu.PrefetchScalarGridSpec(
            num_scalar_prefetch=1,
            grid=(total // tile,),
            in_specs=[pl.BlockSpec(memory_space=pl.ANY)] * len(pieces)
            + [among_all(cots.shape[1], tile), all_of(gate_rows.shape), all_of(down_rows.shape)],
            out_specs=[among_all(width, tile), among_all(pad, tile), among_all(2 * pad, tile)]
            + [all_of(shape) for shape in shapes],
            scratch_shapes=[
                pltpu.VMEM((2 * pad, width), f32),
                pltpu.VMEM((pad, width), f32),
                pltpu.VMEM((2, tile, width), bf16),
                pltpu.SemaphoreType.DMA((2, tile // pieces[0].shape[0])),
            ],
        ),
        out_shape=[
            jax.ShapeDtypeStruct((total, width), bf16),
            jax.ShapeDtypeStruct((total, pad), bf16),
            jax.ShapeDtypeStruct((total, 2 * pad), bf16),
            jax.ShapeDtypeStruct(shapes[0], bf16),
            jax.ShapeDtypeStruct(shapes[1], f32),
        ],
        compiler_params=pltpu.CompilerParams(vmem_limit_bytes=60 * 1024 * 1024),
        cost_estimate=pl.CostEstimate(flops=12 * total * width * pad, bytes_accessed=4 * total * width, transcendentals=0),
    )(where, *pieces, cots, gate_rows, down_rows)
    return rows, hidden, grad, to_owners(weights, wide, count), router


def weight_grads(where, rows, cots, hidden, grad, wide, count):
    total, width = rows.shape
    pad = hidden.shape[1]
    steps, tile, token_specs = token_grid(cots, rows)
    shapes = grads_out(wide, pad, width, count)
    weights, router = pl.pallas_call(
        functools.partial(grads_kernel, wide),
        grid_spec=pltpu.PrefetchScalarGridSpec(
            num_scalar_prefetch=1,
            grid=(steps,),
            in_specs=token_specs + [among_all(pad, tile), among_all(2 * pad, tile)],
            out_specs=[all_of(shapes[0]), all_of(shapes[1])],
            scratch_shapes=[pltpu.VMEM((2 * pad, width), f32), pltpu.VMEM((pad, width), f32)],
        ),
        out_shape=[jax.ShapeDtypeStruct(shapes[0], bf16), jax.ShapeDtypeStruct(shapes[1], f32)],
        compiler_params=pltpu.CompilerParams(vmem_limit_bytes=58 * 1024 * 1024),
        cost_estimate=pl.CostEstimate(flops=6 * total * width * pad, bytes_accessed=4 * total * width, transcendentals=0),
    )(where, rows, cots, hidden, grad)
    return to_owners(weights, wide, count), router


def second_units(groups, first, chunks, where, rows, cots, before, own, kept, units, experts):
    total, width = rows.shape
    steps, tile = chunks * 2, 512
    hidden_in, grad_in, gate_in, down_in = before
    gate_rows, down_rows = own
    pad = down_rows.shape[0]

    def half(w):
        return pl.BlockSpec((tile // 2, w), lambda i, where: (i, 0))

    def tokens_of(v):
        return among_all(v if isinstance(v, int) else v.shape[1], tile, first * 2)

    kept = list(kept)
    shapes = [(steps * tile // 2, width)] * 4 + [(total, pad), (total, 2 * pad)]
    return pl.pallas_call(
        functools.partial(second_kernel, groups, units, experts),
        grid_spec=pltpu.PrefetchScalarGridSpec(
            num_scalar_prefetch=1,
            grid=(steps,),
            in_specs=[tokens_of(rows), tokens_of(cots)]
            + [tokens_of(hidden_in), tokens_of(grad_in)]
            + [all_of(v.shape) for v in (gate_in, down_in, gate_rows, down_rows)]
            + [pl.BlockSpec(memory_space=pl.ANY)] * len(kept),
            out_specs=[half(width)] * 4 + [tokens_of(pad), tokens_of(2 * pad)],
        ),
        out_shape=[jax.ShapeDtypeStruct(shape, bf16) for shape in shapes],
        input_output_aliases={9 + i: 4 + i for i in range(len(kept))},
        compiler_params=pltpu.CompilerParams(vmem_limit_bytes=58 * 1024 * 1024),
        cost_estimate=pl.CostEstimate(flops=10 * steps * tile * width * pad, bytes_accessed=8 * steps * tile * width, transcendentals=0),
    )(where, rows, cots, hidden_in, grad_in, gate_in, down_in, gate_rows, down_rows, *kept)


def whole_tiles(units, rows):
    return units % 16 == 0 and rows % 128 == 0


def turn_kernel(columns_ref, out_ref):
    count, units, rows = out_ref.shape
    out_ref[...] = columns_ref[...].T.reshape(count, units, rows)


def turn_weights(columns, who, count, which=0):
    rows, width = columns.shape
    span = width // (3 * who)
    units = span // count
    if not whole_tiles(units, rows):
        columns = columns.reshape(rows, who, 3, count, units)[:, which]
        return columns.transpose(2, 1, 3, 0).reshape(count, -1, rows)
    return pl.pallas_call(
        turn_kernel,
        grid=(3,),
        in_specs=[pl.BlockSpec((rows, span), lambda k: (0, which * 3 + k))],
        out_specs=pl.BlockSpec((count, units, rows), lambda k: (0, k, 0)),
        out_shape=jax.ShapeDtypeStruct((count, 3 * units, rows), bf16),
        compiler_params=pltpu.CompilerParams(vmem_limit_bytes=32 * 1024 * 1024),
        cost_estimate=pl.CostEstimate(flops=0, bytes_accessed=4 * rows * 3 * span, transcendentals=0),
    )(columns)


def turn_back_kernel(first_ref, second_ref, shared_ref, routed_ref):
    count, units, rows = first_ref.shape

    def turned(block):
        return block.reshape(count * units, rows).T

    routed_ref[:, 0, :] = turned(first_ref[...]).astype(f32)
    routed_ref[:, 1, :] = turned(second_ref[:, :units]).astype(f32)
    shared_ref[...] = turned(second_ref[:, units:])


def turn_grads(first, second):
    count, units, rows = first.shape
    units = units // 3
    span = units * count
    if not whole_tiles(units, rows):
        second = second.reshape(count, 3, 2, units, rows)
        first = first.reshape(count, 3, units, rows)
        three = jnp.stack([first, second[:, :, 0], second[:, :, 1]]).transpose(0, 4, 2, 1, 3).reshape(3, rows, 3 * span)
        return three[2], jnp.moveaxis(three[:2], 0, 1).astype(f32)
    return pl.pallas_call(
        turn_back_kernel,
        grid=(3,),
        in_specs=[
            pl.BlockSpec((count, units, rows), lambda k: (0, k, 0)),
            pl.BlockSpec((count, 2 * units, rows), lambda k: (0, k, 0)),
        ],
        out_specs=[
            pl.BlockSpec((rows, span), lambda k: (0, k)),
            pl.BlockSpec((rows, 2, span), lambda k: (0, 0, k)),
        ],
        out_shape=[jax.ShapeDtypeStruct((rows, 3 * span), bf16), jax.ShapeDtypeStruct((rows, 2, 3 * span), f32)],
        compiler_params=pltpu.CompilerParams(vmem_limit_bytes=56 * 1024 * 1024),
        cost_estimate=pl.CostEstimate(flops=0, bytes_accessed=48 * rows * span, transcendentals=0),
    )(first, second)


def deal_kernel(share, dense_ref, attn_ref, shared_ref):
    width = share * 8
    for o in range(8):
        for k in range(4):
            at = k * width + o * share
            attn_ref[o, :, k * share : (k + 1) * share] = dense_ref[:, at : at + share]
    owners, _, columns = shared_ref.shape
    span = columns // 3
    for o in range(owners):
        for k in range(3):
            at = 4 * width + (k * owners + o) * span
            shared_ref[o, :, k * span : (k + 1) * span] = dense_ref[:, at : at + span]


def deal_columns(dense, share, owners):
    rows, columns = dense.shape
    shapes = [(8, rows, 4 * share), (owners, rows, (columns - 32 * share) // owners)]
    return pl.pallas_call(
        functools.partial(deal_kernel, share),
        out_shape=[jax.ShapeDtypeStruct(shape, bf16) for shape in shapes],
        compiler_params=pltpu.CompilerParams(vmem_limit_bytes=32 * 1024 * 1024),
        cost_estimate=pl.CostEstimate(flops=0, bytes_accessed=4 * rows * columns, transcendentals=0),
    )(dense)


def collect_kernel(share, attn_ref, shared_ref, dense_ref):
    width = share * 8
    for o in range(8):
        for k in range(4):
            at = k * width + o * share
            dense_ref[:, at : at + share] = attn_ref[o, :, k * share : (k + 1) * share].astype(f32)
    owners, _, columns = shared_ref.shape
    span = columns // 3
    for o in range(owners):
        for k in range(3):
            at = 4 * width + (k * owners + o) * span
            dense_ref[:, at : at + span] = shared_ref[o, :, k * span : (k + 1) * span].astype(f32)


def collect_columns(attn, shared, share):
    rows = attn.shape[1]
    columns = 32 * share + shared.shape[0] * shared.shape[2]
    return pl.pallas_call(
        functools.partial(collect_kernel, share),
        out_shape=jax.ShapeDtypeStruct((rows, columns), f32),
        compiler_params=pltpu.CompilerParams(vmem_limit_bytes=32 * 1024 * 1024),
        cost_estimate=pl.CostEstimate(flops=0, bytes_accessed=6 * rows * columns, transcendentals=0),
    )(attn, shared)


def place_kernel(units, *refs):
    parts, (router_ref, gate_ref, down_ref) = refs[:-3], refs[-3:]
    pad = down_ref.shape[0]
    wide = units * len(parts)
    blank = jnp.zeros((pad - wide, down_ref.shape[1]), bf16)
    for w, part in enumerate(parts):
        for k, (out_ref, at) in enumerate(((gate_ref, 0), (gate_ref, pad), (down_ref, 0))):
            out_ref[at + w * units : at + (w + 1) * units] = part[0, k * units : (k + 1) * units]
    gate_ref[wide:pad] = router_ref[...]
    gate_ref[pad + wide :] = blank
    down_ref[wide:] = blank


def place_weights(ffn, router):
    count, _, block = ffn.shape
    units = FF // count
    who = ffn.shape[1] // (3 * units)
    wide = units * who
    width = count * block
    pad = (wide + router.shape[0] + 127) // 128 * 128
    router = stack(router, jnp.zeros((pad - wide - router.shape[0], width), bf16))
    if not whole_tiles(units, block):
        gate, up, down = ffn.transpose(1, 0, 2).reshape(who, 3, units, width).transpose(1, 0, 2, 3).reshape(3, wide, width)
        blank = jnp.zeros((pad - wide, width), bf16)
        return stack(gate, router, up, blank), stack(down, blank)

    def column(r):
        return pl.BlockSpec((r, block), lambda i: (0, i))

    return pl.pallas_call(
        functools.partial(place_kernel, units),
        grid=(count,),
        in_specs=[pl.BlockSpec((1, 3 * units, block), lambda i, w=w: (i, w, 0)) for w in range(who)] + [column(pad - wide)],
        out_specs=[column(2 * pad), column(pad)],
        out_shape=[jax.ShapeDtypeStruct((r, width), bf16) for r in (2 * pad, pad)],
        compiler_params=pltpu.CompilerParams(vmem_limit_bytes=32 * 1024 * 1024),
        cost_estimate=pl.CostEstimate(flops=0, bytes_accessed=12 * wide * width, transcendentals=0),
    )(*[ffn] * who, router)


def attend_rows(queries, keys, allowed):
    scores = jnp.where(allowed, dot_nt(queries, keys) * HD ** (-0.5), -1e30)
    raw = jnp.exp(scores - jnp.max(scores, axis=1, keepdims=True))
    return raw / jnp.sum(raw, axis=1, keepdims=True)


def allowed_pairs(own_ref, all_ref):
    return (own_ref[:, :1] == all_ref[0, :1]) & (all_ref[0, 1:2] <= own_ref[:, 1:2])


def piece_at(where_ref, s, piece_ref):
    size = piece_ref.shape[0]
    return pl.ds(pl.multiple_of(where_ref[s] * size, size), size)


def attend_kernel(heads, where_ref, rows_ref, bias_ref, cosine_ref, sine_ref, own_ref, all_ref, *refs):
    pieces, (packed_ref, mixed_ref) = refs[:-2], refs[-2:]
    share = heads * HD
    packed = bias_ref[...]
    for s, piece in enumerate(pieces):
        packed = packed + dot(rows_ref[:, piece_at(where_ref, s, piece)], piece[:, : 3 * share])
    cosine, sine = cosine_ref[...], sine_ref[...]
    allowed = allowed_pairs(own_ref, all_ref)

    def turned(at):
        v = packed[:, at : at + HD]
        return (v * cosine + pltpu.roll(v, HD // 2, 1) * sine).astype(bf16)

    for h in range(heads):
        queries, keys = turned(h * HD), turned(share + h * HD)
        values = packed[:, 2 * share + h * HD : 2 * share + (h + 1) * HD].astype(bf16)
        attend = attend_rows(queries, keys, allowed)
        mixed_ref[:, h * HD : (h + 1) * HD] = dot(attend.astype(bf16), values).astype(bf16)
        for k, v in enumerate((queries, keys, values)):
            packed_ref[:, k * share + h * HD : k * share + (h + 1) * HD] = v


def project_kernel(where_ref, mixed_ref, *refs):
    pieces, (near_ref, far_ref) = refs[:-2], refs[-2:]
    half = near_ref.shape[0]
    for s, piece in enumerate(pieces):
        rows = dot_nt(mixed_ref[...], piece[:, piece.shape[1] * 3 // 4 :]).astype(bf16)
        columns = piece_at(where_ref, s, piece)
        near_ref[:, columns] = rows[:half]
        far_ref[:, columns] = rows[half:]


def attend_back_kernel(heads, where_ref, grad_ref, packed_ref, cosine_ref, sine_ref, own_ref, all_ref, *refs):
    pieces, (packed_grad_ref, near_ref, far_ref, bias_ref) = refs[:-4], refs[-4:]
    share = heads * HD
    scale = HD ** (-0.5)
    mixed_grad = 0.0
    for s, piece in enumerate(pieces):
        mixed_grad = mixed_grad + dot(grad_ref[:, piece_at(where_ref, s, piece)], piece[:, 3 * share :])
    mixed_grad = mixed_grad.astype(bf16)
    cosine, sine = cosine_ref[...], sine_ref[...]
    allowed = allowed_pairs(own_ref, all_ref)

    def back(v):
        v = v.astype(bf16).astype(f32)
        return (v * cosine - pltpu.roll(v, HD // 2, 1) * sine).astype(bf16)

    for h in range(heads):
        queries, keys, values = (
            packed_ref[:, k * share + h * HD : k * share + (h + 1) * HD] for k in range(3)
        )
        own_grad = mixed_grad[:, h * HD : (h + 1) * HD]
        attend = attend_rows(queries, keys, allowed)
        attend_grad = dot_nt(own_grad, values)
        scores_grad = attend * (attend_grad - jnp.sum(attend * attend_grad, axis=1, keepdims=True))
        scores_grad = scores_grad.astype(bf16)
        grads = (
            back(dot(scores_grad, keys) * scale),
            back(dot_tn(scores_grad, queries) * scale),
            dot_tn(attend.astype(bf16), own_grad).astype(bf16),
        )
        for k, v in enumerate(grads):
            packed_grad_ref[:, k * share + h * HD : k * share + (h + 1) * HD] = v
    packed_grad = packed_grad_ref[...]
    bias_ref[...] = jnp.broadcast_to(jnp.sum(packed_grad.astype(f32), axis=0, keepdims=True), bias_ref.shape)
    half = near_ref.shape[0]
    for s, piece in enumerate(pieces):
        rows_grad = dot_nt(packed_grad, piece[:, : 3 * share]).astype(bf16)
        columns = piece_at(where_ref, s, piece)
        near_ref[:, columns] = rows_grad[:half]
        far_ref[:, columns] = rows_grad[half:]


def group_call(kernel, group_len, where, operands, specs, pieces, out_widths, out_types, flops):
    def spec(kind, shape):
        if kind == "rows":
            return pl.BlockSpec((group_len, shape[1]), lambda i, where: (i, 0))
        if kind == "pair":
            return pl.BlockSpec((1,) + shape[1:], lambda i, where: (i, 0, 0))
        return pl.BlockSpec(shape, lambda i, where: (0, 0), pipeline_mode=pl.Buffered(1))

    operands = tuple(operands) + tuple(pieces)
    specs = tuple(specs) + ("all",) * len(pieces)
    return pl.pallas_call(
        kernel,
        grid_spec=pltpu.PrefetchScalarGridSpec(
            num_scalar_prefetch=1,
            grid=(2,),
            in_specs=[spec(k, v.shape) for k, v in zip(specs, operands)],
            out_specs=[pl.BlockSpec((r, w), lambda i, where: (i, 0)) for r, w in out_widths],
        ),
        out_shape=[jax.ShapeDtypeStruct((2 * r, w), t) for (r, w), t in zip(out_widths, out_types)],
        compiler_params=pltpu.CompilerParams(vmem_limit_bytes=48 * 1024 * 1024),
        cost_estimate=pl.CostEstimate(flops=flops, bytes_accessed=sum(2 * v.size for v in operands), transcendentals=0),
    )(where, *operands)


def body(lay, tokens, dense_weights, expert_weights, gain_attn, gain_ffn, qkv_bias, router_weight, routes, doc_ids, out_grad):
    row_count, model_width = tokens.shape
    rings = lay.rings
    ring = lax.axis_index("ring")
    pair = lax.axis_index("pair")
    ep = lax.axis_index("ep")
    local_experts = expert_weights.shape[1]
    expert_count = router_weight.shape[1] - 1
    owners = expert_count // local_experts
    dp_count = rings * 2
    ring_place = jnp.asarray(lay.place, jnp.int32)[ring]
    behind = [jnp.asarray(lay.order, jnp.int32)[(ring_place - s) % rings] for s in range(rings)]
    ring_order = jnp.stack(behind)
    own_expert = ep * local_experts
    where = own_expert[None].astype(jnp.int32)

    stream = tokens.astype(f32)
    gain_one = gain_attn.astype(f32)
    gain_two = gain_ffn.astype(f32)
    heads = H // 8
    share = heads * HD
    unit_share = SFF // owners
    units = FF // dp_count
    n = row_count

    bits = jnp.sum(jnp.left_shift(jnp.int32(1), routes), axis=1, keepdims=True).astype(bf16)
    cot_blocks = [jnp.concatenate([out_grad, jnp.broadcast_to(bits, (row_count, 128))], axis=1)]
    mine, shared = deal_columns(after(dense_weights, cot_blocks[0]), share, owners)
    plane_part = lax.all_to_all(mine, PLANE, split_axis=0, concat_axis=0, tiled=True)
    plane_part = plane_part.reshape(-1, 4 * share)
    cot_blocks.append(permute(cot_blocks[0], lay.onward))
    mine, cot_blocks[1] = together(mine, cot_blocks[1])
    for _ in range(rings - 3):
        cot_blocks.append(permute(cot_blocks[-1], lay.onward))

    inverse_one = lax.rsqrt(jnp.mean(stream * stream, axis=1, keepdims=True) + norm_eps)
    normed = (stream * inverse_one * gain_one).astype(bf16)
    doc_pair = jnp.stack([doc_ids, permute(doc_ids, lay.up)])
    group_len = doc_ids.shape[0]
    before = jnp.sum((doc_pair[:, None, :] < doc_pair[:, :, None]).astype(jnp.int32), axis=2)
    spot = jnp.arange(group_len, dtype=jnp.int32)
    near_blocks = jnp.stack([ep, ep ^ 2, ep ^ 1, ep ^ 3])

    def in_order(values):
        return values.reshape(2, 4, row_count)[:, near_blocks].reshape(2, group_len)

    places = in_order(spot[None, :] - before)
    docs = in_order(doc_pair)
    spots = in_order(jnp.stack([spot, spot]))
    cosine, sine = rope_tables(places.reshape(-1))
    sine = jnp.where(jnp.arange(HD) < HD // 2, -sine, sine)
    spots_all = jnp.stack([docs, spots], axis=1)
    spots_own = jnp.stack([docs.reshape(-1), spots.reshape(-1)], axis=1)
    routed = expert_weights.reshape(expert_weights.shape[0], -1)
    router = router_weight.T
    turn = (own_expert + jnp.arange(expert_count, dtype=jnp.int32)) % expert_count
    router = stack(jnp.take(router, turn, axis=0), router[expert_count:])
    slot = pair * 4 + ep
    bias_share = lax.dynamic_slice_in_dim(qkv_bias.astype(f32).reshape(3, 8, share), slot, 1, 1).reshape(1, 3 * share)
    plane_part, cot_blocks[-1], routed, normed = together(plane_part, cot_blocks[-1], routed, normed)

    qkv = [plane_part, permute(plane_part, lay.onward)]
    cot_blocks.append(permute(cot_blocks[-1], lay.onward))
    side, up = permute(normed, lay.side), permute(normed, lay.up)

    def between_cores(*pieces):
        return [permute(piece, lay.core) for piece in pieces]

    def over(pairs, pieces):
        return [permute(piece, pairs) for piece in pieces]

    cot_sides, cot_ups = over(lay.side, cot_blocks[:1]), over(lay.up, cot_blocks[:1])
    cot_cores = between_cores(*cot_blocks)
    first_ffn, second_ffn = (turn_weights(routed, local_experts, dp_count, w) for w in range(local_experts))
    qkv[-1], cot_blocks[-1], side, up, cot_sides, cot_ups, cosine, sine, first_ffn, second_ffn = lax.optimization_barrier(
        (qkv[-1], cot_blocks[-1], side, up, cot_sides, cot_ups, cosine, sine, first_ffn, second_ffn)
    )
    for s in range(2, rings):
        qkv.append(permute(qkv[-1], lay.onward))
        sides, ups = [], []
        if s == 2:
            cross = permute(up, lay.side)
            cores = between_cores(normed, side, up)
            sides, ups = over(lay.side, cot_blocks[1:2]), over(lay.up, cot_blocks[1:3])
            cross, cores = lax.optimization_barrier((cross, cores))
        elif s == 3:
            cores += between_cores(cross)
            normed_group = assemble((normed, side, *cores[:2], up, cross, *cores[2:]))
            sides, ups = over(lay.side, cot_blocks[2:]), over(lay.up, cot_blocks[3:])
        sides, ups, qkv[-1] = lax.optimization_barrier((sides, ups, qkv[-1]))
        cot_sides, cot_ups = cot_sides + sides, cot_ups + ups
    qkv[-1], normed_group = together(qkv[-1], normed_group)

    cot_crosses = [
        permute(cot_sides[s], lay.up) if s % 2 else permute(cot_ups[s], lay.side) for s in range(rings)
    ]
    heads_flops = 8 * heads * group_len * group_len * HD
    packed, mixed = group_call(
        functools.partial(attend_kernel, heads),
        group_len,
        ring_order,
        (normed_group, bias_share, cosine, sine, spots_own, spots_all),
        ("rows", "all", "rows", "rows", "rows", "pair"),
        qkv,
        [(group_len, 3 * share), (group_len, share)],
        [bf16, bf16],
        4 * group_len * model_width * 3 * share + heads_flops,
    )
    received = [lax.dynamic_index_in_dim(shared, ep ^ k, 0, keepdims=False) for k in range(4)]
    received[1:3] = [permute(v, pairs) for v, pairs in zip(received[1:3], (lay.core, lay.side))]
    branch_parts = group_call(
        project_kernel,
        group_len,
        ring_order,
        (mixed,),
        ("rows",),
        qkv,
        [(group_len // 2, model_width)] * 2,
        [bf16, bf16],
        4 * group_len * model_width * share,
    )
    *branch_parts, cot_crosses, first_ffn = lax.optimization_barrier((*branch_parts, cot_crosses, first_ffn))

    def to_units(ffn):
        return lax.all_to_all(ffn, ("ring", "pair"), split_axis=0, concat_axis=0, tiled=True)

    first_ffn = to_units(first_ffn)
    here = plus(branch_parts[0], permute(branch_parts[1], lay.core))
    cross, side = permute(here[3 * n :], lay.side), permute(here[n : 2 * n], lay.side)
    cots = []
    for s in range(rings):
        cores = [cot_cores[s]] + between_cores(cot_ups[s], cot_sides[s], cot_crosses[s])
        cots += [cot_blocks[s], cot_ups[s], *cores[:2], cot_sides[s], cot_crosses[s], *cores[2:]]
    cots = assemble(cots)
    cross, cots = together(cross, cots)
    received[3] = permute(after(received[3], cross), lay.side_core)
    up = permute(plus(here[2 * n : 3 * n], cross), lay.up)
    branch = here[:n].astype(f32) + side.astype(f32) + after(up, first_ffn, *received[:3]).astype(f32)
    residual = stream + branch
    inverse_two = lax.rsqrt(jnp.mean(residual * residual, axis=1, keepdims=True) + norm_eps)
    normed_two = (residual * inverse_two * gain_two).astype(bf16)

    blocks, ups, sides, crosses, inner = [normed_two], [], [], [], []

    for s in range(rings):
        up = permute(blocks[s], lay.up)
        going = {}
        if s < rings - 1:
            going["onward"] = permute(blocks[s], lay.onward)
        if s == 0:
            going["received"] = received[3]
        else:
            going["side"] = permute(blocks[s - 1], lay.side)
        if s == rings - 2:
            first_rows = place_weights(first_ffn, router)
            going["first_rows"] = first_rows
        if s == rings - 1:
            crosses = {k: permute(sides[k], lay.up) for k in range(1, rings - 2, 2)}
            crosses[0] = permute(ups[0], lay.side)
            shared_ffn = jnp.stack(received)[jnp.arange(4, dtype=jnp.int32) ^ ep].reshape(-1, 3 * unit_share)
            second_ffn = jnp.concatenate([second_ffn, turn_weights(shared_ffn, 1, dp_count)], axis=1)
            going["crosses"], going["second_ffn"] = crosses, second_ffn
        up, going = lax.optimization_barrier((up, going))
        ups.append(up)
        if "onward" in going:
            blocks.append(going["onward"])
        if "side" in going:
            sides.append(going["side"])
        if "received" in going:
            received[3] = going["received"]
        if "first_rows" in going:
            first_rows = going["first_rows"]
        if "crosses" in going:
            crosses, second_ffn = going["crosses"], going["second_ffn"]
    second_ffn = to_units(second_ffn)
    sides.append(permute(blocks[-1], lay.side))
    crosses.update({k: permute(ups[k], lay.side) for k in range(rings) if k not in crosses})
    inner = [between_cores(blocks[s], ups[s], sides[s]) for s in range(rings)]
    rows = []
    for s in range(rings):
        cores = inner[s] + between_cores(crosses[s])
        rows += [blocks[s], ups[s], *cores[:2], sides[s], crosses[s], *cores[2:]]

    late = rings // 2
    rows, first_hidden, first_grad, first_weights_grad, first_router = first_units(
        (0,), where, rows, cots, *first_rows, units, expert_count, dp_count
    )
    first_weights_grad = to_units(first_weights_grad)
    second_rows = place_weights(after(second_ffn, first_hidden), router)

    chunk, half = 4 * n, 2 * n
    order = list(range(rings))[::-1]
    first_half, last_half = order[: rings - late], order[rings - late :]

    def cut_chunk(which, s, at):
        begin = (s % late if s < late else s - late) * chunk + at
        return which[begin : begin + half]

    def crossed(part, there, some):
        keep = {s: plus(cut_chunk(part, s, 0), cut_chunk(there, s, 0)) for s in some}
        send = {s: plus(cut_chunk(part, s, half), cut_chunk(there, s, half)) for s in some}
        return keep, send

    def all_there(*groups):
        flat, tree = jax.tree.flatten(groups)
        return jax.tree.unflatten(tree, lax.optimization_barrier(tuple(flat)))

    def ffn_half(first, chunks, kept):
        return second_units(
            (1, SHARED), first, chunks, where, rows, cots, (first_hidden, first_grad) + tuple(first_rows), second_rows, kept, units, expert_count
        )

    out_own_a, out_far_a, own_a, far_a, hidden, gate_up_grad = ffn_half(late, rings - late, ())
    own_a, far_a, first_weights_grad = all_there(own_a, far_a, first_weights_grad)

    keep, send = crossed(own_a, permute(far_a, lay.core), first_half)
    keep, send, hidden, gate_up_grad = all_there(keep, send, hidden, gate_up_grad)
    out_there_a = permute(after(out_far_a, hidden), lay.core)
    sided = {s: permute(send[s], lay.side) for s in first_half}
    out_own_b, out_far_b, own_b, far_b, hidden, gate_up_grad = ffn_half(0, late, (hidden, gate_up_grad))
    sided, own_b, far_b, hidden, gate_up_grad, out_there_a = all_there(
        sided, own_b, far_b, hidden, gate_up_grad, out_there_a
    )

    far_there = permute(far_b, lay.core)
    halves = {s: plus(keep[s], sided[s]) for s in first_half}
    upped = {order[0]: permute(halves[order[0]][n:], lay.up)}
    keep, send = crossed(own_b, far_there, last_half)
    keep, send, halves, hidden, upped = all_there(keep, send, halves, hidden, upped)
    own_sums = {order[0]: halves[order[0]][:n].astype(f32) + upped[order[0]].astype(f32)}
    total = own_sums[order[0]]
    queue = list(order[1:])

    def step_on(total):
        return permute(total.astype(bf16), lay.backward)

    def step_in(arrived):
        return own_sums[queue.pop(0)] + arrived.astype(f32)

    few = (len(last_half) + 1) // 2
    sided = {s: permute(send[s], lay.side) for s in last_half[:few]}
    upped = {s: permute(halves[s][n:], lay.up) for s in first_half[1:]}
    moving = step_on(total)
    ffn_grad, second_router = weight_grads(where, rows, cots, hidden, gate_up_grad, 2 * units, dp_count)
    out_there_b = permute(out_far_b, lay.core)
    sided, upped, moving, ffn_grad, out_there_b = all_there(sided, upped, moving, ffn_grad, out_there_b)
    own_sums.update({s: halves[s][:n].astype(f32) + upped[s].astype(f32) for s in first_half[1:]})
    total = step_in(moving)

    halves = {s: plus(keep[s], sided[s]) for s in last_half[:few]}
    sided = {s: permute(send[s], lay.side) for s in last_half[few:]}
    upped = {s: permute(halves[s][n:], lay.up) for s in last_half[:few]}
    moving = step_on(total)
    out_keep, out_send = crossed(out_own_a, out_there_a, first_half)
    sided, upped, moving, out_keep, out_send = all_there(sided, upped, moving, out_keep, out_send)
    own_sums.update({s: halves[s][:n].astype(f32) + upped[s].astype(f32) for s in last_half[:few]})
    total = step_in(moving)

    halves = {s: plus(keep[s], sided[s]) for s in last_half[few:]}
    upped = {s: permute(halves[s][n:], lay.up) for s in last_half[few:]}
    moving = step_on(total)
    more_keep, more_send = crossed(out_own_b, out_there_b, last_half)
    upped, moving, more_keep, more_send = all_there(upped, moving, more_keep, more_send)
    out_keep.update(more_keep)
    out_send.update(more_send)
    own_sums.update({s: halves[s][:n].astype(f32) + upped[s].astype(f32) for s in last_half[few:]})
    total = step_in(moving)
    while queue:
        total = step_in(step_on(total))
    normed_two_grad = total

    def router_rows(part, wide):
        start = wide - wide // 8 * 8
        return part[start : start + expert_count + 1]

    router_part = router_rows(first_router, units) + router_rows(second_router, 2 * units)
    turn_back = (jnp.arange(expert_count, dtype=jnp.int32) - own_expert) % expert_count
    router_part = stack(jnp.take(router_part[:expert_count], turn_back, axis=0), router_part[expert_count:])

    cotangent = out_grad.astype(f32)
    scaled_two = normed_two_grad * gain_two
    gain_two_grad = jnp.sum(normed_two_grad * residual * inverse_two, axis=0)
    residual_grad = (
        cotangent
        + inverse_two * scaled_two
        - residual * inverse_two**3 * jnp.mean(scaled_two * residual, axis=1, keepdims=True)
    )
    branch_grad = residual_grad.astype(bf16)

    side, up = permute(branch_grad, lay.side), permute(branch_grad, lay.up)
    core = permute(branch_grad, lay.core)
    side, up, core, ffn_grad = together(side, up, core, ffn_grad)
    ffn_grad = lax.all_to_all(ffn_grad, ("ring", "pair"), split_axis=0, concat_axis=0, tiled=True)
    cross = permute(up, lay.side)
    cores = [core, *between_cores(side, up)]
    cores.append(permute(cross, lay.core))
    branch_grad_group = assemble((branch_grad, side, *cores[:2], up, cross, *cores[2:]))
    keep, send = out_keep, out_send
    branch_grad_group = together(branch_grad_group)[0]

    quarter = [order[k :: 4] for k in range(4)] if rings > 4 else [[s] for s in order]
    sided = {s: permute(send[s], lay.side) for s in quarter[0]}
    packed_grad, near, far, bias_part = group_call(
        functools.partial(attend_back_kernel, heads),
        group_len,
        ring_order,
        (branch_grad_group, packed, cosine, sine, spots_own, spots_all),
        ("rows", "rows", "rows", "rows", "rows", "pair"),
        qkv,
        [(group_len, 3 * share), (group_len // 2, model_width), (group_len // 2, model_width), (8, 3 * share)],
        [bf16, bf16, bf16, f32],
        4 * group_len * model_width * 4 * share + 3 * heads_flops,
    )
    sided, packed_grad, near, far = all_there(sided, packed_grad, near, far)

    halves = {s: plus(keep[s], sided[s]) for s in quarter[0]}
    sided = {s: permute(send[s], lay.side) for s in quarter[1]}
    here = plus(near, permute(far, lay.core))
    attn_grads = jnp.concatenate([dot_over(normed_group, packed_grad), dot_over(branch_grad_group, mixed)], axis=1)
    attn_grads = attn_grads.astype(bf16).reshape(rings, -1, 4 * share)
    sided, attn_grads, here, halves = all_there(sided, attn_grads, here, halves)

    out_halves = {s: plus(keep[s], sided[s]) for s in quarter[1]}
    out_halves.update(halves)
    side, cross = permute(here[n : 2 * n], lay.side), permute(here[3 * n :], lay.side)
    def grads_at(s):
        return lax.dynamic_index_in_dim(attn_grads, behind[s], 0, keepdims=False).astype(f32)

    moving = permute(grads_at(order[0]).astype(bf16), lay.backward)
    side, cross, ffn_grad = together(side, cross, ffn_grad)

    up = permute(plus(here[2 * n : 3 * n], cross), lay.up)
    sided = {s: permute(send[s], lay.side) for s in quarter[2]}
    first_up = permute(out_halves[order[0]][n:], lay.up)
    sided, up, moving, first_up = all_there(sided, up, moving, first_up)
    output_sum = out_halves[order[0]][:n].astype(f32) + first_up.astype(f32)
    normed_grad = here[:n].astype(f32) + side.astype(f32) + up.astype(f32)
    scaled_one = normed_grad * gain_one
    gain_one_grad = jnp.sum(normed_grad * stream * inverse_one, axis=0)
    input_grad = (
        residual_grad
        + inverse_one * scaled_one
        - stream * inverse_one**3 * jnp.mean(scaled_one * stream, axis=1, keepdims=True)
    )
    bias_part = (bias_part[0] + bias_part[8]).reshape(3, 1, share)
    bias_part = lax.dynamic_update_slice(jnp.zeros((3, 8, share), f32), bias_part, (0, slot, 0))
    small = stack(router_part, gain_two_grad[None], gain_one_grad[None], bias_part.reshape(3, model_width))
    doubling = lay.doubling()

    total = grads_at(order[1]) + moving.astype(f32)
    out_halves.update({s: plus(keep[s], sided[s]) for s in quarter[2]})
    out_sums, out_queue = {}, list(order[1:])

    def outs_on(output_sum):
        return permute(output_sum.astype(bf16), lay.backward)

    def outs_over(some):
        return {s: permute(out_halves[s][n:], lay.up) for s in some}

    def outs_in(outs_up):
        out_sums.update({s: out_halves[s][:n].astype(f32) + outs_up[s].astype(f32) for s in outs_up})

    moving = permute(total.astype(bf16), lay.backward)
    outs_up = outs_over((quarter[0] + quarter[1])[1:])
    sided = {s: permute(send[s], lay.side) for s in quarter[3]}
    small = small + permute(small, doubling[0])
    shared_columns_grad, expert_grad = turn_grads(first_weights_grad, ffn_grad)
    shared_columns_grad = lax.all_to_all(
        shared_columns_grad.reshape(owners, -1, 3 * unit_share), "ep", split_axis=0, concat_axis=0, tiled=True
    )
    moving, outs_up, sided, small, expert_grad = all_there(moving, outs_up, sided, small, expert_grad)
    outs_in(outs_up)
    out_halves.update({s: plus(keep[s], sided[s]) for s in quarter[3]})

    total = grads_at(order[2]) + moving.astype(f32)
    moving = permute(total.astype(bf16), lay.backward)
    outs_up = outs_over(quarter[2] + quarter[3])
    output_sum = after(output_sum, outs_up[order[2]])
    outgoing = [outs_on(v) for v in (output_sum[: n // 2], output_sum[n // 2 :])]
    for step in doubling[1:3]:
        small = small + permute(small, step)
    moving, shared_columns_grad, outs_up, small = all_there(moving, shared_columns_grad, outs_up, small)
    outs_in(outs_up)
    total = grads_at(order[3]) + moving.astype(f32)
    for s in order[4:]:
        total = grads_at(s) + permute(total.astype(bf16), lay.backward).astype(f32)

    total, small = all_there(total.astype(bf16), small)
    total = total.reshape(8, -1, 4 * share)
    total = lax.all_to_all(total, PLANE, split_axis=0, concat_axis=0, tiled=True)
    for s in out_queue[:-1]:
        outgoing = [outs_on(out_sums[s][k * n // 2 : (k + 1) * n // 2] + v.astype(f32)) for k, v in enumerate(outgoing)]
    output_sum = out_sums[out_queue[-1]] + stack(*outgoing).astype(f32)
    for step in doubling[3:]:
        small = small + permute(small, step)
    output = (residual + output_sum).astype(bf16)
    dense_grad = collect_columns(total, shared_columns_grad, share)

    router_sum, gain_two_sum, gain_one_sum, bias_sum = jnp.split(small, [expert_count + 1, expert_count + 2, expert_count + 3])
    return (
        output,
        input_grad,
        dense_grad,
        expert_grad,
        gain_one_sum[0],
        gain_two_sum[0],
        bias_sum.reshape(-1),
        router_sum.T,
    )


def solution(mesh):
    devices = mesh.devices
    lay = Layout(devices.shape[0] // 2)
    inner = Mesh(devices.reshape(lay.rings, 2, devices.shape[1]), AXES)
    rows = P(AXES, None)
    experts = P(("ring", "pair"), "ep", None)
    in_specs = (rows, rows, experts, P(), P(), P(), P(), rows, P(("ring", "pair")), rows)
    out_specs = (rows, rows, rows, experts, P(), P(), P(), P())

    def run(*arguments):
        return body(lay, *arguments)

    return jax.shard_map(run, mesh=inner, in_specs=in_specs, out_specs=out_specs, check_vma=False)
```

```python
import functools

import jax
import jax.numpy as jnp
from jax import lax
from jax.experimental import pallas as pl
from jax.experimental.pallas import tpu as pltpu
from jax.sharding import Mesh, PartitionSpec as P

H = 16
HD = 128
FF = 1408
SFF = 5632

norm_eps = 1e-06
rope_base = 1000000.0
AXES = ("ring", "pair", "ep")
PLANE = ("pair", "ep")
SHARED = -1
f32 = jnp.float32
bf16 = jnp.bfloat16


class Layout:
    def __init__(self, rings):
        self.rings = rings
        self.order = list(range(0, rings, 2)) + list(range(1, rings, 2))[::-1]
        place = {r: i for i, r in enumerate(self.order)}
        self.place = [place[r] for r in range(rings)]
        self.core = self.pairs(lambda r, y, x, c: (r, y, x, 1 - c))
        self.side = self.pairs(lambda r, y, x, c: (r, y, 1 - x, c))
        self.side_core = self.pairs(lambda r, y, x, c: (r, y, 1 - x, 1 - c))
        self.up = self.pairs(lambda r, y, x, c: (r, 1 - y, x, c))
        self.cross = self.pairs(lambda r, y, x, c: (r, 1 - y, 1 - x, c))
        self.onward = self.pairs(lambda r, y, x, c: (self.order[(place[r] + 1) % rings], y, x, c))
        self.backward = self.pairs(lambda r, y, x, c: (self.order[(place[r] - 1) % rings], y, x, c))

    def pairs(self, move):
        found = []
        for r in range(self.rings):
            for y in range(2):
                for x in range(2):
                    for c in range(2):
                        u, v, w, q = move(r, y, x, c)
                        found.append((((r * 2 + y) * 2 + x) * 2 + c, ((u * 2 + v) * 2 + w) * 2 + q))
        return found

    def doubling(self):
        steps = []
        bit = 1
        while bit < self.rings * 8:
            steps.append([(i, i ^ bit) for i in range(self.rings * 8)])
            bit *= 2
        return steps


def permute(rows, pairs):
    return lax.ppermute(rows, AXES, pairs)


def stack(*parts):
    return jnp.concatenate(parts, axis=0)


def plus(a, b):
    return (a.astype(f32) + b.astype(f32)).astype(bf16)


def assemble_kernel(*refs):
    parts, out_ref, sems = refs[:-2], refs[-2], refs[-1]
    copies, at = [], 0
    for i, part in enumerate(parts):
        size = part.shape[0]
        copies.append(pltpu.make_async_copy(part, out_ref.at[pl.ds(at, size)], sems.at[i]))
        copies[-1].start()
        at += size
    for copy in copies:
        copy.wait()


def assemble(parts):
    rows = sum(part.shape[0] for part in parts)
    width = parts[0].shape[1]
    if rows * width > 1 << 24:
        return stack(*parts)
    return pl.pallas_call(
        assemble_kernel,
        in_specs=[pl.BlockSpec(memory_space=pltpu.VMEM)] * len(parts),
        out_specs=pl.BlockSpec(memory_space=pl.ANY),
        out_shape=jax.ShapeDtypeStruct((rows, width), bf16),
        scratch_shapes=[pltpu.SemaphoreType.DMA((len(parts),))],
        compiler_params=pltpu.CompilerParams(vmem_limit_bytes=48 * 1024 * 1024),
        cost_estimate=pl.CostEstimate(flops=0, bytes_accessed=4 * rows * width, transcendentals=0),
    )(*parts)


def rope_tables(places):
    steps_along = jnp.arange(HD // 2, dtype=f32) * (2.0 / HD)
    inverse = jnp.power(jnp.float32(rope_base), -steps_along)
    angles = places.astype(f32)[..., None] * inverse
    angles = jnp.concatenate([angles, angles], axis=-1)
    return jnp.cos(angles), jnp.sin(angles)


def dot(a, b):
    return jnp.dot(a, b, preferred_element_type=f32)


def dot_over(a, b):
    return jnp.einsum("tc,tf->cf", a, b, preferred_element_type=f32)


def after(value, *others):
    return lax.optimization_barrier((value,) + others)[0]


def together(*values):
    return lax.optimization_barrier(values)


def dot_nt(a, b):
    return lax.dot_general(a, b, (((1,), (1,)), ((), ())), preferred_element_type=f32)


def dot_tn(a, b):
    return lax.dot_general(a, b, (((0,), (0,)), ((), ())), preferred_element_type=f32)


def units_pass(gate_up, hidden_grad, gates):
    pad = hidden_grad.shape[1]
    g, u = gate_up[:, :pad], gate_up[:, pad:]
    sig = jax.nn.sigmoid(g)
    silu = g * sig
    hidden = (silu * u).astype(bf16).astype(f32)
    gated_grad = hidden_grad * gates
    up_grad = gated_grad * silu
    gate_grad = gated_grad * u * (sig + silu * (1.0 - sig))
    return (gates * hidden).astype(bf16), gate_grad, up_grad, hidden_grad * hidden


def with_logits(gate_grad, logit_grad, up_grad, base, at):
    lane = lax.broadcasted_iota(jnp.int32, logit_grad.shape, 1)
    parts = [gate_grad[:, :base]] if base else []
    parts.append(jnp.where(lane < at, gate_grad[:, base : base + 128], logit_grad))
    if base + 128 < gate_grad.shape[1]:
        parts.append(gate_grad[:, base + 128 :])
    return jnp.concatenate(parts + [up_grad], axis=1).astype(bf16)


def hand_out(wide, gate_sums, down_sums, out_ref, router_ref):
    pad = down_sums.shape[0]
    first = wide // 8 * 8
    router_ref[...] = gate_sums[first : first + router_ref.shape[0]]
    if len(out_ref.shape) == 2:
        out_ref[: 2 * pad] = gate_sums[...].astype(bf16)
        out_ref[2 * pad :] = down_sums[...].astype(bf16)
        return
    count, _, block = out_ref.shape
    for d in range(count):
        lanes = slice(d * block, (d + 1) * block)
        out_ref[d, :wide] = gate_sums[:wide, lanes].astype(bf16)
        out_ref[d, wide : 2 * wide] = gate_sums[pad : pad + wide, lanes].astype(bf16)
        out_ref[d, 2 * wide :] = down_sums[:wide, lanes].astype(bf16)


def add_grads(grad, rows, hidden, cots, gate_sums, down_sums):
    @pl.when(pl.program_id(0) == 0)
    def _():
        gate_sums[...] = jnp.zeros_like(gate_sums)
        down_sums[...] = jnp.zeros_like(down_sums)

    gate_sums[...] += dot_tn(grad, rows)
    down_sums[...] += dot_tn(hidden, cots)


def group_pass(groups, units, experts, where_ref, rows_ref, cots_ref, gate_ref, down_ref):
    n, width = rows_ref.shape
    pad = down_ref.shape[0]
    wide = units * len(groups)
    base = wide // 128 * 128
    at = wide - base
    gate_up = dot_nt(rows_ref[...], gate_ref[...])
    hidden_grad = dot_nt(cots_ref[:, :width], down_ref[...])
    logits = gate_up[:, base : base + 128]
    place = lax.broadcasted_iota(jnp.int32, (n, 128), 1) - at
    routed = (place >= 0) & (place < experts)
    bits = cots_ref[:, width : width + 128].astype(f32).astype(jnp.int32)
    turn = jnp.where(routed, lax.rem(where_ref[0] + place, experts), 0)
    chosen = (jnp.right_shift(bits, turn) & 1).astype(f32)
    peak = jnp.max(jnp.where(routed, logits, -jnp.inf), axis=1, keepdims=True)
    weights = jnp.where(routed, jnp.exp(logits - peak), 0.0)
    probs = weights / jnp.sum(weights, axis=1, keepdims=True)
    shared = jax.nn.sigmoid(logits)
    spot = lax.broadcasted_iota(jnp.int32, (128, pad), 1)
    lane = lax.broadcasted_iota(jnp.int32, (128, pad), 0) - at
    spread = jnp.zeros((128, pad), f32)
    for i, group in enumerate(groups):
        own = (spot >= i * units) & (spot < (i + 1) * units) & (lane == (experts if group == SHARED else group))
        spread = jnp.where(own, 1.0, spread)
    spread = spread.astype(bf16)
    gates = dot(jnp.where(place == experts, shared, probs * chosen).astype(bf16), spread)
    gated, gate_grad, up_grad, products = units_pass(gate_up, hidden_grad, gates)
    sums = dot_nt(products.astype(bf16), spread)
    own = sums * chosen
    mean = jnp.sum(jnp.where(routed, probs * own, 0.0), axis=1, keepdims=True)
    logit_grad = jnp.where(routed, probs * (own - mean), jnp.where(place == experts, sums * shared * (1.0 - shared), 0.0))
    return gated, with_logits(gate_grad, logit_grad, up_grad, base, at)


def first_kernel(groups, units, experts, count, where_ref, *refs):
    pieces, cot_pieces, refs = refs[:count], refs[count : 2 * count], refs[2 * count :]
    gate_ref, down_ref, rows_ref, cots_ref, hidden_ref, grad_ref, out_ref, router_ref, *scratch = refs
    gate_sums, down_sums, held, held_cots, sems = scratch
    step, steps = pl.program_id(0), pl.num_programs(0)
    each, size = held.shape[1] // pieces[0].shape[0], pieces[0].shape[0]

    def copies(at, slot, t):
        place = pl.ds(t * size, size)
        return (
            pltpu.make_async_copy(pieces[at], held.at[slot, place], sems.at[slot, t]),
            pltpu.make_async_copy(cot_pieces[at], held_cots.at[slot, place], sems.at[slot, each + t]),
        )

    for j in range(count // each):

        @pl.when(step == max(j - 1, 0))
        def _(j=j):
            for t in range(each):
                for copy in copies(j * each + t, j % 2, t):
                    copy.start()

    slot = lax.rem(step, 2)
    for t in range(each):
        for copy in copies(t, slot, t):
            copy.wait()
    rows_ref[...] = held[slot]
    cots_ref[...] = held_cots[slot]
    gated, grad = group_pass(groups, units, experts, where_ref, rows_ref, cots_ref, gate_ref, down_ref)
    hidden_ref[...] = gated
    grad_ref[...] = grad
    add_grads(grad, rows_ref[...], gated, cots_ref[:, : rows_ref.shape[1]], gate_sums, down_sums)

    @pl.when(step == steps - 1)
    def _():
        hand_out(units * len(groups), gate_sums, down_sums, out_ref, router_ref)


def grads_kernel(wide, where_ref, rows_ref, cots_ref, hidden_ref, grad_ref, out_ref, router_ref, gate_sums, down_sums):
    cots = cots_ref[:, : rows_ref.shape[1]]
    add_grads(grad_ref[...], rows_ref[...], hidden_ref[...], cots, gate_sums, down_sums)

    @pl.when(pl.program_id(0) == pl.num_programs(0) - 1)
    def _():
        hand_out(wide, gate_sums, down_sums, out_ref, router_ref)


def second_kernel(
    groups, units, experts, where_ref, rows_ref, cots_ref, hidden_in_ref, grad_in_ref, gate_in_ref, down_in_ref, gate_ref, down_ref, *refs
):
    out_own_ref, out_far_ref, own_ref, far_ref, hidden_ref, grad_ref = refs[-6:]
    half = own_ref.shape[0]
    gated, grad = group_pass(groups, units, experts, where_ref, rows_ref, cots_ref, gate_ref, down_ref)
    hidden_ref[...] = gated
    grad_ref[...] = grad
    rows_grad = (dot(grad_in_ref[...], gate_in_ref[...]) + dot(grad, gate_ref[...])).astype(bf16)
    own_ref[...] = rows_grad[:half]
    far_ref[...] = rows_grad[half:]
    out_part = (dot(hidden_in_ref[...], down_in_ref[...]) + dot(gated, down_ref[...])).astype(bf16)
    out_own_ref[...] = out_part[:half]
    out_far_ref[...] = out_part[half:]


def among_all(w, tile, first=0):
    return pl.BlockSpec((tile, w), lambda i, where: (first + i, 0))


def all_of(shape):
    return pl.BlockSpec(shape, lambda i, where: (0,) * len(shape), pipeline_mode=pl.Buffered(1))


def grads_out(wide, pad, width, count):
    direct = whole_tiles(wide, width // count)
    return (count, 3 * wide, width // count) if direct else (3 * pad, width), (24, width)


def to_owners(grad, wide, count):
    if len(grad.shape) == 3:
        return grad
    grad = grad.reshape(3, -1, grad.shape[1])[:, :wide]
    return grad.reshape(3 * wide, count, -1).transpose(1, 0, 2)


def token_grid(cots, rows, tile=512):
    return rows.shape[0] // tile, tile, [among_all(rows.shape[1], tile), among_all(cots.shape[1], tile)]


def first_units(groups, where, pieces, cot_pieces, gate_rows, down_rows, units, experts, count):
    total, width, wider = sum(v.shape[0] for v in pieces), gate_rows.shape[1], cot_pieces[0].shape[1]
    pad = down_rows.shape[0]
    wide = units * len(groups)
    tile = 512
    shapes = grads_out(wide, pad, width, count)
    rows, cots, hidden, grad, weights, router = pl.pallas_call(
        functools.partial(first_kernel, groups, units, experts, len(pieces)),
        grid_spec=pltpu.PrefetchScalarGridSpec(
            num_scalar_prefetch=1,
            grid=(total // tile,),
            in_specs=[pl.BlockSpec(memory_space=pl.ANY)] * (2 * len(pieces))
            + [all_of(gate_rows.shape), all_of(down_rows.shape)],
            out_specs=[among_all(width, tile), among_all(wider, tile), among_all(pad, tile), among_all(2 * pad, tile)]
            + [all_of(shape) for shape in shapes],
            scratch_shapes=[
                pltpu.VMEM((2 * pad, width), f32),
                pltpu.VMEM((pad, width), f32),
                pltpu.VMEM((2, tile, width), bf16),
                pltpu.VMEM((2, tile, wider), bf16),
                pltpu.SemaphoreType.DMA((2, 2 * tile // pieces[0].shape[0])),
            ],
        ),
        out_shape=[
            jax.ShapeDtypeStruct((total, width), bf16),
            jax.ShapeDtypeStruct((total, wider), bf16),
            jax.ShapeDtypeStruct((total, pad), bf16),
            jax.ShapeDtypeStruct((total, 2 * pad), bf16),
            jax.ShapeDtypeStruct(shapes[0], bf16),
            jax.ShapeDtypeStruct(shapes[1], f32),
        ],
        compiler_params=pltpu.CompilerParams(vmem_limit_bytes=60 * 1024 * 1024),
        cost_estimate=pl.CostEstimate(flops=12 * total * width * pad, bytes_accessed=4 * total * width, transcendentals=0),
    )(where, *pieces, *cot_pieces, gate_rows, down_rows)
    return rows, cots, hidden, grad, to_owners(weights, wide, count), router


def weight_grads(where, rows, cots, hidden, grad, wide, count):
    total, width = rows.shape
    pad = hidden.shape[1]
    steps, tile, token_specs = token_grid(cots, rows)
    shapes = grads_out(wide, pad, width, count)
    weights, router = pl.pallas_call(
        functools.partial(grads_kernel, wide),
        grid_spec=pltpu.PrefetchScalarGridSpec(
            num_scalar_prefetch=1,
            grid=(steps,),
            in_specs=token_specs + [among_all(pad, tile), among_all(2 * pad, tile)],
            out_specs=[all_of(shapes[0]), all_of(shapes[1])],
            scratch_shapes=[pltpu.VMEM((2 * pad, width), f32), pltpu.VMEM((pad, width), f32)],
        ),
        out_shape=[jax.ShapeDtypeStruct(shapes[0], bf16), jax.ShapeDtypeStruct(shapes[1], f32)],
        compiler_params=pltpu.CompilerParams(vmem_limit_bytes=58 * 1024 * 1024),
        cost_estimate=pl.CostEstimate(flops=6 * total * width * pad, bytes_accessed=4 * total * width, transcendentals=0),
    )(where, rows, cots, hidden, grad)
    return to_owners(weights, wide, count), router


def second_units(groups, first, chunks, where, rows, cots, before, own, kept, units, experts):
    total, width = rows.shape
    steps, tile = chunks * 2, 512
    hidden_in, grad_in, gate_in, down_in = before
    gate_rows, down_rows = own
    pad = down_rows.shape[0]

    def half(w):
        return pl.BlockSpec((tile // 2, w), lambda i, where: (i, 0))

    def tokens_of(v):
        return among_all(v if isinstance(v, int) else v.shape[1], tile, first * 2)

    kept = list(kept)
    shapes = [(steps * tile // 2, width)] * 4 + [(total, pad), (total, 2 * pad)]
    return pl.pallas_call(
        functools.partial(second_kernel, groups, units, experts),
        grid_spec=pltpu.PrefetchScalarGridSpec(
            num_scalar_prefetch=1,
            grid=(steps,),
            in_specs=[tokens_of(rows), tokens_of(cots)]
            + [tokens_of(hidden_in), tokens_of(grad_in)]
            + [all_of(v.shape) for v in (gate_in, down_in, gate_rows, down_rows)]
            + [pl.BlockSpec(memory_space=pl.ANY)] * len(kept),
            out_specs=[half(width)] * 4 + [tokens_of(pad), tokens_of(2 * pad)],
        ),
        out_shape=[jax.ShapeDtypeStruct(shape, bf16) for shape in shapes],
        input_output_aliases={9 + i: 4 + i for i in range(len(kept))},
        compiler_params=pltpu.CompilerParams(vmem_limit_bytes=58 * 1024 * 1024),
        cost_estimate=pl.CostEstimate(flops=10 * steps * tile * width * pad, bytes_accessed=8 * steps * tile * width, transcendentals=0),
    )(where, rows, cots, hidden_in, grad_in, gate_in, down_in, gate_rows, down_rows, *kept)


def whole_tiles(units, rows):
    return units % 16 == 0 and rows % 128 == 0


def turn_kernel(columns_ref, out_ref):
    count, units, rows = out_ref.shape
    out_ref[...] = columns_ref[...].T.reshape(count, units, rows)


def turn_weights(columns, who, count, which=0):
    rows, width = columns.shape
    span = width // (3 * who)
    units = span // count
    if not whole_tiles(units, rows):
        columns = columns.reshape(rows, who, 3, count, units)[:, which]
        return columns.transpose(2, 1, 3, 0).reshape(count, -1, rows)
    return pl.pallas_call(
        turn_kernel,
        grid=(3,),
        in_specs=[pl.BlockSpec((rows, span), lambda k: (0, which * 3 + k))],
        out_specs=pl.BlockSpec((count, units, rows), lambda k: (0, k, 0)),
        out_shape=jax.ShapeDtypeStruct((count, 3 * units, rows), bf16),
        compiler_params=pltpu.CompilerParams(vmem_limit_bytes=32 * 1024 * 1024),
        cost_estimate=pl.CostEstimate(flops=0, bytes_accessed=4 * rows * 3 * span, transcendentals=0),
    )(columns)


def turn_back_kernel(first_ref, second_ref, shared_ref, routed_ref):
    count, units, rows = first_ref.shape

    def turned(block):
        return block.reshape(count * units, rows).T

    routed_ref[:, 0, :] = turned(first_ref[...]).astype(f32)
    routed_ref[:, 1, :] = turned(second_ref[:, :units]).astype(f32)
    shared_ref[...] = turned(second_ref[:, units:])


def turn_grads(first, second):
    count, units, rows = first.shape
    units = units // 3
    span = units * count
    if not whole_tiles(units, rows):
        second = second.reshape(count, 3, 2, units, rows)
        first = first.reshape(count, 3, units, rows)
        three = jnp.stack([first, second[:, :, 0], second[:, :, 1]]).transpose(0, 4, 2, 1, 3).reshape(3, rows, 3 * span)
        return three[2], jnp.moveaxis(three[:2], 0, 1).astype(f32)
    return pl.pallas_call(
        turn_back_kernel,
        grid=(3,),
        in_specs=[
            pl.BlockSpec((count, units, rows), lambda k: (0, k, 0)),
            pl.BlockSpec((count, 2 * units, rows), lambda k: (0, k, 0)),
        ],
        out_specs=[
            pl.BlockSpec((rows, span), lambda k: (0, k)),
            pl.BlockSpec((rows, 2, span), lambda k: (0, 0, k)),
        ],
        out_shape=[jax.ShapeDtypeStruct((rows, 3 * span), bf16), jax.ShapeDtypeStruct((rows, 2, 3 * span), f32)],
        compiler_params=pltpu.CompilerParams(vmem_limit_bytes=56 * 1024 * 1024),
        cost_estimate=pl.CostEstimate(flops=0, bytes_accessed=48 * rows * span, transcendentals=0),
    )(first, second)


def deal_kernel(share, dense_ref, attn_ref, shared_ref):
    width = share * 8
    for o in range(8):
        for k in range(4):
            at = k * width + o * share
            attn_ref[o, :, k * share : (k + 1) * share] = dense_ref[:, at : at + share]
    owners, _, columns = shared_ref.shape
    span = columns // 3
    for o in range(owners):
        for k in range(3):
            at = 4 * width + (k * owners + o) * span
            shared_ref[o, :, k * span : (k + 1) * span] = dense_ref[:, at : at + span]


def deal_columns(dense, share, owners):
    rows, columns = dense.shape
    shapes = [(8, rows, 4 * share), (owners, rows, (columns - 32 * share) // owners)]
    return pl.pallas_call(
        functools.partial(deal_kernel, share),
        out_shape=[jax.ShapeDtypeStruct(shape, bf16) for shape in shapes],
        compiler_params=pltpu.CompilerParams(vmem_limit_bytes=32 * 1024 * 1024),
        cost_estimate=pl.CostEstimate(flops=0, bytes_accessed=4 * rows * columns, transcendentals=0),
    )(dense)


def collect_kernel(share, attn_ref, shared_ref, dense_ref):
    width = share * 8
    for o in range(8):
        for k in range(4):
            at = k * width + o * share
            dense_ref[:, at : at + share] = attn_ref[o, :, k * share : (k + 1) * share].astype(f32)
    owners, _, columns = shared_ref.shape
    span = columns // 3
    for o in range(owners):
        for k in range(3):
            at = 4 * width + (k * owners + o) * span
            dense_ref[:, at : at + span] = shared_ref[o, :, k * span : (k + 1) * span].astype(f32)


def collect_columns(attn, shared, share):
    rows = attn.shape[1]
    columns = 32 * share + shared.shape[0] * shared.shape[2]
    return pl.pallas_call(
        functools.partial(collect_kernel, share),
        out_shape=jax.ShapeDtypeStruct((rows, columns), f32),
        compiler_params=pltpu.CompilerParams(vmem_limit_bytes=32 * 1024 * 1024),
        cost_estimate=pl.CostEstimate(flops=0, bytes_accessed=6 * rows * columns, transcendentals=0),
    )(attn, shared)


def place_kernel(units, *refs):
    parts, (router_ref, gate_ref, down_ref) = refs[:-3], refs[-3:]
    pad = down_ref.shape[0]
    wide = units * len(parts)
    blank = jnp.zeros((pad - wide, down_ref.shape[1]), bf16)
    for w, part in enumerate(parts):
        for k, (out_ref, at) in enumerate(((gate_ref, 0), (gate_ref, pad), (down_ref, 0))):
            out_ref[at + w * units : at + (w + 1) * units] = part[0, k * units : (k + 1) * units]
    gate_ref[wide:pad] = router_ref[...]
    gate_ref[pad + wide :] = blank
    down_ref[wide:] = blank


def place_weights(ffn, router):
    count, _, block = ffn.shape
    units = FF // count
    who = ffn.shape[1] // (3 * units)
    wide = units * who
    width = count * block
    pad = (wide + router.shape[0] + 127) // 128 * 128
    router = stack(router, jnp.zeros((pad - wide - router.shape[0], width), bf16))
    if not whole_tiles(units, block):
        gate, up, down = ffn.transpose(1, 0, 2).reshape(who, 3, units, width).transpose(1, 0, 2, 3).reshape(3, wide, width)
        blank = jnp.zeros((pad - wide, width), bf16)
        return stack(gate, router, up, blank), stack(down, blank)

    def column(r):
        return pl.BlockSpec((r, block), lambda i: (0, i))

    return pl.pallas_call(
        functools.partial(place_kernel, units),
        grid=(count,),
        in_specs=[pl.BlockSpec((1, 3 * units, block), lambda i, w=w: (i, w, 0)) for w in range(who)] + [column(pad - wide)],
        out_specs=[column(2 * pad), column(pad)],
        out_shape=[jax.ShapeDtypeStruct((r, width), bf16) for r in (2 * pad, pad)],
        compiler_params=pltpu.CompilerParams(vmem_limit_bytes=32 * 1024 * 1024),
        cost_estimate=pl.CostEstimate(flops=0, bytes_accessed=12 * wide * width, transcendentals=0),
    )(*[ffn] * who, router)


def attend_rows(queries, keys, allowed):
    scores = jnp.where(allowed, dot_nt(queries, keys) * HD ** (-0.5), -1e30)
    raw = jnp.exp(scores - jnp.max(scores, axis=1, keepdims=True))
    return raw / jnp.sum(raw, axis=1, keepdims=True)


def allowed_pairs(own_ref, all_ref):
    return (own_ref[:, :1] == all_ref[0, :1]) & (all_ref[0, 1:2] <= own_ref[:, 1:2])


def piece_at(where_ref, s, piece_ref):
    size = piece_ref.shape[0]
    return pl.ds(pl.multiple_of(where_ref[s] * size, size), size)


def attend_kernel(heads, where_ref, rows_ref, bias_ref, cosine_ref, sine_ref, own_ref, all_ref, *refs):
    pieces, (packed_ref, mixed_ref) = refs[:-2], refs[-2:]
    share = heads * HD
    packed = bias_ref[...]
    for s, piece in enumerate(pieces):
        packed = packed + dot(rows_ref[:, piece_at(where_ref, s, piece)], piece[:, : 3 * share])
    cosine, sine = cosine_ref[...], sine_ref[...]
    allowed = allowed_pairs(own_ref, all_ref)

    def turned(at):
        v = packed[:, at : at + HD]
        return (v * cosine + pltpu.roll(v, HD // 2, 1) * sine).astype(bf16)

    for h in range(heads):
        queries, keys = turned(h * HD), turned(share + h * HD)
        values = packed[:, 2 * share + h * HD : 2 * share + (h + 1) * HD].astype(bf16)
        attend = attend_rows(queries, keys, allowed)
        mixed_ref[:, h * HD : (h + 1) * HD] = dot(attend.astype(bf16), values).astype(bf16)
        for k, v in enumerate((queries, keys, values)):
            packed_ref[:, k * share + h * HD : k * share + (h + 1) * HD] = v


def project_kernel(where_ref, mixed_ref, *refs):
    pieces, (near_ref, far_ref) = refs[:-2], refs[-2:]
    half = near_ref.shape[0]
    for s, piece in enumerate(pieces):
        rows = dot_nt(mixed_ref[...], piece[:, piece.shape[1] * 3 // 4 :]).astype(bf16)
        columns = piece_at(where_ref, s, piece)
        near_ref[:, columns] = rows[:half]
        far_ref[:, columns] = rows[half:]


def attend_back_kernel(heads, where_ref, grad_ref, packed_ref, cosine_ref, sine_ref, own_ref, all_ref, *refs):
    pieces, (packed_grad_ref, near_ref, far_ref, bias_ref) = refs[:-4], refs[-4:]
    share = heads * HD
    scale = HD ** (-0.5)
    mixed_grad = 0.0
    for s, piece in enumerate(pieces):
        mixed_grad = mixed_grad + dot(grad_ref[:, piece_at(where_ref, s, piece)], piece[:, 3 * share :])
    mixed_grad = mixed_grad.astype(bf16)
    cosine, sine = cosine_ref[...], sine_ref[...]
    allowed = allowed_pairs(own_ref, all_ref)

    def back(v):
        v = v.astype(bf16).astype(f32)
        return (v * cosine - pltpu.roll(v, HD // 2, 1) * sine).astype(bf16)

    for h in range(heads):
        queries, keys, values = (
            packed_ref[:, k * share + h * HD : k * share + (h + 1) * HD] for k in range(3)
        )
        own_grad = mixed_grad[:, h * HD : (h + 1) * HD]
        attend = attend_rows(queries, keys, allowed)
        attend_grad = dot_nt(own_grad, values)
        scores_grad = attend * (attend_grad - jnp.sum(attend * attend_grad, axis=1, keepdims=True))
        scores_grad = scores_grad.astype(bf16)
        grads = (
            back(dot(scores_grad, keys) * scale),
            back(dot_tn(scores_grad, queries) * scale),
            dot_tn(attend.astype(bf16), own_grad).astype(bf16),
        )
        for k, v in enumerate(grads):
            packed_grad_ref[:, k * share + h * HD : k * share + (h + 1) * HD] = v
    packed_grad = packed_grad_ref[...]
    bias_ref[...] = jnp.broadcast_to(jnp.sum(packed_grad.astype(f32), axis=0, keepdims=True), bias_ref.shape)
    half = near_ref.shape[0]
    for s, piece in enumerate(pieces):
        rows_grad = dot_nt(packed_grad, piece[:, : 3 * share]).astype(bf16)
        columns = piece_at(where_ref, s, piece)
        near_ref[:, columns] = rows_grad[:half]
        far_ref[:, columns] = rows_grad[half:]


def group_call(kernel, group_len, where, operands, specs, pieces, out_widths, out_types, flops):
    def spec(kind, shape):
        if kind == "rows":
            return pl.BlockSpec((group_len, shape[1]), lambda i, where: (i, 0))
        if kind == "pair":
            return pl.BlockSpec((1,) + shape[1:], lambda i, where: (i, 0, 0))
        return pl.BlockSpec(shape, lambda i, where: (0, 0), pipeline_mode=pl.Buffered(1))

    operands = tuple(operands) + tuple(pieces)
    specs = tuple(specs) + ("all",) * len(pieces)
    return pl.pallas_call(
        kernel,
        grid_spec=pltpu.PrefetchScalarGridSpec(
            num_scalar_prefetch=1,
            grid=(2,),
            in_specs=[spec(k, v.shape) for k, v in zip(specs, operands)],
            out_specs=[pl.BlockSpec((r, w), lambda i, where: (i, 0)) for r, w in out_widths],
        ),
        out_shape=[jax.ShapeDtypeStruct((2 * r, w), t) for (r, w), t in zip(out_widths, out_types)],
        compiler_params=pltpu.CompilerParams(vmem_limit_bytes=48 * 1024 * 1024),
        cost_estimate=pl.CostEstimate(flops=flops, bytes_accessed=sum(2 * v.size for v in operands), transcendentals=0),
    )(where, *operands)


def body(lay, tokens, dense_weights, expert_weights, gain_attn, gain_ffn, qkv_bias, router_weight, routes, doc_ids, out_grad):
    row_count, model_width = tokens.shape
    rings = lay.rings
    ring = lax.axis_index("ring")
    pair = lax.axis_index("pair")
    ep = lax.axis_index("ep")
    local_experts = expert_weights.shape[1]
    expert_count = router_weight.shape[1] - 1
    owners = expert_count // local_experts
    dp_count = rings * 2
    ring_place = jnp.asarray(lay.place, jnp.int32)[ring]
    behind = [jnp.asarray(lay.order, jnp.int32)[(ring_place - s) % rings] for s in range(rings)]
    ring_order = jnp.stack(behind)
    own_expert = ep * local_experts
    where = own_expert[None].astype(jnp.int32)

    stream = tokens.astype(f32)
    gain_one = gain_attn.astype(f32)
    gain_two = gain_ffn.astype(f32)
    heads = H // 8
    share = heads * HD
    unit_share = SFF // owners
    units = FF // dp_count
    n = row_count

    bits = jnp.sum(jnp.left_shift(jnp.int32(1), routes), axis=1, keepdims=True).astype(bf16)
    cot_blocks = [jnp.concatenate([out_grad, jnp.broadcast_to(bits, (row_count, 128))], axis=1)]
    mine, shared = deal_columns(after(dense_weights, cot_blocks[0]), share, owners)
    plane_part = lax.all_to_all(mine, PLANE, split_axis=0, concat_axis=0, tiled=True)
    plane_part = plane_part.reshape(-1, 4 * share)
    cot_blocks.append(permute(cot_blocks[0], lay.onward))
    mine, cot_blocks[1] = together(mine, cot_blocks[1])
    for _ in range(rings - 3):
        cot_blocks.append(permute(cot_blocks[-1], lay.onward))

    inverse_one = lax.rsqrt(jnp.mean(stream * stream, axis=1, keepdims=True) + norm_eps)
    normed = (stream * inverse_one * gain_one).astype(bf16)
    doc_pair = jnp.stack([doc_ids, permute(doc_ids, lay.up)])
    group_len = doc_ids.shape[0]
    before = jnp.sum((doc_pair[:, None, :] < doc_pair[:, :, None]).astype(jnp.int32), axis=2)
    spot = jnp.arange(group_len, dtype=jnp.int32)
    near_blocks = jnp.stack([ep, ep ^ 2, ep ^ 1, ep ^ 3])

    def in_order(values):
        return values.reshape(2, 4, row_count)[:, near_blocks].reshape(2, group_len)

    places = in_order(spot[None, :] - before)
    docs = in_order(doc_pair)
    spots = in_order(jnp.stack([spot, spot]))
    cosine, sine = rope_tables(places.reshape(-1))
    sine = jnp.where(jnp.arange(HD) < HD // 2, -sine, sine)
    spots_all = jnp.stack([docs, spots], axis=1)
    spots_own = jnp.stack([docs.reshape(-1), spots.reshape(-1)], axis=1)
    routed = expert_weights.reshape(expert_weights.shape[0], -1)
    router = router_weight.T
    turn = (own_expert + jnp.arange(expert_count, dtype=jnp.int32)) % expert_count
    router = stack(jnp.take(router, turn, axis=0), router[expert_count:])
    slot = pair * 4 + ep
    bias_share = lax.dynamic_slice_in_dim(qkv_bias.astype(f32).reshape(3, 8, share), slot, 1, 1, allow_negative_indices=False).reshape(1, 3 * share)
    plane_part, cot_blocks[-1], routed, normed = together(plane_part, cot_blocks[-1], routed, normed)

    qkv = [plane_part, permute(plane_part, lay.onward)]
    side, up = permute(normed, lay.side), permute(normed, lay.up)

    def between_cores(*pieces):
        return [permute(piece, lay.core) for piece in pieces]

    def over(pairs, pieces):
        return [permute(piece, pairs) for piece in pieces]

    cot_sides, cot_ups = over(lay.side, cot_blocks[:1]), over(lay.up, cot_blocks[:1])
    first_ffn, second_ffn = (turn_weights(routed, local_experts, dp_count, w) for w in range(local_experts))
    qkv[-1], side, up, cot_sides, cot_ups, cosine, sine, first_ffn, second_ffn = lax.optimization_barrier(
        (qkv[-1], side, up, cot_sides, cot_ups, cosine, sine, first_ffn, second_ffn)
    )
    cot_crosses = []

    def crossing(s):
        return permute(cot_sides[s], lay.up) if s % 2 else permute(cot_ups[s], lay.side)

    for s in range(2, rings):
        qkv.append(permute(qkv[-1], lay.onward))
        sides, ups = [], []
        if s == 2:
            cross = permute(up, lay.side)
            cores = between_cores(normed, side, up)
            sides, ups = over(lay.side, cot_blocks[1:2]), over(lay.up, cot_blocks[1:3])
            cross, cores = lax.optimization_barrier((cross, cores))
        elif s == 3:
            cores += between_cores(cross)
            normed_group = assemble((normed, side, *cores[:2], up, cross, *cores[2:]))
            sides, ups = over(lay.side, cot_blocks[2:]), over(lay.up, cot_blocks[3:])
            cot_crosses = [crossing(0), crossing(1)]
        sides, ups, qkv[-1], cot_crosses = lax.optimization_barrier((sides, ups, qkv[-1], cot_crosses))
        cot_sides, cot_ups = cot_sides + sides, cot_ups + ups
    qkv[-1], normed_group = together(qkv[-1], normed_group)

    cot_blocks.append(permute(after(cot_blocks[-1], qkv[-1]), lay.onward))
    cot_crosses += [crossing(s) for s in range(2, rings - 1)]
    heads_flops = 8 * heads * group_len * group_len * HD
    packed, mixed = group_call(
        functools.partial(attend_kernel, heads),
        group_len,
        ring_order,
        (normed_group, bias_share, cosine, sine, spots_own, spots_all),
        ("rows", "all", "rows", "rows", "rows", "pair"),
        qkv,
        [(group_len, 3 * share), (group_len, share)],
        [bf16, bf16],
        4 * group_len * model_width * 3 * share + heads_flops,
    )
    packed, mixed, cot_crosses, cot_blocks = lax.optimization_barrier((packed, mixed, cot_crosses, cot_blocks))
    cot_sides += over(lay.side, cot_blocks[-1:])
    cot_ups += over(lay.up, cot_blocks[-1:])
    received = [lax.dynamic_index_in_dim(shared, ep ^ k, 0, keepdims=False, allow_negative_indices=False) for k in range(4)]
    received[1:3] = [permute(v, pairs) for v, pairs in zip(received[1:3], (lay.core, lay.side))]
    branch_parts = group_call(
        project_kernel,
        group_len,
        ring_order,
        (mixed,),
        ("rows",),
        qkv,
        [(group_len // 2, model_width)] * 2,
        [bf16, bf16],
        4 * group_len * model_width * share,
    )

    def to_units(ffn):
        return lax.all_to_all(ffn, ("ring", "pair"), split_axis=0, concat_axis=0, tiled=True)

    first_ffn = to_units(after(first_ffn, packed))
    here = plus(branch_parts[0], permute(branch_parts[1], lay.core))
    cross, side = permute(here[3 * n :], lay.side), permute(here[n : 2 * n], lay.side)
    received[3] = permute(after(received[3], cross), lay.side_core)
    up = permute(plus(here[2 * n : 3 * n], cross), lay.up)
    up, cot_sides, cot_ups = lax.optimization_barrier((up, cot_sides, cot_ups))
    branch = here[:n].astype(f32) + side.astype(f32) + after(up, first_ffn, *received[:3]).astype(f32)
    cot_crosses.append(permute(cot_ups[-1], lay.side))
    residual = stream + branch
    inverse_two = lax.rsqrt(jnp.mean(residual * residual, axis=1, keepdims=True) + norm_eps)
    normed_two = (residual * inverse_two * gain_two).astype(bf16)

    blocks, ups, sides, crosses, inner = [normed_two], [], [], [], []

    for s in range(rings):
        up = permute(blocks[s], lay.up)
        going = {}
        if s < rings - 1:
            going["onward"] = permute(blocks[s], lay.onward)
        if s == 0:
            going["received"] = received[3]
        else:
            going["side"] = permute(blocks[s - 1], lay.side)
        if s == 1:
            going["crosses_too"] = cot_crosses
        if s == rings - 2:
            first_rows = place_weights(first_ffn, router)
            going["first_rows"] = first_rows
        if s == rings - 1:
            crosses = {k: permute(sides[k], lay.up) for k in range(1, rings - 2, 2)}
            crosses[0] = permute(ups[0], lay.side)
            shared_ffn = jnp.stack(received)[jnp.arange(4, dtype=jnp.int32) ^ ep].reshape(-1, 3 * unit_share)
            second_ffn = jnp.concatenate([second_ffn, turn_weights(shared_ffn, 1, dp_count)], axis=1)
            going["crosses"], going["second_ffn"] = crosses, second_ffn
        up, going = lax.optimization_barrier((up, going))
        ups.append(up)
        if "onward" in going:
            blocks.append(going["onward"])
        if "side" in going:
            sides.append(going["side"])
        if "crosses_too" in going:
            cot_crosses = going["crosses_too"]
        if "received" in going:
            received[3] = going["received"]
        if "first_rows" in going:
            first_rows = going["first_rows"]
        if "crosses" in going:
            crosses, second_ffn = going["crosses"], going["second_ffn"]
    second_ffn = to_units(second_ffn)
    sides.append(permute(blocks[-1], lay.side))
    crosses.update({k: permute(ups[k], lay.side) for k in range(2, rings - 1) if k not in crosses})
    cots = list(zip(cot_blocks, cot_ups, cot_sides, cot_crosses))
    cot_cores = [between_cores(*v) for v in cots]
    inner = [between_cores(blocks[s], ups[s], sides[s]) for s in range(rings - 1)]
    sides[-1], ups[-1], crosses, cot_cores, inner = lax.optimization_barrier((sides[-1], ups[-1], crosses, cot_cores, inner))
    crosses[rings - 1] = permute(ups[-1], lay.side)
    inner.append(between_cores(blocks[-1], ups[-1], sides[-1]))
    cot_pieces = []
    for (block, up, side, cross), cores in zip(cots, cot_cores):
        cot_pieces += [block, up, *cores[:2], side, cross, *cores[2:]]
    rows = []
    for s in range(rings):
        cores = inner[s] + between_cores(crosses[s])
        rows += [blocks[s], ups[s], *cores[:2], sides[s], crosses[s], *cores[2:]]

    late = rings // 2
    rows, cots, first_hidden, first_grad, first_weights_grad, first_router = first_units(
        (0,), where, rows, cot_pieces, *first_rows, units, expert_count, dp_count
    )
    first_weights_grad = to_units(first_weights_grad)
    second_rows = place_weights(after(second_ffn, first_hidden), router)

    chunk, half = 4 * n, 2 * n
    order = list(range(rings))[::-1]
    first_half, last_half = order[: rings - late], order[rings - late :]

    def cut_chunk(which, s, at):
        begin = (s % late if s < late else s - late) * chunk + at
        return which[begin : begin + half]

    def crossed(part, there, some):
        keep = {s: plus(cut_chunk(part, s, 0), cut_chunk(there, s, 0)) for s in some}
        send = {s: plus(cut_chunk(part, s, half), cut_chunk(there, s, half)) for s in some}
        return keep, send

    def all_there(*groups):
        flat, tree = jax.tree.flatten(groups)
        return jax.tree.unflatten(tree, lax.optimization_barrier(tuple(flat)))

    def ffn_half(first, chunks, kept):
        return second_units(
            (1, SHARED), first, chunks, where, rows, cots, (first_hidden, first_grad) + tuple(first_rows), second_rows, kept, units, expert_count
        )

    out_own_a, out_far_a, own_a, far_a, hidden, gate_up_grad = ffn_half(late, rings - late, ())
    own_a, far_a, first_weights_grad = all_there(own_a, far_a, first_weights_grad)

    pair_first = order[1::2]

    def link(s, second):
        return lay.side if (s in pair_first) == second else lay.up

    def split(part, there, some):
        keep, send = crossed(part, there, [s for s in some if s not in pair_first])
        for s in some:
            if s in pair_first:
                pieces = [plus(*(cut_chunk(v, s, t * n)[:n] for v in (part, there))) for t in range(4)]
                keep[s], send[s] = stack(pieces[0], pieces[2]), stack(pieces[1], pieces[3])
        return keep, send

    def start(send, some):
        return {s: permute(send[s], link(s, False)) for s in some}

    def go_on(keep, arrived, some):
        halves = {s: plus(keep[s], arrived[s]) for s in some}
        return halves, {s: permute(halves[s][n:], link(s, True)) for s in some}

    def finish(halves, arrived):
        return {s: halves[s][:n].astype(f32) + arrived[s].astype(f32) for s in halves}

    keep, send = split(own_a, permute(far_a, lay.core), first_half)
    keep, send, hidden, gate_up_grad = all_there(keep, send, hidden, gate_up_grad)
    out_there_a = permute(after(out_far_a, hidden), lay.core)
    arrived = start(send, first_half)
    out_own_b, out_far_b, own_b, far_b, hidden, gate_up_grad = ffn_half(0, late, (hidden, gate_up_grad))
    arrived, own_b, far_b, hidden, gate_up_grad, out_there_a = all_there(
        arrived, own_b, far_b, hidden, gate_up_grad, out_there_a
    )

    far_there = permute(far_b, lay.core)
    halves, arrived = go_on(keep, arrived, first_half)
    keep, send = split(own_b, far_there, last_half)
    keep, send, halves, arrived, hidden = all_there(keep, send, halves, arrived, hidden)
    own_sums = finish(halves, arrived)
    total = own_sums[order[0]]
    queue = list(order[1:])

    def step_on(total):
        return permute(total.astype(bf16), lay.backward)

    def step_in(arrived):
        return own_sums[queue.pop(0)] + arrived.astype(f32)

    arrived = start(send, last_half)
    moving = step_on(total)
    ffn_grad, second_router = weight_grads(where, rows, cots, hidden, gate_up_grad, 2 * units, dp_count)
    out_there_b = permute(out_far_b, lay.core)
    arrived, moving, ffn_grad, out_there_b = all_there(arrived, moving, ffn_grad, out_there_b)
    total = step_in(moving)

    halves, arrived = go_on(keep, arrived, last_half)
    moving = step_on(total)
    out_keep, out_send = crossed(out_own_a, out_there_a, first_half)
    halves, arrived, moving, out_keep, out_send = all_there(halves, arrived, moving, out_keep, out_send)
    own_sums.update(finish(halves, arrived))
    total = step_in(moving)

    moving = step_on(total)
    more_keep, more_send = crossed(out_own_b, out_there_b, last_half)
    moving, more_keep, more_send = all_there(moving, more_keep, more_send)
    out_keep.update(more_keep)
    out_send.update(more_send)
    total = step_in(moving)
    while queue:
        total = step_in(step_on(total))
    normed_two_grad = total

    def router_rows(part, wide):
        start = wide - wide // 8 * 8
        return part[start : start + expert_count + 1]

    router_part = router_rows(first_router, units) + router_rows(second_router, 2 * units)
    turn_back = (jnp.arange(expert_count, dtype=jnp.int32) - own_expert) % expert_count
    router_part = stack(jnp.take(router_part[:expert_count], turn_back, axis=0), router_part[expert_count:])

    cotangent = out_grad.astype(f32)
    scaled_two = normed_two_grad * gain_two
    gain_two_grad = jnp.sum(normed_two_grad * residual * inverse_two, axis=0)
    residual_grad = (
        cotangent
        + inverse_two * scaled_two
        - residual * inverse_two**3 * jnp.mean(scaled_two * residual, axis=1, keepdims=True)
    )
    branch_grad = residual_grad.astype(bf16)

    side, up = permute(branch_grad, lay.side), permute(branch_grad, lay.up)
    core = permute(branch_grad, lay.core)
    side, up, core, ffn_grad = together(side, up, core, ffn_grad)
    ffn_grad = lax.all_to_all(ffn_grad, ("ring", "pair"), split_axis=0, concat_axis=0, tiled=True)
    cross = permute(up, lay.side)
    cores = [core, *between_cores(side, up)]
    cores.append(permute(cross, lay.core))
    branch_grad_group = assemble((branch_grad, side, *cores[:2], up, cross, *cores[2:]))
    keep, send = out_keep, out_send
    branch_grad_group = together(branch_grad_group)[0]

    quarter = [order[k :: 4] for k in range(4)] if rings > 4 else [[s] for s in order]
    sided = {s: permute(send[s], lay.side) for s in quarter[0]}
    packed_grad, near, far, bias_part = group_call(
        functools.partial(attend_back_kernel, heads),
        group_len,
        ring_order,
        (branch_grad_group, packed, cosine, sine, spots_own, spots_all),
        ("rows", "rows", "rows", "rows", "rows", "pair"),
        qkv,
        [(group_len, 3 * share), (group_len // 2, model_width), (group_len // 2, model_width), (8, 3 * share)],
        [bf16, bf16, bf16, f32],
        4 * group_len * model_width * 4 * share + 3 * heads_flops,
    )
    sided, packed_grad, near, far = all_there(sided, packed_grad, near, far)

    halves = {s: plus(keep[s], sided[s]) for s in quarter[0]}
    sided = {s: permute(send[s], lay.side) for s in quarter[1]}
    here = plus(near, permute(far, lay.core))
    attn_grads = jnp.concatenate([dot_over(normed_group, packed_grad), dot_over(branch_grad_group, mixed)], axis=1)
    attn_grads = attn_grads.astype(bf16).reshape(rings, -1, 4 * share)
    sided, attn_grads, here, halves = all_there(sided, attn_grads, here, halves)

    out_halves = {s: plus(keep[s], sided[s]) for s in quarter[1]}
    out_halves.update(halves)
    side, cross = permute(here[n : 2 * n], lay.side), permute(here[3 * n :], lay.side)
    def grads_at(s):
        return lax.dynamic_index_in_dim(attn_grads, behind[s], 0, keepdims=False, allow_negative_indices=False).astype(f32)

    moving = permute(grads_at(order[0]).astype(bf16), lay.backward)
    side, cross, ffn_grad = together(side, cross, ffn_grad)

    up = permute(plus(here[2 * n : 3 * n], cross), lay.up)
    sided = {s: permute(send[s], lay.side) for s in quarter[2]}
    first_up = permute(out_halves[order[0]][n:], lay.up)
    sided, up, moving, first_up = all_there(sided, up, moving, first_up)
    output_sum = out_halves[order[0]][:n].astype(f32) + first_up.astype(f32)
    normed_grad = here[:n].astype(f32) + side.astype(f32) + up.astype(f32)
    scaled_one = normed_grad * gain_one
    gain_one_grad = jnp.sum(normed_grad * stream * inverse_one, axis=0)
    input_grad = (
        residual_grad
        + inverse_one * scaled_one
        - stream * inverse_one**3 * jnp.mean(scaled_one * stream, axis=1, keepdims=True)
    )
    bias_part = (bias_part[0] + bias_part[8]).reshape(3, 1, share)
    bias_part = lax.dynamic_update_slice(jnp.zeros((3, 8, share), f32), bias_part, (0, slot, 0), allow_negative_indices=False)
    small = stack(router_part, gain_two_grad[None], gain_one_grad[None], bias_part.reshape(3, model_width))
    doubling = lay.doubling()

    total = grads_at(order[1]) + moving.astype(f32)
    out_halves.update({s: plus(keep[s], sided[s]) for s in quarter[2]})
    out_sums, out_queue = {}, list(order[1:])

    def outs_on(output_sum):
        return permute(output_sum.astype(bf16), lay.backward)

    def outs_over(some):
        return {s: permute(out_halves[s][n:], lay.up) for s in some}

    def outs_in(outs_up):
        out_sums.update({s: out_halves[s][:n].astype(f32) + outs_up[s].astype(f32) for s in outs_up})

    moving = permute(total.astype(bf16), lay.backward)
    outs_up = outs_over((quarter[0] + quarter[1])[1:])
    sided = {s: permute(send[s], lay.side) for s in quarter[3]}
    small = small + permute(small, doubling[3])
    shared_columns_grad, expert_grad = turn_grads(first_weights_grad, ffn_grad)
    shared_columns_grad = lax.all_to_all(
        shared_columns_grad.reshape(owners, -1, 3 * unit_share), "ep", split_axis=0, concat_axis=0, tiled=True
    )
    moving, outs_up, sided, small, expert_grad = all_there(moving, outs_up, sided, small, expert_grad)
    outs_in(outs_up)
    out_halves.update({s: plus(keep[s], sided[s]) for s in quarter[3]})

    total = grads_at(order[2]) + moving.astype(f32)
    moving = permute(total.astype(bf16), lay.backward)
    outs_up = outs_over(quarter[2] + quarter[3])
    output_sum = after(output_sum, outs_up[order[2]])
    outgoing = [outs_on(v) for v in (output_sum[: n // 2], output_sum[n // 2 :])]
    for step in doubling[:3]:
        small = small + permute(small, step)
    moving, shared_columns_grad, outs_up, small = all_there(moving, shared_columns_grad, outs_up, small)
    outs_in(outs_up)
    total = grads_at(order[3]) + moving.astype(f32)
    for s in order[4:]:
        total = grads_at(s) + permute(total.astype(bf16), lay.backward).astype(f32)

    total, small = all_there(total.astype(bf16), small)
    total = total.reshape(8, -1, 4 * share)
    total = lax.all_to_all(total, PLANE, split_axis=0, concat_axis=0, tiled=True)
    for s in out_queue[:-1]:
        outgoing = [outs_on(out_sums[s][k * n // 2 : (k + 1) * n // 2] + v.astype(f32)) for k, v in enumerate(outgoing)]
    total, small = together(total, small)
    dense_grad = collect_columns(total, shared_columns_grad, share)
    dense_grad, *outgoing = together(dense_grad, *outgoing)
    output_sum = out_sums[out_queue[-1]] + stack(*outgoing).astype(f32)
    for step in doubling[4:]:
        small = small + permute(small, step)
    output = (residual + output_sum).astype(bf16)

    router_sum, gain_two_sum, gain_one_sum, bias_sum = jnp.split(small, [expert_count + 1, expert_count + 2, expert_count + 3])
    return (
        output,
        input_grad,
        dense_grad,
        expert_grad,
        gain_one_sum[0],
        gain_two_sum[0],
        bias_sum.reshape(-1),
        router_sum.T,
    )


def solution(mesh):
    devices = mesh.devices
    lay = Layout(devices.shape[0] // 2)
    inner = Mesh(devices.reshape(lay.rings, 2, devices.shape[1]), AXES)
    rows = P(AXES, None)
    experts = P(("ring", "pair"), "ep", None)
    in_specs = (rows, rows, experts, P(), P(), P(), P(), rows, P(("ring", "pair")), rows)
    out_specs = (rows, rows, rows, experts, P(), P(), P(), P())

    def run(*arguments):
        return body(lay, *arguments)

    return jax.shard_map(run, mesh=inner, in_specs=in_specs, out_specs=out_specs, check_vma=False)
```

```python
import functools

import jax
import jax.numpy as jnp
from jax import lax
from jax.experimental import pallas as pl
from jax.experimental.pallas import tpu as pltpu
from jax.sharding import Mesh, PartitionSpec as P

H = 16
HD = 128
FF = 1408
SFF = 5632

norm_eps = 1e-06
rope_base = 1000000.0
AXES = ("ring", "pair", "ep")
PLANE = ("pair", "ep")
SHARED = -1
f32 = jnp.float32
bf16 = jnp.bfloat16


class Layout:
    def __init__(self, rings):
        self.rings = rings
        self.order = list(range(0, rings, 2)) + list(range(1, rings, 2))[::-1]
        place = {r: i for i, r in enumerate(self.order)}
        self.place = [place[r] for r in range(rings)]
        self.core = self.pairs(lambda r, y, x, c: (r, y, x, 1 - c))
        self.side = self.pairs(lambda r, y, x, c: (r, y, 1 - x, c))
        self.side_core = self.pairs(lambda r, y, x, c: (r, y, 1 - x, 1 - c))
        self.up = self.pairs(lambda r, y, x, c: (r, 1 - y, x, c))
        self.cross = self.pairs(lambda r, y, x, c: (r, 1 - y, 1 - x, c))
        self.onward = self.pairs(lambda r, y, x, c: (self.order[(place[r] + 1) % rings], y, x, c))
        self.backward = self.pairs(lambda r, y, x, c: (self.order[(place[r] - 1) % rings], y, x, c))

    def pairs(self, move):
        found = []
        for r in range(self.rings):
            for y in range(2):
                for x in range(2):
                    for c in range(2):
                        u, v, w, q = move(r, y, x, c)
                        found.append((((r * 2 + y) * 2 + x) * 2 + c, ((u * 2 + v) * 2 + w) * 2 + q))
        return found

    def doubling(self):
        steps = []
        bit = 1
        while bit < self.rings * 8:
            steps.append([(i, i ^ bit) for i in range(self.rings * 8)])
            bit *= 2
        return steps


def permute(rows, pairs):
    return lax.ppermute(rows, AXES, pairs)


def stack(*parts):
    return jnp.concatenate(parts, axis=0)


def plus(a, b):
    return (a.astype(f32) + b.astype(f32)).astype(bf16)


def assemble_kernel(*refs):
    parts, out_ref, sems = refs[:-2], refs[-2], refs[-1]
    copies, at = [], 0
    for i, part in enumerate(parts):
        size = part.shape[0]
        copies.append(pltpu.make_async_copy(part, out_ref.at[pl.ds(at, size)], sems.at[i]))
        copies[-1].start()
        at += size
    for copy in copies:
        copy.wait()


def assemble(parts):
    rows = sum(part.shape[0] for part in parts)
    width = parts[0].shape[1]
    if rows * width > 1 << 24:
        return stack(*parts)
    return pl.pallas_call(
        assemble_kernel,
        in_specs=[pl.BlockSpec(memory_space=pltpu.VMEM)] * len(parts),
        out_specs=pl.BlockSpec(memory_space=pl.ANY),
        out_shape=jax.ShapeDtypeStruct((rows, width), bf16),
        scratch_shapes=[pltpu.SemaphoreType.DMA((len(parts),))],
        compiler_params=pltpu.CompilerParams(vmem_limit_bytes=48 * 1024 * 1024),
        cost_estimate=pl.CostEstimate(flops=0, bytes_accessed=4 * rows * width, transcendentals=0),
    )(*parts)


def rope_tables(places):
    steps_along = jnp.arange(HD // 2, dtype=f32) * (2.0 / HD)
    inverse = jnp.power(jnp.float32(rope_base), -steps_along)
    angles = places.astype(f32)[..., None] * inverse
    angles = jnp.concatenate([angles, angles], axis=-1)
    return jnp.cos(angles), jnp.sin(angles)


def dot(a, b):
    return jnp.dot(a, b, preferred_element_type=f32)


def dot_over(a, b):
    return jnp.einsum("tc,tf->cf", a, b, preferred_element_type=f32)


def after(value, *others):
    return lax.optimization_barrier((value,) + others)[0]


def together(*values):
    return lax.optimization_barrier(values)


def dot_nt(a, b):
    return lax.dot_general(a, b, (((1,), (1,)), ((), ())), preferred_element_type=f32)


def dot_tn(a, b):
    return lax.dot_general(a, b, (((0,), (0,)), ((), ())), preferred_element_type=f32)


def units_pass(gate_up, hidden_grad, gates):
    pad = hidden_grad.shape[1]
    g, u = gate_up[:, :pad], gate_up[:, pad:]
    sig = jax.nn.sigmoid(g)
    silu = g * sig
    hidden = (silu * u).astype(bf16).astype(f32)
    gated_grad = hidden_grad * gates
    up_grad = gated_grad * silu
    gate_grad = gated_grad * u * (sig + silu * (1.0 - sig))
    return (gates * hidden).astype(bf16), gate_grad, up_grad, hidden_grad * hidden


def with_logits(gate_grad, logit_grad, up_grad, base, at):
    lane = lax.broadcasted_iota(jnp.int32, logit_grad.shape, 1)
    parts = [gate_grad[:, :base]] if base else []
    parts.append(jnp.where(lane < at, gate_grad[:, base : base + 128], logit_grad))
    if base + 128 < gate_grad.shape[1]:
        parts.append(gate_grad[:, base + 128 :])
    return jnp.concatenate(parts + [up_grad], axis=1).astype(bf16)


def hand_out(wide, gate_sums, down_sums, out_ref, router_ref):
    pad = down_sums.shape[0]
    first = wide // 8 * 8
    router_ref[...] = gate_sums[first : first + router_ref.shape[0]]
    if len(out_ref.shape) == 2:
        out_ref[: 2 * pad] = gate_sums[...].astype(bf16)
        out_ref[2 * pad :] = down_sums[...].astype(bf16)
        return
    count, _, block = out_ref.shape
    for d in range(count):
        lanes = slice(d * block, (d + 1) * block)
        out_ref[d, :wide] = gate_sums[:wide, lanes].astype(bf16)
        out_ref[d, wide : 2 * wide] = gate_sums[pad : pad + wide, lanes].astype(bf16)
        out_ref[d, 2 * wide :] = down_sums[:wide, lanes].astype(bf16)


def add_grads(grad, rows, hidden, cots, gate_sums, down_sums, before=()):
    @pl.when(pl.program_id(0) == 0)
    def _():
        gate_sums[...] = before[0][...] if before else jnp.zeros_like(gate_sums)
        down_sums[...] = before[1][...] if before else jnp.zeros_like(down_sums)

    gate_sums[...] += dot_tn(grad, rows)
    down_sums[...] += dot_tn(hidden, cots)


def group_pass(groups, units, experts, where_ref, rows_ref, cots_ref, gate_ref, down_ref):
    n, width = rows_ref.shape
    pad = down_ref.shape[0]
    wide = units * len(groups)
    base = wide // 128 * 128
    at = wide - base
    gate_up = dot_nt(rows_ref[...], gate_ref[...])
    hidden_grad = dot_nt(cots_ref[:, :width], down_ref[...])
    logits = gate_up[:, base : base + 128]
    place = lax.broadcasted_iota(jnp.int32, (n, 128), 1) - at
    routed = (place >= 0) & (place < experts)
    bits = cots_ref[:, width : width + 128].astype(f32).astype(jnp.int32)
    turn = jnp.where(routed, lax.rem(where_ref[0] + place, experts), 0)
    chosen = (jnp.right_shift(bits, turn) & 1).astype(f32)
    peak = jnp.max(jnp.where(routed, logits, -jnp.inf), axis=1, keepdims=True)
    weights = jnp.where(routed, jnp.exp(logits - peak), 0.0)
    probs = weights / jnp.sum(weights, axis=1, keepdims=True)
    shared = jax.nn.sigmoid(logits)
    spot = lax.broadcasted_iota(jnp.int32, (128, pad), 1)
    lane = lax.broadcasted_iota(jnp.int32, (128, pad), 0) - at
    spread = jnp.zeros((128, pad), f32)
    for i, group in enumerate(groups):
        own = (spot >= i * units) & (spot < (i + 1) * units) & (lane == (experts if group == SHARED else group))
        spread = jnp.where(own, 1.0, spread)
    spread = spread.astype(bf16)
    gates = dot(jnp.where(place == experts, shared, probs * chosen).astype(bf16), spread)
    gated, gate_grad, up_grad, products = units_pass(gate_up, hidden_grad, gates)
    sums = dot_nt(products.astype(bf16), spread)
    own = sums * chosen
    mean = jnp.sum(jnp.where(routed, probs * own, 0.0), axis=1, keepdims=True)
    logit_grad = jnp.where(routed, probs * (own - mean), jnp.where(place == experts, sums * shared * (1.0 - shared), 0.0))
    return gated, with_logits(gate_grad, logit_grad, up_grad, base, at)


def first_kernel(groups, units, experts, count, last, where_ref, *refs):
    pieces, cot_pieces, refs = refs[:count], refs[count : 2 * count], refs[2 * count :]
    gate_ref, down_ref, *before = refs[: 4 if last else 2]
    rows_ref, cots_ref, hidden_ref, grad_ref, *outs, held, held_cots, sems = refs[8 if last else 2 :]
    gate_sums, down_sums = outs[-2:]
    step, steps = pl.program_id(0), pl.num_programs(0)
    each, size = held.shape[1] // pieces[0].shape[0], pieces[0].shape[0]

    def copies(at, slot, t):
        place = pl.ds(t * size, size)
        return (
            pltpu.make_async_copy(pieces[at], held.at[slot, place], sems.at[slot, t]),
            pltpu.make_async_copy(cot_pieces[at], held_cots.at[slot, place], sems.at[slot, each + t]),
        )

    for j in range(count // each):

        @pl.when(step == max(j - 1, 0))
        def _(j=j):
            for t in range(each):
                for copy in copies(j * each + t, j % 2, t):
                    copy.start()

    slot = lax.rem(step, 2)
    for t in range(each):
        for copy in copies(t, slot, t):
            copy.wait()
    rows_ref[...] = held[slot]
    cots_ref[...] = held_cots[slot]
    gated, grad = group_pass(groups, units, experts, where_ref, rows_ref, cots_ref, gate_ref, down_ref)
    hidden_ref[...] = gated
    grad_ref[...] = grad
    add_grads(grad, rows_ref[...], gated, cots_ref[:, : rows_ref.shape[1]], gate_sums, down_sums, before)

    if last:

        @pl.when(step == steps - 1)
        def _():
            hand_out(units * len(groups), gate_sums, down_sums, *outs[:2])


def grads_kernel(wide, where_ref, rows_ref, cots_ref, hidden_ref, grad_ref, out_ref, router_ref, gate_sums, down_sums):
    cots = cots_ref[:, : rows_ref.shape[1]]
    add_grads(grad_ref[...], rows_ref[...], hidden_ref[...], cots, gate_sums, down_sums)

    @pl.when(pl.program_id(0) == pl.num_programs(0) - 1)
    def _():
        hand_out(wide, gate_sums, down_sums, out_ref, router_ref)


def second_kernel(
    groups, units, experts, where_ref, rows_ref, cots_ref, hidden_in_ref, grad_in_ref, gate_in_ref, down_in_ref, gate_ref, down_ref, *refs
):
    out_own_ref, out_far_ref, own_ref, far_ref, hidden_ref, grad_ref = refs[-6:]
    half = own_ref.shape[0]
    gated, grad = group_pass(groups, units, experts, where_ref, rows_ref, cots_ref, gate_ref, down_ref)
    hidden_ref[...] = gated
    grad_ref[...] = grad
    rows_grad = (dot(grad_in_ref[...], gate_in_ref[...]) + dot(grad, gate_ref[...])).astype(bf16)
    own_ref[...] = rows_grad[:half]
    far_ref[...] = rows_grad[half:]
    out_part = (dot(hidden_in_ref[...], down_in_ref[...]) + dot(gated, down_ref[...])).astype(bf16)
    out_own_ref[...] = out_part[:half]
    out_far_ref[...] = out_part[half:]


def among_all(w, tile, first=0):
    return pl.BlockSpec((tile, w), lambda i, where: (first + i, 0))


def all_of(shape):
    return pl.BlockSpec(shape, lambda i, where: (0,) * len(shape), pipeline_mode=pl.Buffered(1))


def grads_out(wide, pad, width, count):
    direct = whole_tiles(wide, width // count)
    return (count, 3 * wide, width // count) if direct else (3 * pad, width), (24, width)


def to_owners(grad, wide, count):
    if len(grad.shape) == 3:
        return grad
    grad = grad.reshape(3, -1, grad.shape[1])[:, :wide]
    return grad.reshape(3 * wide, count, -1).transpose(1, 0, 2)


def token_grid(cots, rows, tile=512):
    return rows.shape[0] // tile, tile, [among_all(rows.shape[1], tile), among_all(cots.shape[1], tile)]


def first_units(groups, where, pieces, cot_pieces, gate_rows, down_rows, units, experts, count, total, before=()):
    width, wider = gate_rows.shape[1], cot_pieces[0].shape[1]
    pad = down_rows.shape[0]
    wide = units * len(groups)
    tile = 512
    steps = sum(v.shape[0] for v in pieces) // tile
    first = total // tile - steps if before else 0
    sums = [(2 * pad, width), (pad, width)]
    shapes = grads_out(wide, pad, width, count)
    widths = (width, wider, pad, 2 * pad)
    whole = [jax.ShapeDtypeStruct((total, w), bf16) for w in widths]
    outs = [among_all(w, tile, first) for w in widths]
    held = [
        pltpu.VMEM((2, tile, width), bf16),
        pltpu.VMEM((2, tile, wider), bf16),
        pltpu.SemaphoreType.DMA((2, 2 * tile // pieces[0].shape[0])),
    ]
    if before:
        outs += [all_of(shape) for shape in shapes]
        whole += [jax.ShapeDtypeStruct(shapes[0], bf16), jax.ShapeDtypeStruct(shapes[1], f32)]
        held = [pltpu.VMEM(shape, f32) for shape in sums] + held
    else:
        outs += [all_of(shape) for shape in sums]
        whole += [jax.ShapeDtypeStruct(shape, f32) for shape in sums]
    kept = [pl.BlockSpec(memory_space=pl.ANY)] * 4
    return pl.pallas_call(
        functools.partial(first_kernel, groups, units, experts, len(pieces), bool(before)),
        grid_spec=pltpu.PrefetchScalarGridSpec(
            num_scalar_prefetch=1,
            grid=(steps,),
            in_specs=[pl.BlockSpec(memory_space=pl.ANY)] * (2 * len(pieces))
            + [all_of(gate_rows.shape), all_of(down_rows.shape)]
            + ([all_of(shape) for shape in sums] + kept if before else []),
            out_specs=outs,
            scratch_shapes=held,
        ),
        out_shape=whole,
        input_output_aliases={2 * len(pieces) + 5 + i: i for i in range(4)} if before else {},
        compiler_params=pltpu.CompilerParams(vmem_limit_bytes=60 * 1024 * 1024),
        cost_estimate=pl.CostEstimate(flops=12 * steps * tile * width * pad, bytes_accessed=4 * steps * tile * width, transcendentals=0),
    )(where, *pieces, *cot_pieces, gate_rows, down_rows, *before)


def weight_grads(where, rows, cots, hidden, grad, wide, count):
    total, width = rows.shape
    pad = hidden.shape[1]
    steps, tile, token_specs = token_grid(cots, rows)
    shapes = grads_out(wide, pad, width, count)
    weights, router = pl.pallas_call(
        functools.partial(grads_kernel, wide),
        grid_spec=pltpu.PrefetchScalarGridSpec(
            num_scalar_prefetch=1,
            grid=(steps,),
            in_specs=token_specs + [among_all(pad, tile), among_all(2 * pad, tile)],
            out_specs=[all_of(shapes[0]), all_of(shapes[1])],
            scratch_shapes=[pltpu.VMEM((2 * pad, width), f32), pltpu.VMEM((pad, width), f32)],
        ),
        out_shape=[jax.ShapeDtypeStruct(shapes[0], bf16), jax.ShapeDtypeStruct(shapes[1], f32)],
        compiler_params=pltpu.CompilerParams(vmem_limit_bytes=58 * 1024 * 1024),
        cost_estimate=pl.CostEstimate(flops=6 * total * width * pad, bytes_accessed=4 * total * width, transcendentals=0),
    )(where, rows, cots, hidden, grad)
    return to_owners(weights, wide, count), router


def second_units(groups, first, chunks, where, rows, cots, before, own, kept, units, experts):
    total, width = rows.shape
    steps, tile = chunks * 2, 512
    hidden_in, grad_in, gate_in, down_in = before
    gate_rows, down_rows = own
    pad = down_rows.shape[0]

    def half(w):
        return pl.BlockSpec((tile // 2, w), lambda i, where: (i, 0))

    def tokens_of(v):
        return among_all(v if isinstance(v, int) else v.shape[1], tile, first * 2)

    kept = list(kept)
    shapes = [(steps * tile // 2, width)] * 4 + [(total, pad), (total, 2 * pad)]
    return pl.pallas_call(
        functools.partial(second_kernel, groups, units, experts),
        grid_spec=pltpu.PrefetchScalarGridSpec(
            num_scalar_prefetch=1,
            grid=(steps,),
            in_specs=[tokens_of(rows), tokens_of(cots)]
            + [tokens_of(hidden_in), tokens_of(grad_in)]
            + [all_of(v.shape) for v in (gate_in, down_in, gate_rows, down_rows)]
            + [pl.BlockSpec(memory_space=pl.ANY)] * len(kept),
            out_specs=[half(width)] * 4 + [tokens_of(pad), tokens_of(2 * pad)],
        ),
        out_shape=[jax.ShapeDtypeStruct(shape, bf16) for shape in shapes],
        input_output_aliases={9 + i: 4 + i for i in range(len(kept))},
        compiler_params=pltpu.CompilerParams(vmem_limit_bytes=58 * 1024 * 1024),
        cost_estimate=pl.CostEstimate(flops=10 * steps * tile * width * pad, bytes_accessed=8 * steps * tile * width, transcendentals=0),
    )(where, rows, cots, hidden_in, grad_in, gate_in, down_in, gate_rows, down_rows, *kept)


def whole_tiles(units, rows):
    return units % 16 == 0 and rows % 128 == 0


def turn_kernel(columns_ref, out_ref):
    count, units, rows = out_ref.shape
    out_ref[...] = columns_ref[...].T.reshape(count, units, rows)


def turn_weights(columns, who, count, which=0):
    rows, width = columns.shape
    span = width // (3 * who)
    units = span // count
    if not whole_tiles(units, rows):
        columns = columns.reshape(rows, who, 3, count, units)[:, which]
        return columns.transpose(2, 1, 3, 0).reshape(count, -1, rows)
    return pl.pallas_call(
        turn_kernel,
        grid=(3,),
        in_specs=[pl.BlockSpec((rows, span), lambda k: (0, which * 3 + k))],
        out_specs=pl.BlockSpec((count, units, rows), lambda k: (0, k, 0)),
        out_shape=jax.ShapeDtypeStruct((count, 3 * units, rows), bf16),
        compiler_params=pltpu.CompilerParams(vmem_limit_bytes=32 * 1024 * 1024),
        cost_estimate=pl.CostEstimate(flops=0, bytes_accessed=4 * rows * 3 * span, transcendentals=0),
    )(columns)


def turn_back_kernel(first_ref, second_ref, shared_ref, routed_ref):
    count, units, rows = first_ref.shape

    def turned(block):
        return block.reshape(count * units, rows).T

    routed_ref[:, 0, :] = turned(first_ref[...]).astype(f32)
    routed_ref[:, 1, :] = turned(second_ref[:, :units]).astype(f32)
    shared_ref[...] = turned(second_ref[:, units:])


def turn_grads(first, second):
    count, units, rows = first.shape
    units = units // 3
    span = units * count
    if not whole_tiles(units, rows):
        second = second.reshape(count, 3, 2, units, rows)
        first = first.reshape(count, 3, units, rows)
        three = jnp.stack([first, second[:, :, 0], second[:, :, 1]]).transpose(0, 4, 2, 1, 3).reshape(3, rows, 3 * span)
        return three[2], jnp.moveaxis(three[:2], 0, 1).astype(f32)
    return pl.pallas_call(
        turn_back_kernel,
        grid=(3,),
        in_specs=[
            pl.BlockSpec((count, units, rows), lambda k: (0, k, 0)),
            pl.BlockSpec((count, 2 * units, rows), lambda k: (0, k, 0)),
        ],
        out_specs=[
            pl.BlockSpec((rows, span), lambda k: (0, k)),
            pl.BlockSpec((rows, 2, span), lambda k: (0, 0, k)),
        ],
        out_shape=[jax.ShapeDtypeStruct((rows, 3 * span), bf16), jax.ShapeDtypeStruct((rows, 2, 3 * span), f32)],
        compiler_params=pltpu.CompilerParams(vmem_limit_bytes=56 * 1024 * 1024),
        cost_estimate=pl.CostEstimate(flops=0, bytes_accessed=48 * rows * span, transcendentals=0),
    )(first, second)


def deal_kernel(share, dense_ref, attn_ref, shared_ref):
    width = share * 8
    for o in range(8):
        for k in range(4):
            at = k * width + o * share
            attn_ref[o, :, k * share : (k + 1) * share] = dense_ref[:, at : at + share]
    owners, _, columns = shared_ref.shape
    span = columns // 3
    for o in range(owners):
        for k in range(3):
            at = 4 * width + (k * owners + o) * span
            shared_ref[o, :, k * span : (k + 1) * span] = dense_ref[:, at : at + span]


def deal_columns(dense, share, owners):
    rows, columns = dense.shape
    shapes = [(8, rows, 4 * share), (owners, rows, (columns - 32 * share) // owners)]
    return pl.pallas_call(
        functools.partial(deal_kernel, share),
        out_shape=[jax.ShapeDtypeStruct(shape, bf16) for shape in shapes],
        compiler_params=pltpu.CompilerParams(vmem_limit_bytes=32 * 1024 * 1024),
        cost_estimate=pl.CostEstimate(flops=0, bytes_accessed=4 * rows * columns, transcendentals=0),
    )(dense)


def collect_kernel(share, attn_ref, shared_ref, dense_ref):
    width = share * 8
    for o in range(8):
        for k in range(4):
            at = k * width + o * share
            dense_ref[:, at : at + share] = attn_ref[o, :, k * share : (k + 1) * share].astype(f32)
    owners, _, columns = shared_ref.shape
    span = columns // 3
    for o in range(owners):
        for k in range(3):
            at = 4 * width + (k * owners + o) * span
            dense_ref[:, at : at + span] = shared_ref[o, :, k * span : (k + 1) * span].astype(f32)


def collect_columns(attn, shared, share):
    rows = attn.shape[1]
    columns = 32 * share + shared.shape[0] * shared.shape[2]
    return pl.pallas_call(
        functools.partial(collect_kernel, share),
        out_shape=jax.ShapeDtypeStruct((rows, columns), f32),
        compiler_params=pltpu.CompilerParams(vmem_limit_bytes=32 * 1024 * 1024),
        cost_estimate=pl.CostEstimate(flops=0, bytes_accessed=6 * rows * columns, transcendentals=0),
    )(attn, shared)


def place_kernel(units, *refs):
    parts, (router_ref, gate_ref, down_ref) = refs[:-3], refs[-3:]
    pad = down_ref.shape[0]
    wide = units * len(parts)
    blank = jnp.zeros((pad - wide, down_ref.shape[1]), bf16)
    for w, part in enumerate(parts):
        for k, (out_ref, at) in enumerate(((gate_ref, 0), (gate_ref, pad), (down_ref, 0))):
            out_ref[at + w * units : at + (w + 1) * units] = part[0, k * units : (k + 1) * units]
    gate_ref[wide:pad] = router_ref[...]
    gate_ref[pad + wide :] = blank
    down_ref[wide:] = blank


def place_weights(ffn, router):
    count, _, block = ffn.shape
    units = FF // count
    who = ffn.shape[1] // (3 * units)
    wide = units * who
    width = count * block
    pad = (wide + router.shape[0] + 127) // 128 * 128
    router = stack(router, jnp.zeros((pad - wide - router.shape[0], width), bf16))
    if not whole_tiles(units, block):
        gate, up, down = ffn.transpose(1, 0, 2).reshape(who, 3, units, width).transpose(1, 0, 2, 3).reshape(3, wide, width)
        blank = jnp.zeros((pad - wide, width), bf16)
        return stack(gate, router, up, blank), stack(down, blank)

    def column(r):
        return pl.BlockSpec((r, block), lambda i: (0, i))

    return pl.pallas_call(
        functools.partial(place_kernel, units),
        grid=(count,),
        in_specs=[pl.BlockSpec((1, 3 * units, block), lambda i, w=w: (i, w, 0)) for w in range(who)] + [column(pad - wide)],
        out_specs=[column(2 * pad), column(pad)],
        out_shape=[jax.ShapeDtypeStruct((r, width), bf16) for r in (2 * pad, pad)],
        compiler_params=pltpu.CompilerParams(vmem_limit_bytes=32 * 1024 * 1024),
        cost_estimate=pl.CostEstimate(flops=0, bytes_accessed=12 * wide * width, transcendentals=0),
    )(*[ffn] * who, router)


def attend_rows(queries, keys, allowed):
    scores = jnp.where(allowed, dot_nt(queries, keys) * HD ** (-0.5), -1e30)
    raw = jnp.exp(scores - jnp.max(scores, axis=1, keepdims=True))
    return raw / jnp.sum(raw, axis=1, keepdims=True)


def allowed_pairs(own_ref, all_ref):
    return (own_ref[:, :1] == all_ref[0, :1]) & (all_ref[0, 1:2] <= own_ref[:, 1:2])


def piece_at(where_ref, s, piece_ref):
    size = piece_ref.shape[0]
    return pl.ds(pl.multiple_of(where_ref[s] * size, size), size)


def attend_kernel(heads, where_ref, rows_ref, bias_ref, cosine_ref, sine_ref, own_ref, all_ref, *refs):
    pieces, (packed_ref, mixed_ref) = refs[:-2], refs[-2:]
    share = heads * HD
    packed = bias_ref[...]
    for s, piece in enumerate(pieces):
        packed = packed + dot(rows_ref[:, piece_at(where_ref, s, piece)], piece[:, : 3 * share])
    cosine, sine = cosine_ref[...], sine_ref[...]
    allowed = allowed_pairs(own_ref, all_ref)

    def turned(at):
        v = packed[:, at : at + HD]
        return (v * cosine + pltpu.roll(v, HD // 2, 1) * sine).astype(bf16)

    for h in range(heads):
        queries, keys = turned(h * HD), turned(share + h * HD)
        values = packed[:, 2 * share + h * HD : 2 * share + (h + 1) * HD].astype(bf16)
        attend = attend_rows(queries, keys, allowed)
        mixed_ref[:, h * HD : (h + 1) * HD] = dot(attend.astype(bf16), values).astype(bf16)
        for k, v in enumerate((queries, keys, values)):
            packed_ref[:, k * share + h * HD : k * share + (h + 1) * HD] = v


def project_kernel(where_ref, mixed_ref, *refs):
    pieces, (near_ref, far_ref) = refs[:-2], refs[-2:]
    half = near_ref.shape[0]
    for s, piece in enumerate(pieces):
        rows = dot_nt(mixed_ref[...], piece[:, piece.shape[1] * 3 // 4 :]).astype(bf16)
        columns = piece_at(where_ref, s, piece)
        near_ref[:, columns] = rows[:half]
        far_ref[:, columns] = rows[half:]


def attend_back_kernel(heads, where_ref, grad_ref, packed_ref, cosine_ref, sine_ref, own_ref, all_ref, *refs):
    pieces, (packed_grad_ref, near_ref, far_ref, bias_ref) = refs[:-4], refs[-4:]
    share = heads * HD
    scale = HD ** (-0.5)
    mixed_grad = 0.0
    for s, piece in enumerate(pieces):
        mixed_grad = mixed_grad + dot(grad_ref[:, piece_at(where_ref, s, piece)], piece[:, 3 * share :])
    mixed_grad = mixed_grad.astype(bf16)
    cosine, sine = cosine_ref[...], sine_ref[...]
    allowed = allowed_pairs(own_ref, all_ref)

    def back(v):
        v = v.astype(bf16).astype(f32)
        return (v * cosine - pltpu.roll(v, HD // 2, 1) * sine).astype(bf16)

    for h in range(heads):
        queries, keys, values = (
            packed_ref[:, k * share + h * HD : k * share + (h + 1) * HD] for k in range(3)
        )
        own_grad = mixed_grad[:, h * HD : (h + 1) * HD]
        attend = attend_rows(queries, keys, allowed)
        attend_grad = dot_nt(own_grad, values)
        scores_grad = attend * (attend_grad - jnp.sum(attend * attend_grad, axis=1, keepdims=True))
        scores_grad = scores_grad.astype(bf16)
        grads = (
            back(dot(scores_grad, keys) * scale),
            back(dot_tn(scores_grad, queries) * scale),
            dot_tn(attend.astype(bf16), own_grad).astype(bf16),
        )
        for k, v in enumerate(grads):
            packed_grad_ref[:, k * share + h * HD : k * share + (h + 1) * HD] = v
    packed_grad = packed_grad_ref[...]
    bias_ref[...] = jnp.broadcast_to(jnp.sum(packed_grad.astype(f32), axis=0, keepdims=True), bias_ref.shape)
    half = near_ref.shape[0]
    for s, piece in enumerate(pieces):
        rows_grad = dot_nt(packed_grad, piece[:, : 3 * share]).astype(bf16)
        columns = piece_at(where_ref, s, piece)
        near_ref[:, columns] = rows_grad[:half]
        far_ref[:, columns] = rows_grad[half:]


def group_call(kernel, group_len, where, operands, specs, pieces, out_widths, out_types, flops):
    def spec(kind, shape):
        if kind == "rows":
            return pl.BlockSpec((group_len, shape[1]), lambda i, where: (i, 0))
        if kind == "pair":
            return pl.BlockSpec((1,) + shape[1:], lambda i, where: (i, 0, 0))
        return pl.BlockSpec(shape, lambda i, where: (0, 0), pipeline_mode=pl.Buffered(1))

    operands = tuple(operands) + tuple(pieces)
    specs = tuple(specs) + ("all",) * len(pieces)
    return pl.pallas_call(
        kernel,
        grid_spec=pltpu.PrefetchScalarGridSpec(
            num_scalar_prefetch=1,
            grid=(2,),
            in_specs=[spec(k, v.shape) for k, v in zip(specs, operands)],
            out_specs=[pl.BlockSpec((r, w), lambda i, where: (i, 0)) for r, w in out_widths],
        ),
        out_shape=[jax.ShapeDtypeStruct((2 * r, w), t) for (r, w), t in zip(out_widths, out_types)],
        compiler_params=pltpu.CompilerParams(vmem_limit_bytes=48 * 1024 * 1024),
        cost_estimate=pl.CostEstimate(flops=flops, bytes_accessed=sum(2 * v.size for v in operands), transcendentals=0),
    )(where, *operands)


def body(lay, tokens, dense_weights, expert_weights, gain_attn, gain_ffn, qkv_bias, router_weight, routes, doc_ids, out_grad):
    row_count, model_width = tokens.shape
    rings = lay.rings
    ring = lax.axis_index("ring")
    pair = lax.axis_index("pair")
    ep = lax.axis_index("ep")
    local_experts = expert_weights.shape[1]
    expert_count = router_weight.shape[1] - 1
    owners = expert_count // local_experts
    dp_count = rings * 2
    ring_place = jnp.asarray(lay.place, jnp.int32)[ring]
    behind = [jnp.asarray(lay.order, jnp.int32)[(ring_place - s) % rings] for s in range(rings)]
    ring_order = jnp.stack(behind)
    own_expert = ep * local_experts
    where = own_expert[None].astype(jnp.int32)

    stream = tokens.astype(f32)
    gain_one = gain_attn.astype(f32)
    gain_two = gain_ffn.astype(f32)
    heads = H // 8
    share = heads * HD
    unit_share = SFF // owners
    units = FF // dp_count
    n = row_count

    bits = jnp.sum(jnp.left_shift(jnp.int32(1), routes), axis=1, keepdims=True).astype(bf16)
    cot_blocks = [jnp.concatenate([out_grad, jnp.broadcast_to(bits, (row_count, 128))], axis=1)]
    mine, shared = deal_columns(after(dense_weights, cot_blocks[0]), share, owners)
    plane_part = lax.all_to_all(mine, PLANE, split_axis=0, concat_axis=0, tiled=True)
    plane_part = plane_part.reshape(-1, 4 * share)
    cot_blocks.append(permute(cot_blocks[0], lay.onward))
    mine, cot_blocks[1] = together(mine, cot_blocks[1])
    for _ in range(rings - 3):
        cot_blocks.append(permute(cot_blocks[-1], lay.onward))

    inverse_one = lax.rsqrt(jnp.mean(stream * stream, axis=1, keepdims=True) + norm_eps)
    normed = (stream * inverse_one * gain_one).astype(bf16)
    doc_pair = jnp.stack([doc_ids, permute(doc_ids, lay.up)])
    group_len = doc_ids.shape[0]
    before = jnp.sum((doc_pair[:, None, :] < doc_pair[:, :, None]).astype(jnp.int32), axis=2)
    spot = jnp.arange(group_len, dtype=jnp.int32)
    near_blocks = jnp.stack([ep, ep ^ 2, ep ^ 1, ep ^ 3])

    def in_order(values):
        return values.reshape(2, 4, row_count)[:, near_blocks].reshape(2, group_len)

    places = in_order(spot[None, :] - before)
    docs = in_order(doc_pair)
    spots = in_order(jnp.stack([spot, spot]))
    cosine, sine = rope_tables(places.reshape(-1))
    sine = jnp.where(jnp.arange(HD) < HD // 2, -sine, sine)
    spots_all = jnp.stack([docs, spots], axis=1)
    spots_own = jnp.stack([docs.reshape(-1), spots.reshape(-1)], axis=1)
    routed = expert_weights.reshape(expert_weights.shape[0], -1)
    router = router_weight.T
    turn = (own_expert + jnp.arange(expert_count, dtype=jnp.int32)) % expert_count
    router = stack(jnp.take(router, turn, axis=0), router[expert_count:])
    slot = pair * 4 + ep
    bias_share = lax.dynamic_slice_in_dim(qkv_bias.astype(f32).reshape(3, 8, share), slot, 1, 1, allow_negative_indices=False).reshape(1, 3 * share)
    plane_part, cot_blocks[-1], routed, normed = together(plane_part, cot_blocks[-1], routed, normed)

    qkv = [plane_part, permute(plane_part, lay.onward)]
    side, up = permute(normed, lay.side), permute(normed, lay.up)

    def between_cores(*pieces):
        return [permute(piece, lay.core) for piece in pieces]

    def over(pairs, pieces):
        return [permute(piece, pairs) for piece in pieces]

    cot_sides, cot_ups = over(lay.side, cot_blocks[:1]), over(lay.up, cot_blocks[:1])
    first_ffn, second_ffn = (turn_weights(routed, local_experts, dp_count, w) for w in range(local_experts))
    qkv[-1], side, up, cot_sides, cot_ups, cosine, sine, first_ffn, second_ffn = lax.optimization_barrier(
        (qkv[-1], side, up, cot_sides, cot_ups, cosine, sine, first_ffn, second_ffn)
    )
    cot_crosses = []

    def crossing(s):
        return permute(cot_sides[s], lay.up) if s % 2 else permute(cot_ups[s], lay.side)

    for s in range(2, rings):
        qkv.append(permute(qkv[-1], lay.onward))
        sides, ups = [], []
        if s == 2:
            cross = permute(up, lay.side)
            cores = between_cores(normed, side, up)
            sides, ups = over(lay.side, cot_blocks[1:2]), over(lay.up, cot_blocks[1:3])
            cross, cores = lax.optimization_barrier((cross, cores))
        elif s == 3:
            cores += between_cores(cross)
            normed_group = assemble((normed, side, *cores[:2], up, cross, *cores[2:]))
            sides, ups = over(lay.side, cot_blocks[2:]), over(lay.up, cot_blocks[3:])
            cot_crosses = [crossing(0), crossing(1)]
        sides, ups, qkv[-1], cot_crosses = lax.optimization_barrier((sides, ups, qkv[-1], cot_crosses))
        cot_sides, cot_ups = cot_sides + sides, cot_ups + ups
    qkv[-1], normed_group = together(qkv[-1], normed_group)

    cot_blocks.append(permute(after(cot_blocks[-1], qkv[-1]), lay.onward))
    cot_crosses += [crossing(s) for s in range(2, rings - 1)]
    heads_flops = 8 * heads * group_len * group_len * HD
    packed, mixed = group_call(
        functools.partial(attend_kernel, heads),
        group_len,
        ring_order,
        (normed_group, bias_share, cosine, sine, spots_own, spots_all),
        ("rows", "all", "rows", "rows", "rows", "pair"),
        qkv,
        [(group_len, 3 * share), (group_len, share)],
        [bf16, bf16],
        4 * group_len * model_width * 3 * share + heads_flops,
    )
    packed, mixed, cot_crosses, cot_blocks = lax.optimization_barrier((packed, mixed, cot_crosses, cot_blocks))
    cot_sides += over(lay.side, cot_blocks[-1:])
    cot_ups += over(lay.up, cot_blocks[-1:])
    received = [lax.dynamic_index_in_dim(shared, ep ^ k, 0, keepdims=False, allow_negative_indices=False) for k in range(4)]
    received[1:3] = [permute(v, pairs) for v, pairs in zip(received[1:3], (lay.core, lay.side))]
    branch_parts = group_call(
        project_kernel,
        group_len,
        ring_order,
        (mixed,),
        ("rows",),
        qkv,
        [(group_len // 2, model_width)] * 2,
        [bf16, bf16],
        4 * group_len * model_width * share,
    )

    def to_units(ffn):
        return lax.all_to_all(ffn, ("ring", "pair"), split_axis=0, concat_axis=0, tiled=True)

    first_ffn = to_units(after(first_ffn, packed))
    here = plus(branch_parts[0], permute(branch_parts[1], lay.core))
    cross, side = permute(here[3 * n :], lay.side), permute(here[n : 2 * n], lay.side)
    received[3] = permute(after(received[3], cross), lay.side_core)
    up = permute(plus(here[2 * n : 3 * n], cross), lay.up)
    up, cot_sides, cot_ups = lax.optimization_barrier((up, cot_sides, cot_ups))
    branch = here[:n].astype(f32) + side.astype(f32) + after(up, first_ffn, *received[:3]).astype(f32)
    cot_crosses.append(permute(cot_ups[-1], lay.side))
    residual = stream + branch
    inverse_two = lax.rsqrt(jnp.mean(residual * residual, axis=1, keepdims=True) + norm_eps)
    normed_two = (residual * inverse_two * gain_two).astype(bf16)

    blocks, ups, sides, crosses, inner = [normed_two], [], [], [], []

    for s in range(rings):
        up = permute(blocks[s], lay.up)
        going = {}
        if s < rings - 1:
            going["onward"] = permute(blocks[s], lay.onward)
        if s == 0:
            going["received"] = received[3]
        else:
            going["side"] = permute(blocks[s - 1], lay.side)
        if s == 1:
            going["crosses_too"] = cot_crosses
        if s == rings - 2:
            first_rows = place_weights(first_ffn, router)
            going["first_rows"] = first_rows
        if s == rings - 1:
            crosses = {k: permute(sides[k], lay.up) for k in range(1, rings - 2, 2)}
            crosses[0] = permute(ups[0], lay.side)
            shared_ffn = jnp.stack(received)[jnp.arange(4, dtype=jnp.int32) ^ ep].reshape(-1, 3 * unit_share)
            second_ffn = jnp.concatenate([second_ffn, turn_weights(shared_ffn, 1, dp_count)], axis=1)
            going["crosses"], going["second_ffn"] = crosses, second_ffn
        up, going = lax.optimization_barrier((up, going))
        ups.append(up)
        if "onward" in going:
            blocks.append(going["onward"])
        if "side" in going:
            sides.append(going["side"])
        if "crosses_too" in going:
            cot_crosses = going["crosses_too"]
        if "received" in going:
            received[3] = going["received"]
        if "first_rows" in going:
            first_rows = going["first_rows"]
        if "crosses" in going:
            crosses, second_ffn = going["crosses"], going["second_ffn"]
    second_ffn = to_units(second_ffn)
    sides.append(permute(blocks[-1], lay.side))
    crosses.update({k: permute(ups[k], lay.side) for k in range(2, rings - 1) if k not in crosses})
    crosses[rings - 1] = permute(ups[-1], lay.side)
    cots = list(zip(cot_blocks, cot_ups, cot_sides, cot_crosses))

    late = rings // 2

    def first_ffn_half(begin, end, *before):
        rows, cot_rows = [], []
        for s in range(begin, end):
            for pieces, four in ((rows, (blocks[s], ups[s], sides[s], crosses[s])), (cot_rows, cots[s])):
                there = between_cores(*four)
                pieces += [*four[:2], *there[:2], *four[2:], *there[2:]]
        return first_units((0,), where, rows, cot_rows, *first_rows, units, expert_count, dp_count, 8 * n * rings, *before)

    filled = first_ffn_half(0, late)
    filled, blocks, ups, sides, crosses, cots = lax.optimization_barrier((filled, blocks, ups, sides, crosses, cots))
    rows, cots, first_hidden, first_grad, first_weights_grad, first_router = first_ffn_half(late, rings, (*filled[4:], *filled[:4]))
    first_weights_grad = to_owners(first_weights_grad, units, dp_count)
    first_weights_grad = to_units(first_weights_grad)
    second_rows = place_weights(after(second_ffn, first_hidden), router)

    chunk, half = 4 * n, 2 * n
    order = list(range(rings))[::-1]
    first_half, last_half = order[: rings - late], order[rings - late :]

    def cut_chunk(which, s, at):
        begin = (s % late if s < late else s - late) * chunk + at
        return which[begin : begin + half]

    def crossed(part, there, some):
        keep = {s: plus(cut_chunk(part, s, 0), cut_chunk(there, s, 0)) for s in some}
        send = {s: plus(cut_chunk(part, s, half), cut_chunk(there, s, half)) for s in some}
        return keep, send

    def all_there(*groups):
        flat, tree = jax.tree.flatten(groups)
        return jax.tree.unflatten(tree, lax.optimization_barrier(tuple(flat)))

    def ffn_half(first, chunks, kept):
        return second_units(
            (1, SHARED), first, chunks, where, rows, cots, (first_hidden, first_grad) + tuple(first_rows), second_rows, kept, units, expert_count
        )

    out_own_a, out_far_a, own_a, far_a, hidden, gate_up_grad = ffn_half(late, rings - late, ())
    own_a, far_a, first_weights_grad = all_there(own_a, far_a, first_weights_grad)

    pair_first = order[1::2]

    def link(s, second):
        return lay.side if (s in pair_first) == second else lay.up

    def split(part, there, some):
        keep, send = crossed(part, there, [s for s in some if s not in pair_first])
        for s in some:
            if s in pair_first:
                pieces = [plus(*(cut_chunk(v, s, t * n)[:n] for v in (part, there))) for t in range(4)]
                keep[s], send[s] = stack(pieces[0], pieces[2]), stack(pieces[1], pieces[3])
        return keep, send

    def start(send, some):
        return {s: permute(send[s], link(s, False)) for s in some}

    def go_on(keep, arrived, some):
        halves = {s: plus(keep[s], arrived[s]) for s in some}
        return halves, {s: permute(halves[s][n:], link(s, True)) for s in some}

    def finish(halves, arrived):
        return {s: halves[s][:n].astype(f32) + arrived[s].astype(f32) for s in halves}

    keep, send = split(own_a, permute(far_a, lay.core), first_half)
    keep, send, hidden, gate_up_grad = all_there(keep, send, hidden, gate_up_grad)
    out_there_a = permute(after(out_far_a, hidden), lay.core)
    arrived = start(send, first_half)
    out_own_b, out_far_b, own_b, far_b, hidden, gate_up_grad = ffn_half(0, late, (hidden, gate_up_grad))
    arrived, own_b, far_b, hidden, gate_up_grad, out_there_a = all_there(
        arrived, own_b, far_b, hidden, gate_up_grad, out_there_a
    )

    far_there = permute(far_b, lay.core)
    halves, arrived = go_on(keep, arrived, first_half)
    keep, send = split(own_b, far_there, last_half)
    keep, send, halves, arrived, hidden = all_there(keep, send, halves, arrived, hidden)
    own_sums = finish(halves, arrived)
    total = own_sums[order[0]]
    queue = list(order[1:])

    def step_on(total):
        return permute(total.astype(bf16), lay.backward)

    def step_in(arrived):
        return own_sums[queue.pop(0)] + arrived.astype(f32)

    arrived = start(send, last_half)
    moving = step_on(total)
    ffn_grad, second_router = weight_grads(where, rows, cots, hidden, gate_up_grad, 2 * units, dp_count)
    out_there_b = permute(out_far_b, lay.core)
    arrived, moving, ffn_grad, out_there_b = all_there(arrived, moving, ffn_grad, out_there_b)
    total = step_in(moving)

    halves, arrived = go_on(keep, arrived, last_half)
    moving = step_on(total)
    out_keep, out_send = crossed(out_own_a, out_there_a, first_half)
    halves, arrived, moving, out_keep, out_send = all_there(halves, arrived, moving, out_keep, out_send)
    own_sums.update(finish(halves, arrived))
    total = step_in(moving)

    moving = step_on(total)
    more_keep, more_send = crossed(out_own_b, out_there_b, last_half)
    moving, more_keep, more_send = all_there(moving, more_keep, more_send)
    out_keep.update(more_keep)
    out_send.update(more_send)
    total = step_in(moving)
    while queue:
        total = step_in(step_on(total))
    normed_two_grad = total

    def router_rows(part, wide):
        start = wide - wide // 8 * 8
        return part[start : start + expert_count + 1]

    router_part = router_rows(first_router, units) + router_rows(second_router, 2 * units)
    turn_back = (jnp.arange(expert_count, dtype=jnp.int32) - own_expert) % expert_count
    router_part = stack(jnp.take(router_part[:expert_count], turn_back, axis=0), router_part[expert_count:])

    cotangent = out_grad.astype(f32)
    scaled_two = normed_two_grad * gain_two
    gain_two_grad = jnp.sum(normed_two_grad * residual * inverse_two, axis=0)
    residual_grad = (
        cotangent
        + inverse_two * scaled_two
        - residual * inverse_two**3 * jnp.mean(scaled_two * residual, axis=1, keepdims=True)
    )
    branch_grad = residual_grad.astype(bf16)

    side, up = permute(branch_grad, lay.side), permute(branch_grad, lay.up)
    core = permute(branch_grad, lay.core)
    side, up, core, ffn_grad = together(side, up, core, ffn_grad)
    ffn_grad = lax.all_to_all(ffn_grad, ("ring", "pair"), split_axis=0, concat_axis=0, tiled=True)
    cross = permute(up, lay.side)
    cores = [core, *between_cores(side, up)]
    cores.append(permute(cross, lay.core))
    branch_grad_group = assemble((branch_grad, side, *cores[:2], up, cross, *cores[2:]))
    keep, send = out_keep, out_send
    branch_grad_group = together(branch_grad_group)[0]

    quarter = [order[k :: 4] for k in range(4)] if rings > 4 else [[s] for s in order]
    sided = {s: permute(send[s], lay.side) for s in quarter[0]}
    packed_grad, near, far, bias_part = group_call(
        functools.partial(attend_back_kernel, heads),
        group_len,
        ring_order,
        (branch_grad_group, packed, cosine, sine, spots_own, spots_all),
        ("rows", "rows", "rows", "rows", "rows", "pair"),
        qkv,
        [(group_len, 3 * share), (group_len // 2, model_width), (group_len // 2, model_width), (8, 3 * share)],
        [bf16, bf16, bf16, f32],
        4 * group_len * model_width * 4 * share + 3 * heads_flops,
    )
    sided, packed_grad, near, far = all_there(sided, packed_grad, near, far)

    halves = {s: plus(keep[s], sided[s]) for s in quarter[0]}
    sided = {s: permute(send[s], lay.side) for s in quarter[1]}
    here = plus(near, permute(far, lay.core))
    attn_grads = jnp.concatenate([dot_over(normed_group, packed_grad), dot_over(branch_grad_group, mixed)], axis=1)
    attn_grads = attn_grads.astype(bf16).reshape(rings, -1, 4 * share)
    sided, attn_grads, here, halves = all_there(sided, attn_grads, here, halves)

    out_halves = {s: plus(keep[s], sided[s]) for s in quarter[1]}
    out_halves.update(halves)
    side, cross = permute(here[n : 2 * n], lay.side), permute(here[3 * n :], lay.side)
    def grads_at(s):
        return lax.dynamic_index_in_dim(attn_grads, behind[s], 0, keepdims=False, allow_negative_indices=False).astype(f32)

    moving = permute(grads_at(order[0]).astype(bf16), lay.backward)
    side, cross, ffn_grad = together(side, cross, ffn_grad)

    up = permute(plus(here[2 * n : 3 * n], cross), lay.up)
    sided = {s: permute(send[s], lay.side) for s in quarter[2]}
    first_up = permute(out_halves[order[0]][n:], lay.up)
    sided, up, moving, first_up = all_there(sided, up, moving, first_up)
    output_sum = out_halves[order[0]][:n].astype(f32) + first_up.astype(f32)
    normed_grad = here[:n].astype(f32) + side.astype(f32) + up.astype(f32)
    scaled_one = normed_grad * gain_one
    gain_one_grad = jnp.sum(normed_grad * stream * inverse_one, axis=0)
    input_grad = (
        residual_grad
        + inverse_one * scaled_one
        - stream * inverse_one**3 * jnp.mean(scaled_one * stream, axis=1, keepdims=True)
    )
    bias_part = (bias_part[0] + bias_part[8]).reshape(3, 1, share)
    bias_part = lax.dynamic_update_slice(jnp.zeros((3, 8, share), f32), bias_part, (0, slot, 0), allow_negative_indices=False)
    small = stack(router_part, gain_two_grad[None], gain_one_grad[None], bias_part.reshape(3, model_width))
    doubling = lay.doubling()

    total = grads_at(order[1]) + moving.astype(f32)
    out_halves.update({s: plus(keep[s], sided[s]) for s in quarter[2]})
    out_sums, out_queue = {}, list(order[1:])

    def outs_on(output_sum):
        return permute(output_sum.astype(bf16), lay.backward)

    def outs_over(some):
        return {s: permute(out_halves[s][n:], lay.up) for s in some}

    def outs_in(outs_up):
        out_sums.update({s: out_halves[s][:n].astype(f32) + outs_up[s].astype(f32) for s in outs_up})

    moving = permute(total.astype(bf16), lay.backward)
    outs_up = outs_over((quarter[0] + quarter[1])[1:])
    sided = {s: permute(send[s], lay.side) for s in quarter[3]}
    small = small + permute(small, doubling[3])
    shared_columns_grad, expert_grad = turn_grads(first_weights_grad, ffn_grad)
    shared_columns_grad = lax.all_to_all(
        shared_columns_grad.reshape(owners, -1, 3 * unit_share), "ep", split_axis=0, concat_axis=0, tiled=True
    )
    moving, outs_up, sided, small, expert_grad = all_there(moving, outs_up, sided, small, expert_grad)
    outs_in(outs_up)
    out_halves.update({s: plus(keep[s], sided[s]) for s in quarter[3]})

    total = grads_at(order[2]) + moving.astype(f32)
    moving = permute(total.astype(bf16), lay.backward)
    outs_up = outs_over(quarter[2] + quarter[3])
    output_sum = after(output_sum, outs_up[order[2]])
    outgoing = [outs_on(v) for v in (output_sum[: n // 2], output_sum[n // 2 :])]
    for step in doubling[:3]:
        small = small + permute(small, step)
    moving, shared_columns_grad, outs_up, small = all_there(moving, shared_columns_grad, outs_up, small)
    outs_in(outs_up)
    total = grads_at(order[3]) + moving.astype(f32)
    for s in order[4:]:
        total = grads_at(s) + permute(total.astype(bf16), lay.backward).astype(f32)

    total, small = all_there(total.astype(bf16), small)
    total = total.reshape(8, -1, 4 * share)
    total = lax.all_to_all(total, PLANE, split_axis=0, concat_axis=0, tiled=True)
    for s in out_queue[:-1]:
        outgoing = [outs_on(out_sums[s][k * n // 2 : (k + 1) * n // 2] + v.astype(f32)) for k, v in enumerate(outgoing)]
    total, small = together(total, small)
    dense_grad = collect_columns(total, shared_columns_grad, share)
    dense_grad, *outgoing = together(dense_grad, *outgoing)
    output_sum = out_sums[out_queue[-1]] + stack(*outgoing).astype(f32)
    for step in doubling[4:]:
        small = small + permute(small, step)
    output = (residual + output_sum).astype(bf16)

    router_sum, gain_two_sum, gain_one_sum, bias_sum = jnp.split(small, [expert_count + 1, expert_count + 2, expert_count + 3])
    return (
        output,
        input_grad,
        dense_grad,
        expert_grad,
        gain_one_sum[0],
        gain_two_sum[0],
        bias_sum.reshape(-1),
        router_sum.T,
    )


def solution(mesh):
    devices = mesh.devices
    lay = Layout(devices.shape[0] // 2)
    inner = Mesh(devices.reshape(lay.rings, 2, devices.shape[1]), AXES)
    rows = P(AXES, None)
    experts = P(("ring", "pair"), "ep", None)
    in_specs = (rows, rows, experts, P(), P(), P(), P(), rows, P(("ring", "pair")), rows)
    out_specs = (rows, rows, rows, experts, P(), P(), P(), P())

    def run(*arguments):
        return body(lay, *arguments)

    return jax.shard_map(run, mesh=inner, in_specs=in_specs, out_specs=out_specs, check_vma=False)
```
